32 devices in a mesh: rep: 2 (over x), exp: 16 (over z, y, core).
Axes of the slice: x: 2, y: 2, z: 4, core: 2. Of those that a mesh axis runs over, the one named last changes fastest.
Arguments:
- tokens: bfloat16 [5120, 512], P(('rep', 'exp')), may hold values from -6 to 6
- gates: bfloat16 [5120, 2], P(('rep', 'exp')), may hold values from 0.19921875 to 1
- routes: int32 [5120, 2], P(('rep', 'exp')), may hold values from 0 to 15, all different within a row; in each aligned block of 160 rows (0 to 159, 160 to 319, ...) at most 30 rows name the same one
- cotangent: bfloat16 [5120, 512], P(('rep', 'exp')), may hold values from -6 to 6
- w_up: bfloat16 [16, 2048, 512], P('exp'), may hold values from -0.25 to 0.25
- w_down: bfloat16 [16, 2048, 512], P('exp'), may hold values from -0.125 to 0.125
Outputs:
- d_tokens: bfloat16 [5120, 512], P(('rep', 'exp'))
- d_gates: bfloat16 [5120, 2], P(('rep', 'exp'))
- grad_up: bfloat16 [16, 2048, 512], P('exp', 'rep')
- grad_down: bfloat16 [16, 2048, 512], P('exp', 'rep')
The draws below stay inside these ranges and needn't reach their ends.
Inputs may be any that keep to these rules, and one draw needn't show every extreme that they name: `routes`: each row names two different experts. In each aligned block of 160 rows (the rows of one device) no expert is named by more than 30 rows, a bound that some block reaches.
All inputs are finite; a program needn't handle non-finite values.
Results may differ from the reference program's by a relative error of at most 0.014.
Values may be sent and summed in bfloat16 or wider, within the bound.
No kernel may reach another device: no remote copies, remote signals or barrier semaphores. Data moves between devices by JAX's collectives and lax.ppermute only.
A program may use at most 64 MiB of HBM per device.

```python
import math
import jax
import jax.numpy as jnp
import numpy as np
from jax import lax

D = 512
FF = 2048
T_DEV = 160
EXPERTS = 16
CAP = 30
TOKENS = 5120
N_REP = 2
N_EXP = 16


def levels(rng, extent, shards, low, top_value):
    level = 1.0
    for position, parts in shards:
        draws = jax.random.uniform(jax.random.fold_in(jax.random.fold_in(rng, 6), position), (parts,), jnp.float32, low / len(shards), top_value / len(shards))
        level = level * jnp.repeat(jnp.exp(draws), extent[position] // parts).reshape((-1,) + (1,) * (len(extent) - 1 - position))
    return level


def shared_out(own_key, own, number, rows, number_of, top, limit, lean):
    order = jax.random.permutation(own_key, number_of)
    heavy_load, common = shares(number_of, rows * top, limit, lean, True), shares(number_of, rows * top, limit, lean, False)
    places = jnp.arange(number_of)

    def named(sizes, turn):
        used = int((sizes > 0).sum())
        fixed = max(1, used // 4)
        passed = fixed + (places - fixed + turn * (used - fixed)) % max(1, number_of - fixed)
        return jnp.zeros((number_of,), jnp.int32).at[order[jnp.where(places < fixed, places, passed)]].set(jnp.asarray(sizes, jnp.int32))

    sizes = jnp.where(number % 4 == 0, named(heavy_load, number // 4), named(common, number - number // 4 - 1))
    mixed = jax.random.permutation(jax.random.fold_in(own, 3), number_of)
    giver, sink = mixed[0:number_of // 2 * 2:2], mixed[1:number_of // 2 * 2:2]
    margin = jnp.minimum(sizes[giver] - 1, limit - sizes[sink]) // 2
    margin = jnp.where((giver == order[0]) | (sink == order[0]) | (sizes[sink] == 0), 0, jnp.maximum(margin, 0))
    passed = jax.random.randint(jax.random.fold_in(own, 4), (number_of // 2,), 0, 1 << 20) % (margin + 1)
    sizes = sizes.at[giver].add(-passed).at[sink].add(passed)
    labels = jnp.searchsorted(jnp.cumsum(sizes), jnp.arange(rows * top), side="right").astype(jnp.int32)
    listing = labels.reshape(top, rows).T
    listing = listing[jax.random.permutation(jax.random.fold_in(own, 1), rows)]
    turn = jax.random.randint(jax.random.fold_in(own, 2), (rows, 1), 0, top)
    return jnp.take_along_axis(listing, (jnp.arange(top)[None, :] + turn) % top, axis=1)


def shares(amount, total, limit, lean, full):
    weights = [(1 << 20) // math.isqrt(standing ** lean) + 1 for standing in range(1, amount + 1)]
    largest = limit if full else min(limit, max(-(-total // amount), total * weights[0] // sum(weights)))
    least = 1 if total - largest >= amount - 1 else 0
    holding, surplus = [largest] + [least] * (amount - 1), total - largest - least * (amount - 1)
    while surplus > 0:
        candidates = [i for i in range(1, amount) if holding[i] < largest] or [i for i in range(1, amount) if holding[i] < limit]
        mass, budget = sum([weights[i] for i in candidates]), surplus
        for i in candidates:
            extra = min(limit - holding[i], max(1, budget * weights[i] // mass), surplus)
            holding[i] = holding[i] + extra
            surplus = surplus - extra
    return np.array(holding)


def scatter_about(own_key, shape, width, reach, shards=(), held_as=jnp.bfloat16):
    loudness = levels(own_key, shape, shards, -0.22, 0.18) if shards else 1.0
    drawn = jax.random.normal(own_key, shape, jnp.float32) * width * loudness
    return jnp.minimum(jnp.maximum(drawn, -reach), reach).astype(held_as)


def setup_inputs(seed: int = 0) -> dict:
    streams_of = jax.random.split(jax.random.key(seed), 7)
    tokens = scatter_about(streams_of[0], (TOKENS, D), 1.0, 6.0, ((0, 32),))
    gates = jnp.clip(0.19921875 + 0.80078125 * jax.random.uniform(streams_of[1], (TOKENS, 2), jnp.float32) ** levels(streams_of[1], (TOKENS, 2), ((0, 32),), -0.2, 0.2), 0.19921875, 1.0).astype(jnp.bfloat16)
    routes_keys = jax.random.split(jax.random.fold_in(streams_of[2], 1), TOKENS // T_DEV)
    routes_turns = jax.random.permutation(jax.random.fold_in(streams_of[2], 3), TOKENS // T_DEV)
    routes = jax.vmap(lambda own, number: shared_out(jax.random.fold_in(streams_of[2], 2), own, number, T_DEV, EXPERTS, 2, CAP, 1))(routes_keys, routes_turns).reshape((TOKENS, 2))
    cotangent = scatter_about(streams_of[3], (TOKENS, D), 1.0, 6.0, ((0, 32),))
    w_up = scatter_about(streams_of[4], (EXPERTS, FF, D), D ** -0.5, 0.25, ((0, 16),))
    w_down = scatter_about(streams_of[5], (EXPERTS, FF, D), FF ** -0.5, 0.125, ((0, 16),))
    return {"tokens": tokens, "gates": gates, "routes": routes, "cotangent": cotangent, "w_up": w_up, "w_down": w_down}


def silu_parts(preact):
    sigma = jax.nn.sigmoid(preact)
    return preact * sigma, sigma * (1.0 + preact * (1.0 - sigma))


def expert_pass(operands):
    up_mat, down_mat, rows_in, grad_in, gate_in = operands
    preact = jnp.dot(rows_in, up_mat.T, preferred_element_type=jnp.float32)
    active, slopes = silu_parts(preact)
    hidden = active.astype(jnp.bfloat16)
    output = jnp.dot(hidden, down_mat, preferred_element_type=jnp.float32)
    gate_grad = jnp.sum(grad_in.astype(jnp.float32) * output, axis=1).astype(jnp.bfloat16)
    out_grad = (gate_in.astype(jnp.float32)[:, None] * grad_in.astype(jnp.float32)).astype(jnp.bfloat16)
    hid_grad = (jnp.dot(out_grad, down_mat.T, preferred_element_type=jnp.float32) * slopes).astype(jnp.bfloat16)
    in_grad = jnp.dot(hid_grad, up_mat, preferred_element_type=jnp.float32).astype(jnp.bfloat16)
    up_part = jnp.dot(hid_grad.T, rows_in, preferred_element_type=jnp.float32).astype(jnp.bfloat16)
    down_part = jnp.dot(hidden.T, out_grad, preferred_element_type=jnp.float32).astype(jnp.bfloat16)
    return in_grad, gate_grad, up_part, down_part


def reference(tokens, gates, routes, cotangent, w_up, w_down):
    per_mirror = N_EXP * T_DEV
    slots_all = N_EXP * CAP

    def mirror_step(totals, operands):
        tok_part, gate_part, route_part, cot_part = operands
        tok_rows = tok_part.shape[0]
        assigned = 2 * tok_rows
        flat_ids = route_part.reshape(-1).astype(jnp.int32)
        onehot = (flat_ids[:, None] == jnp.arange(EXPERTS).astype(jnp.int32)[None, :]).astype(jnp.int32)
        slot_pos = jnp.sum((jnp.cumsum(onehot, axis=0) - 1) * onehot, axis=1).astype(jnp.int32)
        source = jnp.full((EXPERTS, slots_all), assigned, jnp.int32)
        source = source.at[flat_ids, slot_pos].set(jnp.arange(assigned).astype(jnp.int32))
        padded_tok = jnp.concatenate([tok_part, jnp.zeros((1, D), tok_part.dtype)], axis=0)
        padded_cot = jnp.concatenate([cot_part, jnp.zeros((1, D), cot_part.dtype)], axis=0)
        padded_gate = jnp.concatenate([gate_part.reshape(-1), jnp.zeros((1,), gate_part.dtype)], axis=0)
        rows_in = padded_tok[source // 2]
        grad_in = padded_cot[source // 2]
        gate_in = padded_gate[source]
        in_grad, gate_grad, up_part, down_part = lax.map(expert_pass, (w_up, w_down, rows_in, grad_in, gate_in))
        flat_source = source.reshape(-1)
        tok_grad = jnp.zeros((assigned + 1, D), jnp.float32).at[flat_source].add(in_grad.reshape(-1, D).astype(jnp.float32))
        tok_grad = tok_grad[:assigned].reshape(tok_rows, 2, D).sum(axis=1).astype(jnp.bfloat16)
        gate_out = jnp.zeros((assigned + 1,), jnp.bfloat16).at[flat_source].set(gate_grad.reshape(-1))
        gate_out = gate_out[:assigned].reshape(tok_rows, 2)
        totals = (totals[0] + up_part.astype(jnp.float32), totals[1] + down_part.astype(jnp.float32))
        return totals, (tok_grad, gate_out)

    def split(array):
        return array.reshape((N_REP, per_mirror) + array.shape[1:])

    start = (jnp.zeros((EXPERTS, FF, D), jnp.float32), jnp.zeros((EXPERTS, FF, D), jnp.float32))
    totals, outs = lax.scan(mirror_step, start, (split(tokens), split(gates), split(routes), split(cotangent)))
    tok_grads, gate_grads = outs
    return (tok_grads.reshape(TOKENS, D), gate_grads.reshape(TOKENS, 2),
            totals[0].astype(jnp.bfloat16), totals[1].astype(jnp.bfloat16))
```

```python
import functools

import jax
import jax.numpy as jnp
from jax import lax
from jax.experimental import pallas as pl
from jax.experimental.pallas import tpu as pltpu
from jax.sharding import PartitionSpec as P

F32 = jnp.float32
BF16 = jnp.bfloat16
VMEM_LIMIT = 40 * 1024 * 1024


def dot(left, right, left_dim, right_dim):
    return lax.dot_general(
        left, right, (((left_dim,), (right_dim,)), ((), ())), preferred_element_type=F32
    )


def silu_parts(preact):
    sigma = 0.5 * jnp.tanh(0.5 * preact) + 0.5
    active = preact * sigma
    return active, sigma + active * (1.0 - sigma)


def call(body, name, outs, args, flops, transcendentals=0):
    moved = sum(a.size * a.dtype.itemsize for a in (*args, *outs))
    return pl.pallas_call(
        body,
        name=name,
        out_shape=outs,
        in_specs=[pl.BlockSpec(memory_space=pltpu.VMEM)] * len(args),
        out_specs=[pl.BlockSpec(memory_space=pltpu.VMEM)] * len(outs),
        compiler_params=pltpu.CompilerParams(vmem_limit_bytes=VMEM_LIMIT),
        cost_estimate=pl.CostEstimate(
            flops=flops, bytes_accessed=moved, transcendentals=transcendentals
        ),
    )(*args)


def slots_of(routes, groups):
    rows = routes.shape[1]
    expert = lax.broadcasted_iota(jnp.int32, (groups, rows), 0)
    hot = [expert == routes[k : k + 1, :] for k in range(2)]
    as_num = [jnp.where(h, 1.0, 0.0).astype(F32) for h in hot]
    before = jnp.where(
        lax.broadcasted_iota(jnp.int32, (rows, rows), 0)
        < lax.broadcasted_iota(jnp.int32, (rows, rows), 1),
        1.0,
        0.0,
    ).astype(BF16)
    count = [dot(n.astype(BF16), before, 1, 0) for n in as_num]
    total = jnp.sum(as_num[0], axis=1, keepdims=True)
    place = [count[0], count[1] + total]
    slot = [
        jnp.sum(jnp.where(h, p, 0.0), axis=0, keepdims=True).astype(jnp.int32)
        for h, p in zip(hot, place)
    ]
    return hot, slot


def dispatch_kernel(groups, pad, routes_ref, gates_ref, tok_ref, cot_ref, out_ref, pick_ref):
    routes = routes_ref[...]
    gates = gates_ref[...].astype(F32)
    _, slot = slots_of(routes, groups)
    rows = routes.shape[1]
    index = lax.broadcasted_iota(jnp.int32, (groups * pad, rows), 0)
    pick = [index == routes[k : k + 1, :] * pad + slot[k] for k in range(2)]
    plain = jnp.where(pick[0] | pick[1], 1.0, 0.0).astype(BF16)
    scaled = (
        jnp.where(pick[0], gates[0:1, :], 0.0) + jnp.where(pick[1], gates[1:2, :], 0.0)
    ).astype(BF16)
    pick_ref[...] = plain
    feat = tok_ref.shape[1]
    out_ref[:, 0:pad, :] = dot(plain, tok_ref[...], 1, 0).astype(BF16).reshape(groups, pad, feat)
    out_ref[:, pad:, :] = dot(scaled, cot_ref[...], 1, 0).astype(BF16).reshape(groups, pad, feat)


def own_kernel(cap, block, disp_ref, up_ref, down_ref, out_ref, grad_acc, gate_acc):
    groups, both, feat = disp_ref.shape
    pad = both // 2
    slots = groups * pad
    rows = disp_ref[:, 0:pad, :].reshape(slots, feat)
    grads = disp_ref[:, pad:, :].reshape(slots, feat)
    for step in range(up_ref.shape[1] // block):
        part = pl.ds(step * block, block)
        up = up_ref[0, part, :]
        down = down_ref[0, part, :]
        active, slope = silu_parts(dot(rows, up, 1, 1))
        back = dot(grads, down, 1, 1)
        hid_grad = (back * slope).astype(BF16)
        gate = active.astype(BF16).astype(F32) * back
        gate = sum(gate[:, i : i + 128] for i in range(0, block, 128))
        in_grad = dot(hid_grad, up, 1, 0)
        if step == 0:
            grad_acc[...] = in_grad
            gate_acc[...] = gate
        else:
            grad_acc[...] += in_grad
            gate_acc[...] += gate
    gate = jnp.sum(gate_acc[...], axis=1, keepdims=True)
    spot = lax.broadcasted_iota(jnp.int32, (slots, 128), 0) % pad
    lane = lax.broadcasted_iota(jnp.int32, (slots, 128), 1)
    gate = jnp.where(spot == lane, gate, 0.0).reshape(groups, pad, 128)
    gate = jnp.sum(gate, axis=1, keepdims=True)
    grad = grad_acc[...].reshape(groups, pad, feat)
    line = lax.broadcasted_iota(jnp.int32, (groups, pad, 128), 1)
    out_ref[:, :, 0:128] = jnp.where(line == cap, gate, grad[:, :, 0:128]).astype(BF16)
    out_ref[:, :, 128:] = grad[:, :, 128:].astype(BF16)


def weights_kernel(block, share, *refs):
    mirror_refs = refs[:-6]
    up_ref, down_ref, grad_up_ref, grad_down_ref, up_acc, down_acc = refs[-6:]
    base = lax.axis_index("rep") * share
    pairs = []
    own = mirror_refs[0]
    pad = own.shape[1] // 2
    slots = own.shape[0] * pad
    feat = own.shape[2]
    pairs.append((own[:, 0:pad, :].reshape(slots, feat), own[:, pad:, :].reshape(slots, feat)))
    for i in range(1, len(mirror_refs), 2):
        pairs.append((mirror_refs[i][...], mirror_refs[i + 1][...]))
    for number, (rows, grads) in enumerate(pairs):
        for step in range(share // block):
            part = pl.ds(pl.multiple_of(base + step * block, block), block)
            here = pl.ds(step * block, block)
            active, slope = silu_parts(dot(up_ref[0, part, :], rows, 1, 1))
            hid_grad = (dot(down_ref[0, part, :], grads, 1, 1) * slope).astype(BF16)
            up_part = dot(hid_grad, rows, 1, 0)
            down_part = dot(active.astype(BF16), grads, 1, 0)
            if number:
                up_part += up_acc[here, :]
                down_part += down_acc[here, :]
            if number == len(pairs) - 1:
                grad_up_ref[0, here, :] = up_part.astype(BF16)
                grad_down_ref[0, here, :] = down_part.astype(BF16)
            else:
                up_acc[here, :] = up_part
                down_acc[here, :] = down_part


def combine_kernel(cap, routes_ref, gates_ref, pick_ref, back_ref, d_tok_ref, d_gate_ref):
    groups, pad, feat = back_ref.shape
    back = back_ref[...]
    d_tok_ref[...] = dot(pick_ref[...], back.reshape(groups * pad, feat), 0, 0).astype(BF16)
    routes = routes_ref[...]
    gates = gates_ref[...].astype(F32)
    hot, slot = slots_of(routes, groups)
    lane = lax.broadcasted_iota(jnp.int32, (128, routes.shape[1]), 0)
    values = back[:, cap, 0:128]
    for k in range(2):
        spot = jnp.where(lane == slot[k], 1.0, 0.0).astype(BF16)
        found = jnp.where(hot[k], dot(values, spot, 1, 0), 0.0)
        found = jnp.sum(found, axis=0, keepdims=True)
        d_gate_ref[k : k + 1, :] = (found / gates[k : k + 1, :]).astype(BF16)


def local(tokens, gates, routes, cotangent, w_up, w_down):
    rows, feat = tokens.shape
    hidden = w_up.shape[1]
    groups = lax.axis_size("exp")
    mirrors = lax.axis_size("rep")
    cap = max(2, 3 * rows // groups)
    pad = (cap // 16 + 1) * 16
    slots = groups * pad
    share = hidden // mirrors
    routes_t, gates_t = routes.T, gates.T
    shape = jax.ShapeDtypeStruct
    unit = 2 * slots * feat

    out, pick = call(
        functools.partial(dispatch_kernel, groups, pad),
        "dispatch",
        [shape((groups, 2 * pad, feat), BF16), shape((slots, rows), BF16)],
        [routes_t, gates_t, tokens, cotangent],
        2 * unit * rows,
    )
    disp = lax.all_to_all(out, "exp", split_axis=0, concat_axis=0, tiled=True)
    rows_in = disp[:, 0:pad, :].reshape(slots, feat)
    grads_in = disp[:, pad:, :].reshape(slots, feat)
    others = []
    for shift in range(1, mirrors):
        hops = [(i, (i + shift) % mirrors) for i in range(mirrors)]
        others.append(lax.ppermute(rows_in, "rep", hops))
        others.append(lax.ppermute(grads_in, "rep", hops))

    block = min(512, hidden)
    (back,) = pl.pallas_call(
        functools.partial(own_kernel, cap, block),
        name="own_mirror",
        out_shape=[shape((groups, pad, feat), BF16)],
        in_specs=[pl.BlockSpec(memory_space=pltpu.VMEM)] * 3,
        out_specs=[pl.BlockSpec(memory_space=pltpu.VMEM)],
        scratch_shapes=[pltpu.VMEM((slots, feat), F32), pltpu.VMEM((slots, 128), F32)],
        compiler_params=pltpu.CompilerParams(vmem_limit_bytes=VMEM_LIMIT),
        cost_estimate=pl.CostEstimate(
            flops=3 * unit * hidden,
            bytes_accessed=4 * hidden * feat + 6 * slots * feat,
            transcendentals=slots * hidden,
        ),
    )(disp, w_up, w_down)
    back = lax.all_to_all(back, "exp", split_axis=0, concat_axis=0, tiled=True)

    part = min(512, share)
    grad_up, grad_down = pl.pallas_call(
        functools.partial(weights_kernel, part, share),
        name="weight_grads",
        out_shape=[shape((1, share, feat), BF16)] * 2,
        in_specs=[pl.BlockSpec(memory_space=pltpu.VMEM)] * (len(others) + 3),
        out_specs=[pl.BlockSpec(memory_space=pltpu.VMEM)] * 2,
        scratch_shapes=[pltpu.VMEM((share, feat), F32)] * 2,
        compiler_params=pltpu.CompilerParams(vmem_limit_bytes=VMEM_LIMIT),
        cost_estimate=pl.CostEstimate(
            flops=4 * unit * share * mirrors,
            bytes_accessed=8 * hidden * feat,
            transcendentals=slots * hidden,
        ),
    )(disp, *others, w_up, w_down)

    d_tokens, d_gates = call(
        functools.partial(combine_kernel, cap),
        "combine",
        [shape((rows, feat), BF16), shape((2, rows), BF16)],
        [routes_t, gates_t, pick, back],
        unit * rows,
    )
    return d_tokens, d_gates.T, grad_up, grad_down


def solution(mesh):
    by_both = P(("rep", "exp"), None)
    by_expert = P("exp", None, None)
    return jax.shard_map(
        local,
        mesh=mesh,
        in_specs=(by_both, by_both, by_both, by_both, by_expert, by_expert),
        out_specs=(by_both, by_both, P("exp", "rep", None), P("exp", "rep", None)),
        check_vma=False,
    )
```

```python
import functools
import itertools

import jax
import jax.numpy as jnp
from jax import lax
from jax.experimental import pallas as pl
from jax.experimental.pallas import tpu as pltpu
from jax.sharding import PartitionSpec as P

F32 = jnp.float32
BF16 = jnp.bfloat16
VMEM_LIMIT = 40 * 1024 * 1024
IN_HBM = pl.BlockSpec(memory_space=pltpu.HBM)
IN_VMEM = pl.BlockSpec(memory_space=pltpu.VMEM)
DMA = pltpu.SemaphoreType.DMA


def dot(left, right, left_dim, right_dim):
    return lax.dot_general(
        left, right, (((left_dim,), (right_dim,)), ((), ())), preferred_element_type=F32
    )


def silu_parts(preact):
    sigma = 0.5 * jnp.tanh(0.5 * preact) + 0.5
    active = preact * sigma
    return active, sigma + active * (1.0 - sigma)


def call(body, name, outs, args, in_specs, scratch, flops, transcendentals=0):
    moved = sum(a.size * a.dtype.itemsize for a in (*args, *outs))
    return pl.pallas_call(
        body,
        name=name,
        out_shape=outs,
        in_specs=in_specs,
        out_specs=[IN_VMEM] * len(outs),
        scratch_shapes=scratch,
        compiler_params=pltpu.CompilerParams(vmem_limit_bytes=VMEM_LIMIT),
        cost_estimate=pl.CostEstimate(
            flops=flops, bytes_accessed=moved, transcendentals=transcendentals
        ),
    )(*args)


def paired(groups):
    return groups & (groups - 1) == 0


def hops_to(groups, k):
    if paired(groups):
        return [(i, i ^ k) for i in range(groups)]
    return [(i, (i + k) % groups) for i in range(groups)]


def issue_order(groups):
    far, near = range(groups // 2, groups), range(1, groups // 2)
    return [k for pair in itertools.zip_longest(far, near) for k in pair if k is not None]


def pieces_of(routes, groups):
    me = lax.axis_index("exp")
    if paired(groups):
        return routes ^ me
    return (routes - me + groups) % groups


def slots_of(pieces, groups):
    rows = pieces.shape[1]
    number = lax.broadcasted_iota(jnp.int32, (groups, rows), 0)
    hot = [number == pieces[k : k + 1, :] for k in range(2)]
    as_num = [jnp.where(h, 1.0, 0.0).astype(F32) for h in hot]
    before = jnp.where(
        lax.broadcasted_iota(jnp.int32, (rows, rows), 0)
        < lax.broadcasted_iota(jnp.int32, (rows, rows), 1),
        1.0,
        0.0,
    ).astype(BF16)
    count = [dot(n.astype(BF16), before, 1, 0) for n in as_num]
    total = jnp.sum(as_num[0], axis=1, keepdims=True)
    place = [count[0], count[1] + total]
    slot = [
        jnp.sum(jnp.where(h, p, 0.0), axis=0, keepdims=True).astype(jnp.int32)
        for h, p in zip(hot, place)
    ]
    return hot, slot


def dispatch_kernel(groups, pad, routes_hbm, gates_hbm, tok_hbm, cot_hbm, *refs):
    out_refs, pick_ref = refs[:groups], refs[groups]
    routes_ref, gates_ref, tok_ref, cot_ref, sems = refs[groups + 1 :]
    copies = [
        pltpu.make_async_copy(src, dst, sems.at[i])
        for i, (src, dst) in enumerate(
            [
                (routes_hbm, routes_ref),
                (gates_hbm, gates_ref),
                (tok_hbm, tok_ref),
                (cot_hbm, cot_ref),
            ]
        )
    ]
    for copy in copies:
        copy.start()
    copies[0].wait()
    copies[1].wait()
    pieces = pieces_of(routes_ref[...], groups)
    gates = gates_ref[...].astype(F32)
    _, slot = slots_of(pieces, groups)
    index = lax.broadcasted_iota(jnp.int32, (groups * pad, pieces.shape[1]), 0)
    pick = [index == pieces[k : k + 1, :] * pad + slot[k] for k in range(2)]
    plain = jnp.where(pick[0] | pick[1], 1.0, 0.0).astype(BF16)
    scaled = (
        jnp.where(pick[0], gates[0:1, :], 0.0) + jnp.where(pick[1], gates[1:2, :], 0.0)
    ).astype(BF16)
    pick_ref[...] = plain
    copies[2].wait()
    copies[3].wait()
    rows = dot(plain, tok_ref[...], 1, 0).astype(BF16)
    grads = dot(scaled, cot_ref[...], 1, 0).astype(BF16)
    for k, out_ref in enumerate(out_refs):
        out_ref[0:pad, :] = rows[k * pad : (k + 1) * pad, :]
        out_ref[pad:, :] = grads[k * pad : (k + 1) * pad, :]


def own_kernel(cap, groups, block, early, *refs):
    piece_refs, refs = refs[early : early + groups], refs[early + groups :]
    up_hbm, down_hbm = refs[:2]
    out_refs, refs = refs[2 : 2 + groups], refs[2 + groups :]
    rows_ref, grads_ref, up_ref, down_ref, grad_acc, gate_acc, sems = refs
    steps = up_ref.shape[0] // block
    slots, feat = rows_ref.shape
    pad = slots // groups
    copies = []
    for step in range(steps):
        part = pl.ds(step * block, block)
        for i, (src, dst) in enumerate([(up_hbm, up_ref), (down_hbm, down_ref)]):
            copies.append(
                pltpu.make_async_copy(src.at[0, part, :], dst.at[part, :], sems.at[2 * step + i])
            )
            copies[-1].start()
    for k, piece_ref in enumerate(piece_refs):
        rows_ref[k * pad : (k + 1) * pad, :] = piece_ref[0:pad, :]
        grads_ref[k * pad : (k + 1) * pad, :] = piece_ref[pad:, :]
    for step in range(steps):
        part = pl.ds(step * block, block)
        copies[2 * step].wait()
        up = up_ref[part, :]
        active, slope = silu_parts(dot(rows_ref[...], up, 1, 1))
        copies[2 * step + 1].wait()
        back = dot(grads_ref[...], down_ref[part, :], 1, 1)
        hid_grad = (back * slope).astype(BF16)
        gate = active.astype(BF16).astype(F32) * back
        gate = sum(gate[:, i : i + 128] for i in range(0, block, 128))
        in_grad = dot(hid_grad, up, 1, 0)
        if step == 0:
            grad_acc[...] = in_grad
            gate_acc[...] = gate
        else:
            grad_acc[...] += in_grad
            gate_acc[...] += gate
    gate = jnp.sum(gate_acc[...], axis=1, keepdims=True)
    spot = lax.broadcasted_iota(jnp.int32, (slots, 128), 0) % pad
    lane = lax.broadcasted_iota(jnp.int32, (slots, 128), 1)
    gate = jnp.where(spot == lane, gate, 0.0).reshape(groups, pad, 128)
    gate = jnp.sum(gate, axis=1, keepdims=True)
    line = lax.broadcasted_iota(jnp.int32, (pad, 128), 0)
    for k, out_ref in enumerate(out_refs):
        here = slice(k * pad, (k + 1) * pad)
        out_ref[:, 0:128] = jnp.where(line == cap, gate[k], grad_acc[here, 0:128]).astype(BF16)
        out_ref[:, 128:] = grad_acc[here, 128:].astype(BF16)


def weight_parts(block, share, rows_ref, grads_ref, up_ref, down_ref, store):
    for step in range(share // block):
        here = pl.ds(step * block, block)
        active, slope = silu_parts(dot(up_ref[here, :], rows_ref[...], 1, 1))
        back = dot(down_ref[here, :], grads_ref[...], 1, 1)
        hid_grad = (back * slope).astype(BF16)
        up_part = dot(hid_grad, rows_ref[...], 1, 0)
        down_part = dot(active.astype(BF16), grads_ref[...], 1, 0)
        store(here, up_part, down_part)


def own_weights_kernel(block, share, rows_ref, grads_ref, up_hbm, down_hbm, *refs):
    up_out, down_out, up_acc, down_acc, up_ref, down_ref, sems = refs
    base = pl.multiple_of(lax.axis_index("rep") * share, share)
    copies = [
        pltpu.make_async_copy(src.at[0, pl.ds(base, share), :], dst, sems.at[i])
        for i, (src, dst) in enumerate([(up_hbm, up_ref), (down_hbm, down_ref)])
    ]
    for copy in copies:
        copy.start()
    for copy in copies:
        copy.wait()
    up_out[...] = up_ref[...]
    down_out[...] = down_ref[...]

    def store(here, up_part, down_part):
        up_acc[here, :] = up_part
        down_acc[here, :] = down_part

    weight_parts(block, share, rows_ref, grads_ref, up_ref, down_ref, store)


def other_weights_kernel(block, share, groups, mirrors, *refs):
    pieces, refs = refs[:-8], refs[-8:]
    up_ref, down_ref, up_acc, down_acc, grad_up_ref, grad_down_ref, rows_ref, grads_ref = refs
    pad = rows_ref.shape[0] // groups
    each = len(pieces) // (mirrors - 1)
    batch = groups // each
    for mirror in range(mirrors - 1):
        for k in range(groups):
            piece = pieces[mirror * each + k // batch]
            at = k % batch * 2 * pad
            here = slice(k * pad, (k + 1) * pad)
            rows_ref[here, :] = piece[at : at + pad, :]
            grads_ref[here, :] = piece[at + pad : at + 2 * pad, :]

        def store(here, up_part, down_part):
            up_part += up_acc[here, :]
            down_part += down_acc[here, :]
            if mirror == mirrors - 2:
                grad_up_ref[0, here, :] = up_part.astype(BF16)
                grad_down_ref[0, here, :] = down_part.astype(BF16)
            else:
                up_acc[here, :] = up_part
                down_acc[here, :] = down_part

        weight_parts(block, share, rows_ref, grads_ref, up_ref, down_ref, store)


def combine_kernel(cap, routes_ref, gates_ref, pick_ref, *refs):
    back_refs, d_tok_ref, d_gate_ref, back_ref = refs[:-3], refs[-3], refs[-2], refs[-1]
    groups = len(back_refs)
    pad = back_refs[0].shape[0]
    for k, ref in enumerate(back_refs):
        back_ref[k * pad : (k + 1) * pad, :] = ref[...]
    d_tok_ref[...] = dot(pick_ref[...], back_ref[...], 0, 0).astype(BF16)
    pieces = pieces_of(routes_ref[...], groups)
    gates = gates_ref[...].astype(F32)
    hot, slot = slots_of(pieces, groups)
    lane = lax.broadcasted_iota(jnp.int32, (128, pieces.shape[1]), 0)
    values = jnp.concatenate([ref[cap : cap + 1, 0:128].astype(F32) for ref in back_refs], axis=0)
    for k in range(2):
        spot = jnp.where(lane == slot[k], 1.0, 0.0).astype(BF16)
        found = jnp.where(hot[k], dot(values.astype(BF16), spot, 1, 0), 0.0)
        found = jnp.sum(found, axis=0, keepdims=True)
        d_gate_ref[k : k + 1, :] = (found / gates[k : k + 1, :]).astype(BF16)


def local(tokens, gates, routes, cotangent, w_up, w_down):
    rows, feat = tokens.shape
    hidden = w_up.shape[1]
    groups = lax.axis_size("exp")
    mirrors = lax.axis_size("rep")
    cap = max(2, 3 * rows // groups)
    pad = (cap // 16 + 1) * 16
    slots = groups * pad
    share = hidden // mirrors
    routes_t, gates_t = routes.T, gates.T
    far = functools.partial(pltpu.with_memory_space_constraint, memory_space=pltpu.HBM)
    shape = jax.ShapeDtypeStruct
    unit = 2 * slots * feat

    *out, pick = call(
        functools.partial(dispatch_kernel, groups, pad),
        "dispatch",
        [shape((2 * pad, feat), BF16)] * groups + [shape((slots, rows), BF16)],
        [far(routes_t), far(gates_t), far(tokens), far(cotangent)],
        [IN_HBM] * 4,
        [
            pltpu.VMEM((2, rows), jnp.int32),
            pltpu.VMEM((2, rows), BF16),
            pltpu.VMEM((rows, feat), BF16),
            pltpu.VMEM((rows, feat), BF16),
            DMA((4,)),
        ],
        2 * unit * rows,
    )
    order = issue_order(groups)
    pieces = {0: out[0]}
    for k in order:
        pieces[k] = lax.ppermute(out[k], "exp", hops_to(groups, k))

    pieces = list(pieces.values())
    batch = max(1, groups // 4)
    others = []
    for shift in range(1, mirrors):
        hops = [(i, (i + shift) % mirrors) for i in range(mirrors)]
        for k in range(0, groups, batch):
            group = jnp.concatenate(pieces[k : k + batch], axis=0)
            others.append(lax.ppermute(group, "rep", hops))

    block = min(512, hidden)
    early = others[:3]
    *back, rows_in, grads_in = pl.pallas_call(
        functools.partial(own_kernel, cap, groups, block, len(early)),
        name="own_mirror",
        out_shape=[shape((pad, feat), BF16)] * groups + [shape((slots, feat), BF16)] * 2,
        in_specs=[pl.BlockSpec(memory_space=pl.ANY)] * len(early) + [IN_VMEM] * groups + [IN_HBM] * 2,
        out_specs=[IN_VMEM] * (groups + 2),
        scratch_shapes=[
            pltpu.VMEM((hidden, feat), BF16),
            pltpu.VMEM((hidden, feat), BF16),
            pltpu.VMEM((slots, feat), F32),
            pltpu.VMEM((slots, 128), F32),
            DMA((2 * hidden // block,)),
        ],
        compiler_params=pltpu.CompilerParams(vmem_limit_bytes=VMEM_LIMIT),
        cost_estimate=pl.CostEstimate(
            flops=3 * unit * hidden,
            bytes_accessed=4 * hidden * feat + 6 * slots * feat,
            transcendentals=slots * hidden,
        ),
    )(*early, *pieces, far(w_up), far(w_down))
    returned = {0: back[0]}
    for number, k in enumerate(order):
        hops = [(j, i) for i, j in hops_to(groups, k)]
        returned[k] = lax.ppermute(back[number + 1], "exp", hops)
    back = [returned[k] for k in range(groups)]

    part = min(512, share)
    weight = shape((share, feat), BF16)
    total = shape((share, feat), F32)
    up_own, down_own, up_sum, down_sum = call(
        functools.partial(own_weights_kernel, part, share),
        "own_weights",
        [weight, weight, total, total],
        [rows_in, grads_in, far(w_up), far(w_down)],
        [IN_VMEM] * 2 + [IN_HBM] * 2,
        [pltpu.VMEM((share, feat), BF16)] * 2 + [DMA((2,))],
        4 * unit * share,
        slots * share,
    )
    if mirrors == 1:
        grad_up, grad_down = up_sum.astype(BF16)[None], down_sum.astype(BF16)[None]
    else:
        grad_up, grad_down = call(
            functools.partial(other_weights_kernel, part, share, groups, mirrors),
            "other_weights",
            [shape((1, share, feat), BF16)] * 2,
            [*others, up_own, down_own, up_sum, down_sum],
            [IN_VMEM] * (len(others) + 4),
            [pltpu.VMEM((slots, feat), BF16)] * 2,
            4 * unit * share * (mirrors - 1),
            slots * share,
        )

    d_tokens, d_gates = call(
        functools.partial(combine_kernel, cap),
        "combine",
        [shape((rows, feat), BF16), shape((2, rows), BF16)],
        [routes_t, gates_t, pick, *back],
        [IN_VMEM] * (3 + groups),
        [pltpu.VMEM((slots, feat), BF16)],
        unit * rows,
    )
    return d_tokens, d_gates.T, grad_up, grad_down


def solution(mesh):
    by_both = P(("rep", "exp"), None)
    by_expert = P("exp", None, None)
    return jax.shard_map(
        local,
        mesh=mesh,
        in_specs=(by_both, by_both, by_both, by_both, by_expert, by_expert),
        out_specs=(by_both, by_both, P("exp", "rep", None), P("exp", "rep", None)),
        check_vma=False,
    )
```

```python
import functools

import jax
import jax.numpy as jnp
from jax import lax
from jax.experimental import pallas as pl
from jax.experimental.pallas import tpu as pltpu
from jax.sharding import PartitionSpec as P

F32 = jnp.float32
BF16 = jnp.bfloat16
VMEM_LIMIT = 32 * 1024 * 1024
IN_HBM = pl.BlockSpec(memory_space=pltpu.HBM)
IN_VMEM = pl.BlockSpec(memory_space=pltpu.VMEM)
DMA = pltpu.SemaphoreType.DMA


def dot(left, right, left_dim, right_dim):
    return lax.dot_general(
        left, right, (((left_dim,), (right_dim,)), ((), ())), preferred_element_type=F32
    )


def silu_parts(preact):
    sigma = 0.5 * jnp.tanh(0.5 * preact) + 0.5
    active = preact * sigma
    return active, sigma + active * (1.0 - sigma)


def call(body, name, outs, args, in_specs, scratch, flops, transcendentals=0):
    moved = sum(a.size * a.dtype.itemsize for a in (*args, *outs))
    return pl.pallas_call(
        body,
        name=name,
        out_shape=outs,
        in_specs=in_specs,
        out_specs=[IN_VMEM] * len(outs),
        scratch_shapes=scratch,
        compiler_params=pltpu.CompilerParams(vmem_limit_bytes=VMEM_LIMIT),
        cost_estimate=pl.CostEstimate(
            flops=flops, bytes_accessed=moved, transcendentals=transcendentals
        ),
    )(*args)


def slots_of(routes, experts, first):
    rows = routes.shape[1]
    number = lax.broadcasted_iota(jnp.int32, (experts, rows), 0) + first
    hot = [number == routes[k : k + 1, :] for k in range(2)]
    as_num = [jnp.where(h, 1.0, 0.0).astype(F32) for h in hot]
    before = jnp.where(
        lax.broadcasted_iota(jnp.int32, (rows, rows), 0)
        < lax.broadcasted_iota(jnp.int32, (rows, rows), 1),
        1.0,
        0.0,
    ).astype(BF16)
    count = [dot(n.astype(BF16), before, 1, 0) for n in as_num]
    total = jnp.sum(as_num[0], axis=1, keepdims=True)
    place = [count[0], count[1] + total]
    slot = [
        jnp.sum(jnp.where(h, p, 0.0), axis=0, keepdims=True).astype(jnp.int32)
        for h, p in zip(hot, place)
    ]
    return hot, slot


def picks_of(routes, experts, first, pad):
    _, slot = slots_of(routes, experts, first)
    index = lax.broadcasted_iota(jnp.int32, (experts * pad, routes.shape[1]), 0)
    return [index == (routes[k : k + 1, :] - first) * pad + slot[k] for k in range(2)]


def fill_slots(routes, gates, tok_ref, cot_ref, out_ref, ready):
    experts, both, feat = out_ref.shape
    pad = both // 2
    first = lax.axis_index("exp") // experts * experts
    pick = picks_of(routes, experts, first, pad)
    gates = gates.astype(F32)
    plain = jnp.where(pick[0] | pick[1], 1.0, 0.0).astype(BF16)
    scaled = (
        jnp.where(pick[0], gates[0:1, :], 0.0) + jnp.where(pick[1], gates[1:2, :], 0.0)
    ).astype(BF16)
    ready()
    out_ref[:, 0:pad, :] = dot(plain, tok_ref[...], 1, 0).astype(BF16).reshape(experts, pad, feat)
    out_ref[:, pad:, :] = dot(scaled, cot_ref[...], 1, 0).astype(BF16).reshape(experts, pad, feat)


def near_kernel(routes_hbm, gates_hbm, tok_hbm, cot_hbm, up_hbm, down_hbm, *refs):
    out_ref, up_ref, down_ref, routes_ref, gates_ref, tok_ref, cot_ref, sems = refs
    pairs = [
        (routes_hbm, routes_ref),
        (gates_hbm, gates_ref),
        (tok_hbm, tok_ref),
        (cot_hbm, cot_ref),
        (up_hbm.at[0], up_ref),
        (down_hbm.at[0], down_ref),
    ]
    copies = [
        pltpu.make_async_copy(src, dst, sems.at[i]) for i, (src, dst) in enumerate(pairs)
    ]
    for copy in copies:
        copy.start()
    copies[0].wait()
    copies[1].wait()

    def ready():
        copies[2].wait()
        copies[3].wait()

    fill_slots(routes_ref[...], gates_ref[...], tok_ref, cot_ref, out_ref, ready)
    copies[4].wait()
    copies[5].wait()


def far_kernel(routes_ref, gates_ref, tok_ref, cot_ref, out_ref):
    fill_slots(routes_ref[...], gates_ref[...], tok_ref, cot_ref, out_ref, lambda: None)


def split_rows(ref):
    experts, both, feat = ref.shape
    pad = both // 2
    return (
        ref[:, 0:pad, :].reshape(experts * pad, feat),
        ref[:, pad:, :].reshape(experts * pad, feat),
    )


def backward(cap, block, disp_ref, up_ref, down_ref, grad_acc, gate_acc, put):
    origins, both, feat = disp_ref.shape
    pad = both // 2
    slots = origins * pad
    rows, grads = split_rows(disp_ref)
    for step in range(up_ref.shape[0] // block):
        part = pl.ds(step * block, block)
        up = up_ref[part, :]
        active, slope = silu_parts(dot(rows, up, 1, 1))
        back = dot(grads, down_ref[part, :], 1, 1)
        hid_grad = (back * slope).astype(BF16)
        gate = active.astype(BF16).astype(F32) * back
        gate = sum(gate[:, i : i + 128] for i in range(0, block, 128))
        in_grad = dot(hid_grad, up, 1, 0)
        if step == 0:
            grad_acc[...] = in_grad
            gate_acc[...] = gate
        else:
            grad_acc[...] += in_grad
            gate_acc[...] += gate
    gate = jnp.sum(gate_acc[...], axis=1, keepdims=True)
    spot = lax.broadcasted_iota(jnp.int32, (slots, 128), 0) % pad
    lane = lax.broadcasted_iota(jnp.int32, (slots, 128), 1)
    gate = jnp.where(spot == lane, gate, 0.0).reshape(origins, pad, 128)
    gate = jnp.sum(gate, axis=1, keepdims=True)
    line = lax.broadcasted_iota(jnp.int32, (pad, 128), 0)
    for k in range(origins):
        here = slice(k * pad, (k + 1) * pad)
        first = jnp.where(line == cap, gate[k], grad_acc[here, 0:128])
        put(k, first.astype(BF16), grad_acc[here, 128:].astype(BF16))


def near_back_kernel(cap, block, routes_ref, disp_ref, up_ref, down_ref, *refs):
    out_ref, pick_ref, grad_acc, gate_acc = refs

    def put(k, first, rest):
        out_ref[k, :, 0:128] = first
        out_ref[k, :, 128:] = rest

    backward(cap, block, disp_ref, up_ref, down_ref, grad_acc, gate_acc, put)
    pad = out_ref.shape[1]
    pick = picks_of(routes_ref[...], pick_ref.shape[0] // pad, 0, pad)
    pick_ref[...] = jnp.where(pick[0] | pick[1], 1.0, 0.0).astype(BF16)


def far_back_kernel(cap, block, near_ref, disp_ref, up_ref, down_ref, *refs):
    out_ref, grad_acc, gate_acc = refs
    half = lax.axis_index("exp") // near_ref.shape[0]
    out_ref[half] = near_ref[...]

    def put(k, first, rest):
        out_ref[1 - half, k, :, 0:128] = first
        out_ref[1 - half, k, :, 128:] = rest

    backward(cap, block, disp_ref, up_ref, down_ref, grad_acc, gate_acc, put)


def weight_parts(block, share, disp_refs, up_ref, down_ref, rows_ref, grads_ref, store):
    size = rows_ref.shape[0] // len(disp_refs)
    for i, ref in enumerate(disp_refs):
        here = slice(i * size, (i + 1) * size)
        rows_ref[here, :], grads_ref[here, :] = split_rows(ref)
    base = lax.axis_index("rep") * share
    for step in range(share // block):
        here = pl.ds(step * block, block)
        part = pl.ds(pl.multiple_of(base + step * block, block), block)
        active, slope = silu_parts(dot(up_ref[part, :], rows_ref[...], 1, 1))
        back = dot(down_ref[part, :], grads_ref[...], 1, 1)
        hid_grad = (back * slope).astype(BF16)
        up_part = dot(hid_grad, rows_ref[...], 1, 0)
        down_part = dot(active.astype(BF16), grads_ref[...], 1, 0)
        store(here, up_part, down_part)


def own_weights_kernel(block, share, near_ref, far_ref, up_ref, down_ref, *refs):
    up_acc, down_acc, rows_ref, grads_ref = refs

    def store(here, up_part, down_part):
        up_acc[here, :] = up_part
        down_acc[here, :] = down_part

    both = [near_ref, far_ref]
    weight_parts(block, share, both, up_ref, down_ref, rows_ref, grads_ref, store)


def other_weights_kernel(block, share, mirrors, *refs):
    pieces, refs = refs[:-8], refs[-8:]
    up_ref, down_ref, up_acc, down_acc, grad_up_ref, grad_down_ref, rows_ref, grads_ref = refs
    for mirror in range(mirrors - 1):

        def store(here, up_part, down_part):
            up_part += up_acc[here, :]
            down_part += down_acc[here, :]
            if mirror == mirrors - 2:
                grad_up_ref[0, here, :] = up_part.astype(BF16)
                grad_down_ref[0, here, :] = down_part.astype(BF16)
            else:
                up_acc[here, :] = up_part
                down_acc[here, :] = down_part

        both = pieces[2 * mirror : 2 * mirror + 2]
        weight_parts(block, share, both, up_ref, down_ref, rows_ref, grads_ref, store)


def combine_kernel(cap, routes_ref, gates_ref, pick_ref, back_ref, d_tok_ref, d_gate_ref):
    groups, pad, feat = back_ref.shape
    back = back_ref[...]
    d_tok_ref[...] = dot(pick_ref[...], back.reshape(groups * pad, feat), 0, 0).astype(BF16)
    routes = routes_ref[...]
    gates = gates_ref[...].astype(F32)
    hot, slot = slots_of(routes, groups, 0)
    lane = lax.broadcasted_iota(jnp.int32, (128, routes.shape[1]), 0)
    values = back[:, cap, 0:128]
    for k in range(2):
        spot = jnp.where(lane == slot[k], 1.0, 0.0).astype(BF16)
        found = jnp.where(hot[k], dot(values, spot, 1, 0), 0.0)
        found = jnp.sum(found, axis=0, keepdims=True)
        d_gate_ref[k : k + 1, :] = (found / gates[k : k + 1, :]).astype(BF16)


def local(tokens, gates, routes, cotangent, w_up, w_down):
    rows, feat = tokens.shape
    hidden = w_up.shape[1]
    groups = lax.axis_size("exp")
    mirrors = lax.axis_size("rep")
    cap = max(2, 3 * rows // groups)
    pad = (cap // 16 + 1) * 16
    half = groups // 2
    slots = half * pad
    share = hidden // mirrors
    routes_t, gates_t = routes.T, gates.T
    far = functools.partial(pltpu.with_memory_space_constraint, memory_space=pltpu.HBM)
    shape = jax.ShapeDtypeStruct
    unit = 2 * slots * feat
    disp_shape = shape((half, 2 * pad, feat), BF16)
    weight = shape((hidden, feat), BF16)

    across = [(i, (i + half) % groups) for i in range(groups)]
    partner = [lax.ppermute(a, "exp", across) for a in (routes_t, gates_t, tokens, cotangent)]

    near_out, up_v, down_v = call(
        near_kernel,
        "near_slots",
        [disp_shape, weight, weight],
        [far(a) for a in (routes_t, gates_t, tokens, cotangent, w_up, w_down)],
        [IN_HBM] * 6,
        [
            pltpu.VMEM((2, rows), jnp.int32),
            pltpu.VMEM((2, rows), BF16),
            pltpu.VMEM((rows, feat), BF16),
            pltpu.VMEM((rows, feat), BF16),
            DMA((6,)),
        ],
        2 * unit * rows,
    )
    halves = [list(range(half)), list(range(half, groups))]
    within = functools.partial(
        lax.all_to_all,
        axis_name="exp",
        split_axis=0,
        concat_axis=0,
        axis_index_groups=halves,
        tiled=True,
    )
    near = within(near_out)
    mirror_hops = [
        [(i, (i + shift) % mirrors) for i in range(mirrors)] for shift in range(1, mirrors)
    ]
    near_others = [lax.ppermute(near, "rep", hops) for hops in mirror_hops]
    (far_out,) = call(
        far_kernel, "far_slots", [disp_shape], partner, [IN_VMEM] * 4, [], 2 * unit * rows
    )
    beyond = within(far_out)
    far_others = [lax.ppermute(beyond, "rep", hops) for hops in mirror_hops]

    block = min(512, hidden)
    scratch = [pltpu.VMEM((slots, feat), F32), pltpu.VMEM((slots, 128), F32)]
    near_back, pick = call(
        functools.partial(near_back_kernel, cap, block),
        "near_backward",
        [shape((half, pad, feat), BF16), shape((groups * pad, rows), BF16)],
        [routes_t, near, up_v, down_v],
        [IN_VMEM] * 4,
        scratch,
        3 * unit * hidden,
        slots * hidden,
    )
    (back,) = call(
        functools.partial(far_back_kernel, cap, block),
        "far_backward",
        [shape((2, half, pad, feat), BF16)],
        [near_back, beyond, up_v, down_v],
        [IN_VMEM] * 4,
        scratch,
        3 * unit * hidden,
        slots * hidden,
    )
    back = lax.all_to_all(
        back.reshape(groups, pad, feat), "exp", split_axis=0, concat_axis=0, tiled=True
    )

    part = min(512, share)
    total = shape((share, feat), F32)
    both_rows = [pltpu.VMEM((2 * slots, feat), BF16)] * 2
    up_sum, down_sum = call(
        functools.partial(own_weights_kernel, part, share),
        "own_weights",
        [total, total],
        [near, beyond, up_v, down_v],
        [IN_VMEM] * 4,
        both_rows,
        8 * unit * share,
        2 * slots * share,
    )
    if mirrors == 1:
        grad_up, grad_down = up_sum.astype(BF16)[None], down_sum.astype(BF16)[None]
    else:
        others = [a for pair in zip(near_others, far_others) for a in pair]
        grad_up, grad_down = call(
            functools.partial(other_weights_kernel, part, share, mirrors),
            "other_weights",
            [shape((1, share, feat), BF16)] * 2,
            [*others, up_v, down_v, up_sum, down_sum],
            [IN_VMEM] * (len(others) + 4),
            both_rows,
            8 * unit * share * (mirrors - 1),
            2 * slots * share,
        )

    d_tokens, d_gates = call(
        functools.partial(combine_kernel, cap),
        "combine",
        [shape((rows, feat), BF16), shape((2, rows), BF16)],
        [routes_t, gates_t, pick, back],
        [IN_VMEM] * 4,
        [],
        2 * unit * rows,
    )
    return d_tokens, d_gates.T, grad_up, grad_down


def solution(mesh):
    by_both = P(("rep", "exp"), None)
    by_expert = P("exp", None, None)
    return jax.shard_map(
        local,
        mesh=mesh,
        in_specs=(by_both, by_both, by_both, by_both, by_expert, by_expert),
        out_specs=(by_both, by_both, P("exp", "rep", None), P("exp", "rep", None)),
        check_vma=False,
    )
```

```python
import functools

import jax
import jax.numpy as jnp
from jax import lax
from jax.experimental import pallas as pl
from jax.experimental.pallas import tpu as pltpu
from jax.sharding import PartitionSpec as P

F32 = jnp.float32
BF16 = jnp.bfloat16
SMALL, MEDIUM, LARGE = 8 << 20, 12 << 20, 24 << 20
AHEAD = 10**11
IN_HBM = pl.BlockSpec(memory_space=pltpu.HBM)
IN_VMEM = pl.BlockSpec(memory_space=pltpu.VMEM)
DMA = pltpu.SemaphoreType.DMA


def dot(left, right, left_dim, right_dim):
    return lax.dot_general(
        left, right, (((left_dim,), (right_dim,)), ((), ())), preferred_element_type=F32
    )


def silu_parts(preact):
    sigma = 0.5 * jnp.tanh(0.5 * preact) + 0.5
    active = preact * sigma
    return active, sigma + active * (1.0 - sigma)


def call(body, name, outs, args, in_specs, scratch, flops, transcendentals=0, limit=MEDIUM):
    moved = sum(a.size * a.dtype.itemsize for a in (*args, *outs))
    return pl.pallas_call(
        body,
        name=name,
        out_shape=outs,
        in_specs=in_specs,
        out_specs=[IN_VMEM] * len(outs),
        scratch_shapes=scratch,
        compiler_params=pltpu.CompilerParams(vmem_limit_bytes=limit),
        cost_estimate=pl.CostEstimate(
            flops=flops, bytes_accessed=moved, transcendentals=transcendentals
        ),
    )(*args)


def slots_of(routes, experts, first):
    rows = routes.shape[1]
    number = lax.broadcasted_iota(jnp.int32, (experts, rows), 0) + first
    hot = [number == routes[k : k + 1, :] for k in range(2)]
    as_num = [jnp.where(h, 1.0, 0.0).astype(F32) for h in hot]
    before = jnp.where(
        lax.broadcasted_iota(jnp.int32, (rows, rows), 0)
        < lax.broadcasted_iota(jnp.int32, (rows, rows), 1),
        1.0,
        0.0,
    ).astype(BF16)
    count = [dot(n.astype(BF16), before, 1, 0) for n in as_num]
    total = jnp.sum(as_num[0], axis=1, keepdims=True)
    place = [count[0], count[1] + total]
    slot = [
        jnp.sum(jnp.where(h, p, 0.0), axis=0, keepdims=True).astype(jnp.int32)
        for h, p in zip(hot, place)
    ]
    return hot, slot


def picks_of(routes, experts, first, pad):
    _, slot = slots_of(routes, experts, first)
    index = lax.broadcasted_iota(jnp.int32, (experts * pad, routes.shape[1]), 0)
    return [index == (routes[k : k + 1, :] - first) * pad + slot[k] for k in range(2)]


def unpack(packed_ref, rows):
    notes = packed_ref[2 * rows :, :].astype(F32)
    return notes[0:2, 0:rows].astype(jnp.int32), notes[2:4, 0:rows]


def slots_kernel(rows, packed_ref, out_ref):
    experts, both, feat = out_ref.shape
    pad = both // 2
    first = lax.axis_index("exp") // experts * experts
    routes, gates = unpack(packed_ref, rows)
    pick = picks_of(routes, experts, first, pad)
    plain = jnp.where(pick[0] | pick[1], 1.0, 0.0).astype(BF16)
    scaled = (
        jnp.where(pick[0], gates[0:1, :], 0.0) + jnp.where(pick[1], gates[1:2, :], 0.0)
    ).astype(BF16)
    tok = packed_ref[0:rows, :]
    cot = packed_ref[rows : 2 * rows, :]
    out_ref[:, 0:pad, :] = dot(plain, tok, 1, 0).astype(BF16).reshape(experts, pad, feat)
    out_ref[:, pad:, :] = dot(scaled, cot, 1, 0).astype(BF16).reshape(experts, pad, feat)


def split_rows(ref):
    experts, both, feat = ref.shape
    pad = both // 2
    return (
        ref[:, 0:pad, :].reshape(experts * pad, feat),
        ref[:, pad:, :].reshape(experts * pad, feat),
    )


def backward(cap, block, disp_ref, up_ref, down_ref, grad_acc, gate_acc, put, copies=()):
    origins, both, feat = disp_ref.shape
    pad = both // 2
    slots = origins * pad
    rows, grads = split_rows(disp_ref)
    for step in range(up_ref.shape[0] // block):
        part = pl.ds(step * block, block)
        if copies:
            copies[2 * step].wait()
        up = up_ref[part, :]
        active, slope = silu_parts(dot(rows, up, 1, 1))
        if copies:
            copies[2 * step + 1].wait()
        back = dot(grads, down_ref[part, :], 1, 1)
        hid_grad = (back * slope).astype(BF16)
        gate = active.astype(BF16).astype(F32) * back
        gate = sum(gate[:, i : i + 128] for i in range(0, block, 128))
        in_grad = dot(hid_grad, up, 1, 0)
        if step == 0:
            grad_acc[...] = in_grad
            gate_acc[...] = gate
        else:
            grad_acc[...] += in_grad
            gate_acc[...] += gate
    gate = jnp.sum(gate_acc[...], axis=1, keepdims=True)
    spot = lax.broadcasted_iota(jnp.int32, (slots, 128), 0) % pad
    lane = lax.broadcasted_iota(jnp.int32, (slots, 128), 1)
    gate = jnp.where(spot == lane, gate, 0.0).reshape(origins, pad, 128)
    gate = jnp.sum(gate, axis=1, keepdims=True)
    line = lax.broadcasted_iota(jnp.int32, (pad, 128), 0)
    for k in range(origins):
        here = slice(k * pad, (k + 1) * pad)
        first = jnp.where(line == cap, gate[k], grad_acc[here, 0:128])
        put(k, first.astype(BF16), grad_acc[here, 128:].astype(BF16))


def near_back_kernel(cap, block, rows, packed_ref, disp_ref, up_hbm, down_hbm, *refs):
    out_ref, pick_ref, up_ref, down_ref, grad_acc, gate_acc, sems = refs
    copies = []
    for step in range(up_ref.shape[0] // block):
        part = pl.ds(step * block, block)
        for i, (src, dst) in enumerate([(up_hbm, up_ref), (down_hbm, down_ref)]):
            sem = sems.at[2 * step + i]
            copies.append(pltpu.make_async_copy(src.at[0, part, :], dst.at[part, :], sem))
            copies[-1].start()

    def put(k, first, rest):
        out_ref[k, :, 0:128] = first
        out_ref[k, :, 128:] = rest

    backward(cap, block, disp_ref, up_ref, down_ref, grad_acc, gate_acc, put, copies)
    pad = out_ref.shape[1]
    pick = picks_of(unpack(packed_ref, rows)[0], pick_ref.shape[0] // pad, 0, pad)
    pick_ref[...] = jnp.where(pick[0] | pick[1], 1.0, 0.0).astype(BF16)


def far_back_kernel(cap, block, near_ref, disp_ref, up_ref, down_ref, *refs):
    out_hbm, out_ref, grad_acc, gate_acc, sems = refs
    half = lax.axis_index("exp") // near_ref.shape[0]
    near_copy = pltpu.make_async_copy(near_ref, out_hbm.at[half], sems.at[0])
    near_copy.start()

    def put(k, first, rest):
        out_ref[k, :, 0:128] = first
        out_ref[k, :, 128:] = rest

    backward(cap, block, disp_ref, up_ref, down_ref, grad_acc, gate_acc, put)
    far_copy = pltpu.make_async_copy(out_ref, out_hbm.at[1 - half], sems.at[1])
    far_copy.start()
    near_copy.wait()
    far_copy.wait()


def weight_parts(block, share, disp_refs, up_ref, down_ref, rows_ref, grads_ref, store):
    size = rows_ref.shape[0] // len(disp_refs)
    for i, ref in enumerate(disp_refs):
        here = slice(i * size, (i + 1) * size)
        rows_ref[here, :], grads_ref[here, :] = split_rows(ref)
    base = lax.axis_index("rep") * share
    for step in range(share // block):
        here = pl.ds(step * block, block)
        part = pl.ds(pl.multiple_of(base + step * block, block), block)
        active, slope = silu_parts(dot(up_ref[part, :], rows_ref[...], 1, 1))
        back = dot(down_ref[part, :], grads_ref[...], 1, 1)
        hid_grad = (back * slope).astype(BF16)
        up_part = dot(hid_grad, rows_ref[...], 1, 0)
        down_part = dot(active.astype(BF16), grads_ref[...], 1, 0)
        store(here, up_part, down_part)


def own_weights_kernel(block, share, near_ref, far_ref, up_ref, down_ref, *refs):
    up_acc, down_acc, rows_ref, grads_ref = refs

    def store(here, up_part, down_part):
        up_acc[here, :] = up_part
        down_acc[here, :] = down_part

    both = [near_ref, far_ref]
    weight_parts(block, share, both, up_ref, down_ref, rows_ref, grads_ref, store)


def other_weights_kernel(block, share, mirrors, *refs):
    pieces, refs = refs[:-8], refs[-8:]
    up_ref, down_ref, up_acc, down_acc, grad_up_ref, grad_down_ref, rows_ref, grads_ref = refs
    for mirror in range(mirrors - 1):

        def store(here, up_part, down_part):
            up_part += up_acc[here, :]
            down_part += down_acc[here, :]
            if mirror == mirrors - 2:
                grad_up_ref[0, here, :] = up_part.astype(BF16)
                grad_down_ref[0, here, :] = down_part.astype(BF16)
            else:
                up_acc[here, :] = up_part
                down_acc[here, :] = down_part

        both = pieces[2 * mirror : 2 * mirror + 2]
        weight_parts(block, share, both, up_ref, down_ref, rows_ref, grads_ref, store)


def combine_kernel(cap, routes_ref, gates_ref, pick_ref, back_ref, d_tok_ref, d_gate_ref):
    groups, pad, feat = back_ref.shape
    back = back_ref[...]
    d_tok_ref[...] = dot(pick_ref[...], back.reshape(groups * pad, feat), 0, 0).astype(BF16)
    routes = routes_ref[...]
    gates = gates_ref[...].astype(F32)
    hot, slot = slots_of(routes, groups, 0)
    lane = lax.broadcasted_iota(jnp.int32, (128, routes.shape[1]), 0)
    values = back[:, cap, 0:128]
    for k in range(2):
        spot = jnp.where(lane == slot[k], 1.0, 0.0).astype(BF16)
        found = jnp.where(hot[k], dot(values, spot, 1, 0), 0.0)
        found = jnp.sum(found, axis=0, keepdims=True)
        d_gate_ref[k : k + 1, :] = (found / gates[k : k + 1, :]).astype(BF16)


def local(tokens, gates, routes, cotangent, w_up, w_down):
    rows, feat = tokens.shape
    hidden = w_up.shape[1]
    groups = lax.axis_size("exp")
    mirrors = lax.axis_size("rep")
    cap = max(2, 3 * rows // groups)
    pad = (cap // 16 + 1) * 16
    half = groups // 2
    slots = half * pad
    share = hidden // mirrors
    routes_t, gates_t = routes.T, gates.T
    far = functools.partial(pltpu.with_memory_space_constraint, memory_space=pltpu.HBM)
    shape = jax.ShapeDtypeStruct
    unit = 2 * slots * feat
    disp_shape = shape((half, 2 * pad, feat), BF16)
    weight = shape((hidden, feat), BF16)

    across = [(i, (i + half) % groups) for i in range(groups)]
    notes = jnp.concatenate([routes_t.astype(BF16), gates_t], axis=0)
    notes = jnp.pad(notes, ((0, 12), (0, feat - rows)))
    packed = jnp.concatenate([tokens, cotangent, notes], axis=0)
    partner = lax.ppermute(packed, "exp", across)

    slots_call = functools.partial(call, functools.partial(slots_kernel, rows))
    (near_out,) = slots_call(
        "near_slots", [disp_shape], [packed], [IN_VMEM], [], 2 * unit * rows, 0, SMALL
    )
    halves = [list(range(half)), list(range(half, groups))]
    within = functools.partial(
        lax.all_to_all,
        axis_name="exp",
        split_axis=0,
        concat_axis=0,
        axis_index_groups=halves,
        tiled=True,
    )
    near = within(near_out)
    mirror_hops = [
        [(i, (i + shift) % mirrors) for i in range(mirrors)] for shift in range(1, mirrors)
    ]
    near_others = [lax.ppermute(near, "rep", hops) for hops in mirror_hops]
    (far_out,) = slots_call(
        "far_slots", [disp_shape], [partner], [IN_VMEM], [], AHEAD, 0, SMALL
    )
    beyond = within(far_out)
    far_others = [lax.ppermute(beyond, "rep", hops) for hops in mirror_hops]

    block = min(512, hidden)
    scratch = [pltpu.VMEM((slots, feat), F32), pltpu.VMEM((slots, 128), F32)]
    near_back, pick, up_v, down_v = call(
        functools.partial(near_back_kernel, cap, block, rows),
        "near_backward",
        [shape((half, pad, feat), BF16), shape((groups * pad, rows), BF16), weight, weight],
        [packed, near, far(w_up), far(w_down)],
        [IN_VMEM] * 2 + [IN_HBM] * 2,
        scratch + [DMA((2 * hidden // block,))],
        3 * unit * hidden,
        slots * hidden,
    )
    back = pl.pallas_call(
        functools.partial(far_back_kernel, cap, block),
        name="far_backward",
        out_shape=pltpu.HBM((2, half, pad, feat), BF16),
        in_specs=[IN_VMEM] * 4,
        out_specs=IN_HBM,
        scratch_shapes=[pltpu.VMEM((half, pad, feat), BF16)] + scratch + [DMA((2,))],
        compiler_params=pltpu.CompilerParams(vmem_limit_bytes=MEDIUM),
        cost_estimate=pl.CostEstimate(
            flops=3 * unit * hidden,
            bytes_accessed=4 * hidden * feat,
            transcendentals=slots * hidden,
        ),
    )(near_back, beyond, up_v, down_v)
    back = lax.all_to_all(
        back.reshape(groups, pad, feat), "exp", split_axis=0, concat_axis=0, tiled=True
    )

    part = min(512, share)
    total = shape((share, feat), F32)
    both_rows = [pltpu.VMEM((2 * slots, feat), BF16)] * 2
    up_sum, down_sum = call(
        functools.partial(own_weights_kernel, part, share),
        "own_weights",
        [total, total],
        [near, beyond, up_v, down_v],
        [IN_VMEM] * 4,
        both_rows,
        8 * unit * share,
        2 * slots * share,
        LARGE,
    )
    if mirrors == 1:
        grad_up, grad_down = up_sum.astype(BF16)[None], down_sum.astype(BF16)[None]
    else:
        others = [a for pair in zip(near_others, far_others) for a in pair]
        grad_up, grad_down = call(
            functools.partial(other_weights_kernel, part, share, mirrors),
            "other_weights",
            [shape((1, share, feat), BF16)] * 2,
            [*others, up_v, down_v, up_sum, down_sum],
            [IN_VMEM] * (len(others) + 4),
            both_rows,
            AHEAD,
            2 * slots * share,
            LARGE,
        )

    d_tokens, d_gates = call(
        functools.partial(combine_kernel, cap),
        "combine",
        [shape((rows, feat), BF16), shape((2, rows), BF16)],
        [routes_t, gates_t, pick, back],
        [IN_VMEM] * 4,
        [],
        2 * unit * rows,
    )
    return d_tokens, d_gates.T, grad_up, grad_down


def solution(mesh):
    by_both = P(("rep", "exp"), None)
    by_expert = P("exp", None, None)
    return jax.shard_map(
        local,
        mesh=mesh,
        in_specs=(by_both, by_both, by_both, by_both, by_expert, by_expert),
        out_specs=(by_both, by_both, P("exp", "rep", None), P("exp", "rep", None)),
        check_vma=False,
    )
```

```python
import functools

import jax
import jax.numpy as jnp
from jax import lax
from jax.experimental import pallas as pl
from jax.experimental.pallas import tpu as pltpu
from jax.sharding import PartitionSpec as P

F32 = jnp.float32
BF16 = jnp.bfloat16
SMALL, MEDIUM, LARGE = 8 << 20, 12 << 20, 24 << 20
AHEAD = 10**11
IN_HBM = pl.BlockSpec(memory_space=pltpu.HBM)
IN_VMEM = pl.BlockSpec(memory_space=pltpu.VMEM)
DMA = pltpu.SemaphoreType.DMA


def dot(left, right, left_dim, right_dim):
    return lax.dot_general(
        left, right, (((left_dim,), (right_dim,)), ((), ())), preferred_element_type=F32
    )


def silu_parts(preact):
    sigma = 0.5 * jnp.tanh(0.5 * preact) + 0.5
    active = preact * sigma
    return active, sigma + active * (1.0 - sigma)


def call(body, name, outs, args, in_specs, scratch, flops, transcendentals=0, limit=MEDIUM):
    moved = sum(a.size * a.dtype.itemsize for a in (*args, *outs))
    return pl.pallas_call(
        body,
        name=name,
        out_shape=outs,
        in_specs=in_specs,
        out_specs=[IN_VMEM] * len(outs),
        scratch_shapes=scratch,
        compiler_params=pltpu.CompilerParams(vmem_limit_bytes=limit),
        cost_estimate=pl.CostEstimate(
            flops=flops, bytes_accessed=moved, transcendentals=transcendentals
        ),
    )(*args)


def slots_of(routes, experts, first):
    rows = routes.shape[1]
    number = lax.broadcasted_iota(jnp.int32, (experts, rows), 0) + first
    hot = [number == routes[k : k + 1, :] for k in range(2)]
    as_num = [jnp.where(h, 1.0, 0.0).astype(F32) for h in hot]
    before = jnp.where(
        lax.broadcasted_iota(jnp.int32, (rows, rows), 0)
        < lax.broadcasted_iota(jnp.int32, (rows, rows), 1),
        1.0,
        0.0,
    ).astype(BF16)
    count = [dot(n.astype(BF16), before, 1, 0) for n in as_num]
    total = jnp.sum(as_num[0], axis=1, keepdims=True)
    place = [count[0], count[1] + total]
    slot = [
        jnp.sum(jnp.where(h, p, 0.0), axis=0, keepdims=True).astype(jnp.int32)
        for h, p in zip(hot, place)
    ]
    return hot, slot


def picks_of(routes, experts, first, pad):
    _, slot = slots_of(routes, experts, first)
    index = lax.broadcasted_iota(jnp.int32, (experts * pad, routes.shape[1]), 0)
    return [index == (routes[k : k + 1, :] - first) * pad + slot[k] for k in range(2)]


def unpack(packed_ref, rows):
    notes = packed_ref[2 * rows :, :].astype(F32)
    return notes[0:2, 0:rows].astype(jnp.int32), notes[2:4, 0:rows]


def pack_kernel(routes_hbm, gates_hbm, tok_hbm, cot_hbm, out_ref, routes_ref, gates_ref, sems):
    rows, feat = tok_hbm.shape
    pairs = [
        (routes_hbm, routes_ref),
        (gates_hbm, gates_ref),
        (tok_hbm, out_ref.at[0:rows, :]),
        (cot_hbm, out_ref.at[rows : 2 * rows, :]),
    ]
    copies = [
        pltpu.make_async_copy(src, dst, sems.at[i]) for i, (src, dst) in enumerate(pairs)
    ]
    for copy in copies:
        copy.start()
    copies[0].wait()
    copies[1].wait()
    notes = [routes_ref[...].astype(F32), gates_ref[...].astype(F32), jnp.zeros((12, rows), F32)]
    out_ref[2 * rows :, 0:rows] = jnp.concatenate(notes, axis=0).astype(BF16)
    out_ref[2 * rows :, rows:] = jnp.zeros((16, feat - rows), BF16)
    copies[2].wait()
    copies[3].wait()


def slots_kernel(rows, packed_ref, out_ref):
    experts, both, feat = out_ref.shape
    pad = both // 2
    first = lax.axis_index("exp") // experts * experts
    routes, gates = unpack(packed_ref, rows)
    pick = picks_of(routes, experts, first, pad)
    plain = jnp.where(pick[0] | pick[1], 1.0, 0.0).astype(BF16)
    scaled = (
        jnp.where(pick[0], gates[0:1, :], 0.0) + jnp.where(pick[1], gates[1:2, :], 0.0)
    ).astype(BF16)
    tok = packed_ref[0:rows, :]
    cot = packed_ref[rows : 2 * rows, :]
    out_ref[:, 0:pad, :] = dot(plain, tok, 1, 0).astype(BF16).reshape(experts, pad, feat)
    out_ref[:, pad:, :] = dot(scaled, cot, 1, 0).astype(BF16).reshape(experts, pad, feat)


def split_rows(ref):
    experts, both, feat = ref.shape
    pad = both // 2
    return (
        ref[:, 0:pad, :].reshape(experts * pad, feat),
        ref[:, pad:, :].reshape(experts * pad, feat),
    )


def backward(cap, block, disp_ref, up_ref, down_ref, grad_acc, gate_acc, put, copies=()):
    origins, both, feat = disp_ref.shape
    pad = both // 2
    slots = origins * pad
    rows, grads = split_rows(disp_ref)
    for step in range(up_ref.shape[0] // block):
        part = pl.ds(step * block, block)
        if copies:
            copies[2 * step].wait()
        up = up_ref[part, :]
        active, slope = silu_parts(dot(rows, up, 1, 1))
        if copies:
            copies[2 * step + 1].wait()
        back = dot(grads, down_ref[part, :], 1, 1)
        hid_grad = (back * slope).astype(BF16)
        gate = active.astype(BF16).astype(F32) * back
        gate = sum(gate[:, i : i + 128] for i in range(0, block, 128))
        in_grad = dot(hid_grad, up, 1, 0)
        if step == 0:
            grad_acc[...] = in_grad
            gate_acc[...] = gate
        else:
            grad_acc[...] += in_grad
            gate_acc[...] += gate
    gate = jnp.sum(gate_acc[...], axis=1, keepdims=True)
    spot = lax.broadcasted_iota(jnp.int32, (slots, 128), 0) % pad
    lane = lax.broadcasted_iota(jnp.int32, (slots, 128), 1)
    gate = jnp.where(spot == lane, gate, 0.0).reshape(origins, pad, 128)
    gate = jnp.sum(gate, axis=1, keepdims=True)
    line = lax.broadcasted_iota(jnp.int32, (pad, 128), 0)
    for k in range(origins):
        here = slice(k * pad, (k + 1) * pad)
        first = jnp.where(line == cap, gate[k], grad_acc[here, 0:128])
        put(k, first.astype(BF16), grad_acc[here, 128:].astype(BF16))


def near_back_kernel(cap, block, rows, packed_ref, disp_ref, up_hbm, down_hbm, *refs):
    out_ref, pick_ref, up_ref, down_ref, grad_acc, gate_acc, sems = refs
    copies = []
    for step in range(up_ref.shape[0] // block):
        part = pl.ds(step * block, block)
        for i, (src, dst) in enumerate([(up_hbm, up_ref), (down_hbm, down_ref)]):
            sem = sems.at[2 * step + i]
            copies.append(pltpu.make_async_copy(src.at[0, part, :], dst.at[part, :], sem))
            copies[-1].start()

    def put(k, first, rest):
        out_ref[k, :, 0:128] = first
        out_ref[k, :, 128:] = rest

    backward(cap, block, disp_ref, up_ref, down_ref, grad_acc, gate_acc, put, copies)
    pad = out_ref.shape[1]
    pick = picks_of(unpack(packed_ref, rows)[0], pick_ref.shape[0] // pad, 0, pad)
    pick_ref[...] = jnp.where(pick[0] | pick[1], 1.0, 0.0).astype(BF16)


def far_back_kernel(cap, block, near_ref, disp_ref, up_ref, down_ref, *refs):
    out_hbm, out_ref, grad_acc, gate_acc, sems = refs
    half = lax.axis_index("exp") // near_ref.shape[0]
    near_copy = pltpu.make_async_copy(near_ref, out_hbm.at[half], sems.at[0])
    near_copy.start()

    def put(k, first, rest):
        out_ref[k, :, 0:128] = first
        out_ref[k, :, 128:] = rest

    backward(cap, block, disp_ref, up_ref, down_ref, grad_acc, gate_acc, put)
    far_copy = pltpu.make_async_copy(out_ref, out_hbm.at[1 - half], sems.at[1])
    far_copy.start()
    near_copy.wait()
    far_copy.wait()


def weight_parts(block, share, disp_refs, up_ref, down_ref, rows_ref, grads_ref, store):
    size = rows_ref.shape[0] // len(disp_refs)
    for i, ref in enumerate(disp_refs):
        here = slice(i * size, (i + 1) * size)
        rows_ref[here, :], grads_ref[here, :] = split_rows(ref)
    base = lax.axis_index("rep") * share
    for step in range(share // block):
        here = pl.ds(step * block, block)
        part = pl.ds(pl.multiple_of(base + step * block, block), block)
        active, slope = silu_parts(dot(up_ref[part, :], rows_ref[...], 1, 1))
        back = dot(down_ref[part, :], grads_ref[...], 1, 1)
        hid_grad = (back * slope).astype(BF16)
        up_part = dot(hid_grad, rows_ref[...], 1, 0)
        down_part = dot(active.astype(BF16), grads_ref[...], 1, 0)
        store(here, up_part, down_part)


def own_weights_kernel(block, share, near_ref, far_ref, up_ref, down_ref, *refs):
    up_acc, down_acc, rows_ref, grads_ref = refs

    def store(here, up_part, down_part):
        up_acc[here, :] = up_part
        down_acc[here, :] = down_part

    both = [near_ref, far_ref]
    weight_parts(block, share, both, up_ref, down_ref, rows_ref, grads_ref, store)


def other_weights_kernel(block, share, mirrors, *refs):
    pieces, refs = refs[:-8], refs[-8:]
    up_ref, down_ref, up_acc, down_acc, grad_up_ref, grad_down_ref, rows_ref, grads_ref = refs
    for mirror in range(mirrors - 1):

        def store(here, up_part, down_part):
            up_part += up_acc[here, :]
            down_part += down_acc[here, :]
            if mirror == mirrors - 2:
                grad_up_ref[0, here, :] = up_part.astype(BF16)
                grad_down_ref[0, here, :] = down_part.astype(BF16)
            else:
                up_acc[here, :] = up_part
                down_acc[here, :] = down_part

        both = pieces[2 * mirror : 2 * mirror + 2]
        weight_parts(block, share, both, up_ref, down_ref, rows_ref, grads_ref, store)


def combine_kernel(cap, routes_ref, gates_ref, pick_ref, back_ref, d_tok_ref, d_gate_ref):
    groups, pad, feat = back_ref.shape
    back = back_ref[...]
    d_tok_ref[...] = dot(pick_ref[...], back.reshape(groups * pad, feat), 0, 0).astype(BF16)
    routes = routes_ref[...]
    gates = gates_ref[...].astype(F32)
    hot, slot = slots_of(routes, groups, 0)
    lane = lax.broadcasted_iota(jnp.int32, (128, routes.shape[1]), 0)
    values = back[:, cap, 0:128]
    for k in range(2):
        spot = jnp.where(lane == slot[k], 1.0, 0.0).astype(BF16)
        found = jnp.where(hot[k], dot(values, spot, 1, 0), 0.0)
        found = jnp.sum(found, axis=0, keepdims=True)
        d_gate_ref[k : k + 1, :] = (found / gates[k : k + 1, :]).astype(BF16)


def local(tokens, gates, routes, cotangent, w_up, w_down):
    rows, feat = tokens.shape
    hidden = w_up.shape[1]
    groups = lax.axis_size("exp")
    mirrors = lax.axis_size("rep")
    cap = max(2, 3 * rows // groups)
    pad = (cap // 16 + 1) * 16
    half = groups // 2
    slots = half * pad
    share = hidden // mirrors
    routes_t, gates_t = routes.T, gates.T
    far = functools.partial(pltpu.with_memory_space_constraint, memory_space=pltpu.HBM)
    shape = jax.ShapeDtypeStruct
    unit = 2 * slots * feat
    disp_shape = shape((half, 2 * pad, feat), BF16)
    weight = shape((hidden, feat), BF16)

    across = [(i, (i + half) % groups) for i in range(groups)]
    (packed,) = call(
        pack_kernel,
        "pack",
        [shape((2 * rows + 16, feat), BF16)],
        [far(a) for a in (routes_t, gates_t, tokens, cotangent)],
        [IN_HBM] * 4,
        [pltpu.VMEM((2, rows), jnp.int32), pltpu.VMEM((2, rows), BF16), DMA((4,))],
        0,
        0,
        SMALL,
    )
    partner = lax.ppermute(packed, "exp", across)

    slots_call = functools.partial(call, functools.partial(slots_kernel, rows))
    (near_out,) = slots_call(
        "near_slots", [disp_shape], [packed], [IN_VMEM], [], 2 * unit * rows, 0, SMALL
    )
    halves = [list(range(half)), list(range(half, groups))]
    within = functools.partial(
        lax.all_to_all,
        axis_name="exp",
        split_axis=0,
        concat_axis=0,
        axis_index_groups=halves,
        tiled=True,
    )
    near = within(near_out)
    mirror_hops = [
        [(i, (i + shift) % mirrors) for i in range(mirrors)] for shift in range(1, mirrors)
    ]
    near_others = [lax.ppermute(near, "rep", hops) for hops in mirror_hops]
    (far_out,) = slots_call(
        "far_slots", [disp_shape], [partner], [IN_VMEM], [], AHEAD, 0, SMALL
    )
    beyond = within(far_out)
    far_others = [lax.ppermute(beyond, "rep", hops) for hops in mirror_hops]

    block = min(512, hidden)
    scratch = [pltpu.VMEM((slots, feat), F32), pltpu.VMEM((slots, 128), F32)]
    near_back, pick, up_v, down_v = call(
        functools.partial(near_back_kernel, cap, block, rows),
        "near_backward",
        [shape((half, pad, feat), BF16), shape((groups * pad, rows), BF16), weight, weight],
        [packed, near, far(w_up), far(w_down)],
        [IN_VMEM] * 2 + [IN_HBM] * 2,
        scratch + [DMA((2 * hidden // block,))],
        3 * unit * hidden,
        slots * hidden,
    )
    back = pl.pallas_call(
        functools.partial(far_back_kernel, cap, block),
        name="far_backward",
        out_shape=pltpu.HBM((2, half, pad, feat), BF16),
        in_specs=[IN_VMEM] * 4,
        out_specs=IN_HBM,
        scratch_shapes=[pltpu.VMEM((half, pad, feat), BF16)] + scratch + [DMA((2,))],
        compiler_params=pltpu.CompilerParams(vmem_limit_bytes=MEDIUM),
        cost_estimate=pl.CostEstimate(
            flops=AHEAD,
            bytes_accessed=4 * hidden * feat,
            transcendentals=slots * hidden,
        ),
    )(near_back, beyond, up_v, down_v)
    back = lax.all_to_all(
        back.reshape(groups, pad, feat), "exp", split_axis=0, concat_axis=0, tiled=True
    )

    part = min(512, share)
    total = shape((share, feat), F32)
    both_rows = [pltpu.VMEM((2 * slots, feat), BF16)] * 2
    up_sum, down_sum = call(
        functools.partial(own_weights_kernel, part, share),
        "own_weights",
        [total, total],
        [near, beyond, up_v, down_v],
        [IN_VMEM] * 4,
        both_rows,
        8 * unit * share,
        2 * slots * share,
        LARGE,
    )
    if mirrors == 1:
        grad_up, grad_down = up_sum.astype(BF16)[None], down_sum.astype(BF16)[None]
    else:
        others = [a for pair in zip(near_others, far_others) for a in pair]
        grad_up, grad_down = call(
            functools.partial(other_weights_kernel, part, share, mirrors),
            "other_weights",
            [shape((1, share, feat), BF16)] * 2,
            [*others, up_v, down_v, up_sum, down_sum],
            [IN_VMEM] * (len(others) + 4),
            both_rows,
            AHEAD,
            2 * slots * share,
            LARGE,
        )

    d_tokens, d_gates = call(
        functools.partial(combine_kernel, cap),
        "combine",
        [shape((rows, feat), BF16), shape((2, rows), BF16)],
        [routes_t, gates_t, pick, back],
        [IN_VMEM] * 4,
        [],
        2 * unit * rows,
    )
    return d_tokens, d_gates.T, grad_up, grad_down


def solution(mesh):
    by_both = P(("rep", "exp"), None)
    by_expert = P("exp", None, None)
    return jax.shard_map(
        local,
        mesh=mesh,
        in_specs=(by_both, by_both, by_both, by_both, by_expert, by_expert),
        out_specs=(by_both, by_both, P("exp", "rep", None), P("exp", "rep", None)),
        check_vma=False,
    )
```

```python
import functools
import math

import jax
import jax.numpy as jnp
from jax import lax
from jax.experimental import pallas as pl
from jax.experimental.pallas import tpu as pltpu
from jax.sharding import PartitionSpec as P

F32 = jnp.float32
BF16 = jnp.bfloat16
SMALL, MEDIUM, LARGE = 8 << 20, 12 << 20, 24 << 20
AHEAD = 10**11
IN_HBM = pl.BlockSpec(memory_space=pltpu.HBM)
IN_VMEM = pl.BlockSpec(memory_space=pltpu.VMEM)
DMA = pltpu.SemaphoreType.DMA


def dot(left, right, left_dim, right_dim):
    return lax.dot_general(
        left, right, (((left_dim,), (right_dim,)), ((), ())), preferred_element_type=F32
    )


def silu_parts(preact):
    sigma = 0.5 * jnp.tanh(0.5 * preact) + 0.5
    active = preact * sigma
    return active, sigma + active * (1.0 - sigma)


def call(body, name, outs, args, in_specs, scratch, flops, transcendentals=0, limit=MEDIUM):
    moved = sum(math.prod(a.shape) * a.dtype.itemsize for a in (*args, *outs))
    return pl.pallas_call(
        body,
        name=name,
        out_shape=outs,
        in_specs=in_specs,
        out_specs=[IN_VMEM] * len(outs),
        scratch_shapes=scratch,
        compiler_params=pltpu.CompilerParams(vmem_limit_bytes=limit),
        cost_estimate=pl.CostEstimate(
            flops=flops, bytes_accessed=moved, transcendentals=transcendentals
        ),
    )(*args)


def slots_of(routes, experts, first):
    rows = routes.shape[1]
    number = lax.broadcasted_iota(jnp.int32, (experts, rows), 0) + first
    hot = [number == routes[k : k + 1, :] for k in range(2)]
    as_num = [jnp.where(h, 1.0, 0.0).astype(F32) for h in hot]
    before = jnp.where(
        lax.broadcasted_iota(jnp.int32, (rows, rows), 0)
        < lax.broadcasted_iota(jnp.int32, (rows, rows), 1),
        1.0,
        0.0,
    ).astype(BF16)
    count = [dot(n.astype(BF16), before, 1, 0) for n in as_num]
    total = jnp.sum(as_num[0], axis=1, keepdims=True)
    place = [count[0], count[1] + total]
    slot = [
        jnp.sum(jnp.where(h, p, 0.0), axis=0, keepdims=True).astype(jnp.int32)
        for h, p in zip(hot, place)
    ]
    return hot, slot


def picks_of(routes, experts, first, pad):
    _, slot = slots_of(routes, experts, first)
    index = lax.broadcasted_iota(jnp.int32, (experts * pad, routes.shape[1]), 0)
    return [index == (routes[k : k + 1, :] - first) * pad + slot[k] for k in range(2)]


def unpack(packed_ref, rows):
    notes = packed_ref[2 * rows :, :].astype(F32)
    return notes[0:2, 0:rows].astype(jnp.int32), notes[2:4, 0:rows]


def pack_kernel(routes_hbm, gates_hbm, tok_hbm, cot_hbm, out_ref, routes_ref, gates_ref, sems):
    rows, feat = tok_hbm.shape
    pairs = [
        (routes_hbm, routes_ref),
        (gates_hbm, gates_ref),
        (tok_hbm, out_ref.at[0:rows, :]),
        (cot_hbm, out_ref.at[rows : 2 * rows, :]),
    ]
    copies = [
        pltpu.make_async_copy(src, dst, sems.at[i]) for i, (src, dst) in enumerate(pairs)
    ]
    for copy in copies:
        copy.start()
    copies[0].wait()
    copies[1].wait()
    notes = [routes_ref[...].astype(F32), gates_ref[...].astype(F32), jnp.zeros((12, rows), F32)]
    out_ref[2 * rows :, 0:rows] = jnp.concatenate(notes, axis=0).astype(BF16)
    out_ref[2 * rows :, rows:] = jnp.zeros((16, feat - rows), BF16)
    copies[2].wait()
    copies[3].wait()


def slots_kernel(rows, packed_ref, out_ref):
    experts, both, feat = out_ref.shape
    pad = both // 2
    first = lax.axis_index("exp") // experts * experts
    routes, gates = unpack(packed_ref, rows)
    pick = picks_of(routes, experts, first, pad)
    plain = jnp.where(pick[0] | pick[1], 1.0, 0.0).astype(BF16)
    scaled = (
        jnp.where(pick[0], gates[0:1, :], 0.0) + jnp.where(pick[1], gates[1:2, :], 0.0)
    ).astype(BF16)
    tok = packed_ref[0:rows, :]
    cot = packed_ref[rows : 2 * rows, :]
    out_ref[:, 0:pad, :] = dot(plain, tok, 1, 0).astype(BF16).reshape(experts, pad, feat)
    out_ref[:, pad:, :] = dot(scaled, cot, 1, 0).astype(BF16).reshape(experts, pad, feat)


def fetch_kernel(up_hbm, down_hbm, up_ref, down_ref, sems):
    copies = []
    for i, (src, dst) in enumerate([(up_hbm, up_ref), (down_hbm, down_ref)]):
        copies.append(pltpu.make_async_copy(src.at[0], dst, sems.at[i]))
        copies[i].start()
    for copy in copies:
        copy.wait()


def far_slots_kernel(rows, packed_ref, _, out_ref):
    slots_kernel(rows, packed_ref, out_ref)


def split_rows(ref):
    experts, both, feat = ref.shape
    pad = both // 2
    return (
        ref[:, 0:pad, :].reshape(experts * pad, feat),
        ref[:, pad:, :].reshape(experts * pad, feat),
    )


def backward(cap, block, disp_ref, up_ref, down_ref, grad_acc, gate_acc, put):
    origins, both, feat = disp_ref.shape
    pad = both // 2
    slots = origins * pad
    rows, grads = split_rows(disp_ref)
    for step in range(up_ref.shape[0] // block):
        part = pl.ds(step * block, block)
        up = up_ref[part, :]
        active, slope = silu_parts(dot(rows, up, 1, 1))
        back = dot(grads, down_ref[part, :], 1, 1)
        hid_grad = (back * slope).astype(BF16)
        gate = active.astype(BF16).astype(F32) * back
        gate = sum(gate[:, i : i + 128] for i in range(0, block, 128))
        in_grad = dot(hid_grad, up, 1, 0)
        if step == 0:
            grad_acc[...] = in_grad
            gate_acc[...] = gate
        else:
            grad_acc[...] += in_grad
            gate_acc[...] += gate
    gate = jnp.sum(gate_acc[...], axis=1, keepdims=True)
    spot = lax.broadcasted_iota(jnp.int32, (slots, 128), 0) % pad
    lane = lax.broadcasted_iota(jnp.int32, (slots, 128), 1)
    gate = jnp.where(spot == lane, gate, 0.0).reshape(origins, pad, 128)
    gate = jnp.sum(gate, axis=1, keepdims=True)
    line = lax.broadcasted_iota(jnp.int32, (pad, 128), 0)
    for k in range(origins):
        here = slice(k * pad, (k + 1) * pad)
        first = jnp.where(line == cap, gate[k], grad_acc[here, 0:128])
        put(k, first.astype(BF16), grad_acc[here, 128:].astype(BF16))


def near_back_kernel(cap, block, rows, packed_ref, disp_ref, up_ref, down_ref, *refs):
    out_ref, pick_ref, grad_acc, gate_acc = refs

    def put(k, first, rest):
        out_ref[k, :, 0:128] = first
        out_ref[k, :, 128:] = rest

    backward(cap, block, disp_ref, up_ref, down_ref, grad_acc, gate_acc, put)
    pad = out_ref.shape[1]
    pick = picks_of(unpack(packed_ref, rows)[0], pick_ref.shape[0] // pad, 0, pad)
    pick_ref[...] = jnp.where(pick[0] | pick[1], 1.0, 0.0).astype(BF16)


def far_back_kernel(cap, block, near_ref, disp_ref, up_ref, down_ref, *refs):
    out_hbm, out_ref, grad_acc, gate_acc, sems = refs
    half = lax.axis_index("exp") // near_ref.shape[0]
    near_copy = pltpu.make_async_copy(near_ref, out_hbm.at[half], sems.at[0])
    near_copy.start()

    def put(k, first, rest):
        out_ref[k, :, 0:128] = first
        out_ref[k, :, 128:] = rest

    backward(cap, block, disp_ref, up_ref, down_ref, grad_acc, gate_acc, put)
    far_copy = pltpu.make_async_copy(out_ref, out_hbm.at[1 - half], sems.at[1])
    far_copy.start()
    near_copy.wait()
    far_copy.wait()


def weight_parts(block, share, disp_refs, up_ref, down_ref, rows_ref, grads_ref, store):
    size = rows_ref.shape[0] // len(disp_refs)
    for i, ref in enumerate(disp_refs):
        here = slice(i * size, (i + 1) * size)
        rows_ref[here, :], grads_ref[here, :] = split_rows(ref)
    base = lax.axis_index("rep") * share
    for step in range(share // block):
        here = pl.ds(step * block, block)
        part = pl.ds(pl.multiple_of(base + step * block, block), block)
        active, slope = silu_parts(dot(up_ref[part, :], rows_ref[...], 1, 1))
        back = dot(down_ref[part, :], grads_ref[...], 1, 1)
        hid_grad = (back * slope).astype(BF16)
        up_part = dot(hid_grad, rows_ref[...], 1, 0)
        down_part = dot(active.astype(BF16), grads_ref[...], 1, 0)
        store(here, up_part, down_part)


def own_weights_kernel(block, share, near_ref, far_ref, up_ref, down_ref, *refs):
    up_acc, down_acc, rows_ref, grads_ref = refs

    def store(here, up_part, down_part):
        up_acc[here, :] = up_part
        down_acc[here, :] = down_part

    both = [near_ref, far_ref]
    weight_parts(block, share, both, up_ref, down_ref, rows_ref, grads_ref, store)


def other_weights_kernel(block, share, mirrors, *refs):
    pieces, refs = refs[:-8], refs[-8:]
    up_ref, down_ref, up_acc, down_acc, grad_up_ref, grad_down_ref, rows_ref, grads_ref = refs
    for mirror in range(mirrors - 1):

        def store(here, up_part, down_part):
            up_part += up_acc[here, :]
            down_part += down_acc[here, :]
            if mirror == mirrors - 2:
                grad_up_ref[0, here, :] = up_part.astype(BF16)
                grad_down_ref[0, here, :] = down_part.astype(BF16)
            else:
                up_acc[here, :] = up_part
                down_acc[here, :] = down_part

        both = pieces[2 * mirror : 2 * mirror + 2]
        weight_parts(block, share, both, up_ref, down_ref, rows_ref, grads_ref, store)


def combine_kernel(cap, routes_ref, gates_ref, pick_ref, back_ref, d_tok_ref, d_gate_ref):
    groups, pad, feat = back_ref.shape
    back = back_ref[...]
    d_tok_ref[...] = dot(pick_ref[...], back.reshape(groups * pad, feat), 0, 0).astype(BF16)
    routes = routes_ref[...]
    gates = gates_ref[...].astype(F32)
    hot, slot = slots_of(routes, groups, 0)
    lane = lax.broadcasted_iota(jnp.int32, (128, routes.shape[1]), 0)
    values = back[:, cap, 0:128]
    for k in range(2):
        spot = jnp.where(lane == slot[k], 1.0, 0.0).astype(BF16)
        found = jnp.where(hot[k], dot(values, spot, 1, 0), 0.0)
        found = jnp.sum(found, axis=0, keepdims=True)
        d_gate_ref[k : k + 1, :] = (found / gates[k : k + 1, :]).astype(BF16)


def local(tokens, gates, routes, cotangent, w_up, w_down):
    rows, feat = tokens.shape
    hidden = w_up.shape[1]
    groups = lax.axis_size("exp")
    mirrors = lax.axis_size("rep")
    cap = max(2, 3 * rows // groups)
    pad = (cap // 16 + 1) * 16
    half = groups // 2
    slots = half * pad
    share = hidden // mirrors
    routes_t, gates_t = routes.T, gates.T
    far = functools.partial(pltpu.with_memory_space_constraint, memory_space=pltpu.HBM)
    shape = jax.ShapeDtypeStruct
    unit = 2 * slots * feat
    disp_shape = shape((half, 2 * pad, feat), BF16)
    weight = pltpu.VMEM((hidden, feat), BF16)
    close = functools.partial(pltpu.with_memory_space_constraint, memory_space=pltpu.VMEM)

    across = [(i, (i + half) % groups) for i in range(groups)]
    (packed,) = call(
        pack_kernel,
        "pack",
        [shape((2 * rows + 16, feat), BF16)],
        [far(a) for a in (routes_t, gates_t, tokens, cotangent)],
        [IN_HBM] * 4,
        [pltpu.VMEM((2, rows), jnp.int32), pltpu.VMEM((2, rows), BF16), DMA((4,))],
        0,
        0,
        SMALL,
    )
    partner = lax.ppermute(packed, "exp", across)

    (near_out,) = call(
        functools.partial(slots_kernel, rows),
        "near_slots",
        [disp_shape],
        [packed],
        [IN_VMEM],
        [],
        2 * unit * rows,
        0,
        SMALL,
    )
    up_v, down_v = call(
        fetch_kernel,
        "fetch_weights",
        [weight, weight],
        [far(w_up), far(w_down)],
        [IN_HBM, IN_HBM],
        [DMA((2,))],
        0,
        0,
        SMALL,
    )
    up_v, down_v = close(up_v), close(down_v)
    halves = [list(range(half)), list(range(half, groups))]
    within = functools.partial(
        lax.all_to_all,
        axis_name="exp",
        split_axis=0,
        concat_axis=0,
        axis_index_groups=halves,
        tiled=True,
    )
    near = within(near_out)
    mirror_hops = [
        [(i, (i + shift) % mirrors) for i in range(mirrors)] for shift in range(1, mirrors)
    ]
    near_others = [lax.ppermute(near, "rep", hops) for hops in mirror_hops]
    (far_out,) = call(
        functools.partial(far_slots_kernel, rows),
        "far_slots",
        [disp_shape],
        [partner, up_v],
        [IN_VMEM] * 2,
        [],
        AHEAD,
        0,
        SMALL,
    )
    beyond = within(far_out)
    far_others = [lax.ppermute(beyond, "rep", hops) for hops in mirror_hops]

    block = min(512, hidden)
    scratch = [pltpu.VMEM((slots, feat), F32), pltpu.VMEM((slots, 128), F32)]
    near_back, pick = call(
        functools.partial(near_back_kernel, cap, block, rows),
        "near_backward",
        [shape((half, pad, feat), BF16), shape((groups * pad, rows), BF16)],
        [packed, near, up_v, down_v],
        [IN_VMEM] * 4,
        scratch,
        3 * unit * hidden,
        slots * hidden,
    )
    back = pl.pallas_call(
        functools.partial(far_back_kernel, cap, block),
        name="far_backward",
        out_shape=pltpu.HBM((2, half, pad, feat), BF16),
        in_specs=[IN_VMEM] * 4,
        out_specs=IN_HBM,
        scratch_shapes=[pltpu.VMEM((half, pad, feat), BF16)] + scratch + [DMA((2,))],
        compiler_params=pltpu.CompilerParams(vmem_limit_bytes=MEDIUM),
        cost_estimate=pl.CostEstimate(
            flops=AHEAD,
            bytes_accessed=4 * hidden * feat,
            transcendentals=slots * hidden,
        ),
    )(near_back, beyond, up_v, down_v)
    back = lax.all_to_all(
        back.reshape(groups, pad, feat), "exp", split_axis=0, concat_axis=0, tiled=True
    )

    part = min(512, share)
    total = shape((share, feat), F32)
    both_rows = [pltpu.VMEM((2 * slots, feat), BF16)] * 2
    up_sum, down_sum = call(
        functools.partial(own_weights_kernel, part, share),
        "own_weights",
        [total, total],
        [near, beyond, up_v, down_v],
        [IN_VMEM] * 4,
        both_rows,
        8 * unit * share,
        2 * slots * share,
        LARGE,
    )
    if mirrors == 1:
        grad_up, grad_down = up_sum.astype(BF16)[None], down_sum.astype(BF16)[None]
    else:
        others = [a for pair in zip(near_others, far_others) for a in pair]
        grad_up, grad_down = call(
            functools.partial(other_weights_kernel, part, share, mirrors),
            "other_weights",
            [shape((1, share, feat), BF16)] * 2,
            [*others, up_v, down_v, up_sum, down_sum],
            [IN_VMEM] * (len(others) + 4),
            both_rows,
            AHEAD,
            2 * slots * share,
            LARGE,
        )

    d_tokens, d_gates = call(
        functools.partial(combine_kernel, cap),
        "combine",
        [shape((rows, feat), BF16), shape((2, rows), BF16)],
        [routes_t, gates_t, pick, back],
        [IN_VMEM] * 4,
        [],
        2 * unit * rows,
    )
    return d_tokens, d_gates.T, grad_up, grad_down


def solution(mesh):
    by_both = P(("rep", "exp"), None)
    by_expert = P("exp", None, None)
    return jax.shard_map(
        local,
        mesh=mesh,
        in_specs=(by_both, by_both, by_both, by_both, by_expert, by_expert),
        out_specs=(by_both, by_both, P("exp", "rep", None), P("exp", "rep", None)),
        check_vma=False,
    )
```

```python
import functools
import math

import jax
import jax.numpy as jnp
from jax import lax
from jax.experimental import pallas as pl
from jax.experimental.pallas import tpu as pltpu
from jax.sharding import PartitionSpec as P

F32 = jnp.float32
BF16 = jnp.bfloat16
SMALL, MEDIUM, LARGE = 8 << 20, 12 << 20, 24 << 20
AHEAD = 10**11
IN_HBM = pl.BlockSpec(memory_space=pltpu.HBM)
IN_VMEM = pl.BlockSpec(memory_space=pltpu.VMEM)
DMA = pltpu.SemaphoreType.DMA


def dot(left, right, left_dim, right_dim):
    return lax.dot_general(
        left, right, (((left_dim,), (right_dim,)), ((), ())), preferred_element_type=F32
    )


def silu_parts(preact):
    sigma = 0.5 * jnp.tanh(0.5 * preact) + 0.5
    active = preact * sigma
    return active, sigma + active * (1.0 - sigma)


def call(body, name, outs, args, in_specs, scratch, flops, transcendentals=0, limit=MEDIUM):
    moved = sum(math.prod(a.shape) * a.dtype.itemsize for a in (*args, *outs))
    return pl.pallas_call(
        body,
        name=name,
        out_shape=outs,
        in_specs=in_specs,
        out_specs=[IN_VMEM] * len(outs),
        scratch_shapes=scratch,
        compiler_params=pltpu.CompilerParams(vmem_limit_bytes=limit),
        cost_estimate=pl.CostEstimate(
            flops=flops, bytes_accessed=moved, transcendentals=transcendentals
        ),
    )(*args)


def slots_of(routes, experts, first):
    rows = routes.shape[1]
    number = lax.broadcasted_iota(jnp.int32, (experts, rows), 0) + first
    hot = [number == routes[k : k + 1, :] for k in range(2)]
    as_num = [jnp.where(h, 1.0, 0.0).astype(F32) for h in hot]
    before = jnp.where(
        lax.broadcasted_iota(jnp.int32, (rows, rows), 0)
        < lax.broadcasted_iota(jnp.int32, (rows, rows), 1),
        1.0,
        0.0,
    ).astype(BF16)
    count = [dot(n.astype(BF16), before, 1, 0) for n in as_num]
    total = jnp.sum(as_num[0], axis=1, keepdims=True)
    place = [count[0], count[1] + total]
    slot = [
        jnp.sum(jnp.where(h, p, 0.0), axis=0, keepdims=True).astype(jnp.int32)
        for h, p in zip(hot, place)
    ]
    return hot, slot


def picks_of(routes, experts, first, pad):
    _, slot = slots_of(routes, experts, first)
    index = lax.broadcasted_iota(jnp.int32, (experts * pad, routes.shape[1]), 0)
    return [index == (routes[k : k + 1, :] - first) * pad + slot[k] for k in range(2)]


def unpack(packed_ref, rows):
    notes = packed_ref[2 * rows :, :].astype(F32)
    return notes[0:2, 0:rows].astype(jnp.int32), notes[2:4, 0:rows]


def pack_kernel(routes_hbm, gates_hbm, tok_hbm, cot_hbm, out_ref, routes_ref, gates_ref, sems):
    rows, feat = tok_hbm.shape
    pairs = [
        (routes_hbm, routes_ref),
        (gates_hbm, gates_ref),
        (tok_hbm, out_ref.at[0:rows, :]),
        (cot_hbm, out_ref.at[rows : 2 * rows, :]),
    ]
    copies = [
        pltpu.make_async_copy(src, dst, sems.at[i]) for i, (src, dst) in enumerate(pairs)
    ]
    for copy in copies:
        copy.start()
    copies[0].wait()
    copies[1].wait()
    notes = [routes_ref[...].astype(F32), gates_ref[...].astype(F32), jnp.zeros((12, rows), F32)]
    out_ref[2 * rows :, 0:rows] = jnp.concatenate(notes, axis=0).astype(BF16)
    out_ref[2 * rows :, rows:] = jnp.zeros((16, feat - rows), BF16)
    copies[2].wait()
    copies[3].wait()


def slots_kernel(rows, packed_ref, out_ref):
    experts, both, feat = out_ref.shape
    pad = both // 2
    first = lax.axis_index("exp") // experts * experts
    routes, gates = unpack(packed_ref, rows)
    pick = picks_of(routes, experts, first, pad)
    plain = jnp.where(pick[0] | pick[1], 1.0, 0.0).astype(BF16)
    scaled = (
        jnp.where(pick[0], gates[0:1, :], 0.0) + jnp.where(pick[1], gates[1:2, :], 0.0)
    ).astype(BF16)
    tok = packed_ref[0:rows, :]
    cot = packed_ref[rows : 2 * rows, :]
    out_ref[:, 0:pad, :] = dot(plain, tok, 1, 0).astype(BF16).reshape(experts, pad, feat)
    out_ref[:, pad:, :] = dot(scaled, cot, 1, 0).astype(BF16).reshape(experts, pad, feat)


def fetch(up_hbm, down_hbm, up_ref, down_ref, sems, base, block):
    copies = []
    for step in range(up_ref.shape[0] // block):
        to = pl.ds(step * block, block)
        of = pl.ds(pl.multiple_of(base + step * block, block), block)
        for src, dst in [(up_hbm, up_ref), (down_hbm, down_ref)]:
            sem = sems.at[len(copies)]
            copies.append(pltpu.make_async_copy(src.at[0, of, :], dst.at[to, :], sem))
            copies[-1].start()
    return copies


def split_rows(ref):
    experts, both, feat = ref.shape
    pad = both // 2
    return (
        ref[:, 0:pad, :].reshape(experts * pad, feat),
        ref[:, pad:, :].reshape(experts * pad, feat),
    )


def backward(cap, block, disp_ref, up_ref, down_ref, grad_acc, gate_acc, put, copies):
    origins, both, feat = disp_ref.shape
    pad = both // 2
    slots = origins * pad
    rows, grads = split_rows(disp_ref)
    for step in range(up_ref.shape[0] // block):
        part = pl.ds(step * block, block)
        copies[2 * step].wait()
        up = up_ref[part, :]
        active, slope = silu_parts(dot(rows, up, 1, 1))
        copies[2 * step + 1].wait()
        back = dot(grads, down_ref[part, :], 1, 1)
        hid_grad = (back * slope).astype(BF16)
        gate = active.astype(BF16).astype(F32) * back
        gate = sum(gate[:, i : i + 128] for i in range(0, block, 128))
        in_grad = dot(hid_grad, up, 1, 0)
        if step == 0:
            grad_acc[...] = in_grad
            gate_acc[...] = gate
        else:
            grad_acc[...] += in_grad
            gate_acc[...] += gate
    gate = jnp.sum(gate_acc[...], axis=1, keepdims=True)
    spot = lax.broadcasted_iota(jnp.int32, (slots, 128), 0) % pad
    lane = lax.broadcasted_iota(jnp.int32, (slots, 128), 1)
    gate = jnp.where(spot == lane, gate, 0.0).reshape(origins, pad, 128)
    gate = jnp.sum(gate, axis=1, keepdims=True)
    line = lax.broadcasted_iota(jnp.int32, (pad, 128), 0)
    for k in range(origins):
        here = slice(k * pad, (k + 1) * pad)
        first = jnp.where(line == cap, gate[k], grad_acc[here, 0:128])
        put(k, first.astype(BF16), grad_acc[here, 128:].astype(BF16))


def near_back_kernel(cap, block, rows, packed_ref, disp_ref, up_hbm, down_hbm, *refs):
    out_ref, pick_ref, grad_acc, gate_acc, up_ref, down_ref, w_sems = refs
    copies = fetch(up_hbm, down_hbm, up_ref, down_ref, w_sems, 0, block)

    def put(k, first, rest):
        out_ref[k, :, 0:128] = first
        out_ref[k, :, 128:] = rest

    backward(cap, block, disp_ref, up_ref, down_ref, grad_acc, gate_acc, put, copies)
    pad = out_ref.shape[1]
    pick = picks_of(unpack(packed_ref, rows)[0], pick_ref.shape[0] // pad, 0, pad)
    pick_ref[...] = jnp.where(pick[0] | pick[1], 1.0, 0.0).astype(BF16)


def far_back_kernel(cap, block, near_ref, disp_ref, up_hbm, down_hbm, *refs):
    out_hbm, grad_acc, gate_acc, up_ref, down_ref, w_sems, out_ref, sems = refs
    copies = fetch(up_hbm, down_hbm, up_ref, down_ref, w_sems, 0, block)
    half = lax.axis_index("exp") // near_ref.shape[0]
    near_copy = pltpu.make_async_copy(near_ref, out_hbm.at[half], sems.at[0])
    near_copy.start()

    def put(k, first, rest):
        out_ref[k, :, 0:128] = first
        out_ref[k, :, 128:] = rest

    backward(cap, block, disp_ref, up_ref, down_ref, grad_acc, gate_acc, put, copies)
    far_copy = pltpu.make_async_copy(out_ref, out_hbm.at[1 - half], sems.at[1])
    far_copy.start()
    near_copy.wait()
    far_copy.wait()


def weight_parts(block, share, disp_refs, up_ref, down_ref, rows_ref, grads_ref, store, copies):
    size = rows_ref.shape[0] // len(disp_refs)
    for i, ref in enumerate(disp_refs):
        here = slice(i * size, (i + 1) * size)
        rows_ref[here, :], grads_ref[here, :] = split_rows(ref)
    for step in range(share // block):
        here = pl.ds(step * block, block)
        for copy in copies[2 * step : 2 * step + 2]:
            copy.wait()
        active, slope = silu_parts(dot(up_ref[here, :], rows_ref[...], 1, 1))
        back = dot(down_ref[here, :], grads_ref[...], 1, 1)
        hid_grad = (back * slope).astype(BF16)
        up_part = dot(hid_grad, rows_ref[...], 1, 0)
        down_part = dot(active.astype(BF16), grads_ref[...], 1, 0)
        store(here, up_part, down_part)


def own_weights_kernel(block, share, near_ref, far_ref, up_hbm, down_hbm, *refs):
    up_acc, down_acc, rows_ref, grads_ref, up_ref, down_ref, w_sems = refs
    base = lax.axis_index("rep") * share
    copies = fetch(up_hbm, down_hbm, up_ref, down_ref, w_sems, base, block)

    def store(here, up_part, down_part):
        up_acc[here, :] = up_part
        down_acc[here, :] = down_part

    both = [near_ref, far_ref]
    weight_parts(block, share, both, up_ref, down_ref, rows_ref, grads_ref, store, copies)


def other_weights_kernel(block, share, mirrors, *refs):
    pieces, refs = refs[:-11], refs[-11:]
    up_hbm, down_hbm, up_acc, down_acc, grad_up_ref, grad_down_ref, rows_ref, grads_ref = refs[:8]
    up_ref, down_ref, w_sems = refs[8:]
    base = lax.axis_index("rep") * share
    copies = fetch(up_hbm, down_hbm, up_ref, down_ref, w_sems, base, block)
    for mirror in range(mirrors - 1):

        def store(here, up_part, down_part):
            up_part += up_acc[here, :]
            down_part += down_acc[here, :]
            if mirror == mirrors - 2:
                grad_up_ref[0, here, :] = up_part.astype(BF16)
                grad_down_ref[0, here, :] = down_part.astype(BF16)
            else:
                up_acc[here, :] = up_part
                down_acc[here, :] = down_part

        both = pieces[2 * mirror : 2 * mirror + 2]
        copies = copies if mirror == 0 else []
        weight_parts(block, share, both, up_ref, down_ref, rows_ref, grads_ref, store, copies)


def combine_kernel(cap, routes_ref, gates_ref, pick_ref, back_ref, d_tok_ref, d_gate_ref):
    groups, pad, feat = back_ref.shape
    back = back_ref[...]
    d_tok_ref[...] = dot(pick_ref[...], back.reshape(groups * pad, feat), 0, 0).astype(BF16)
    routes = routes_ref[...]
    gates = gates_ref[...].astype(F32)
    hot, slot = slots_of(routes, groups, 0)
    lane = lax.broadcasted_iota(jnp.int32, (128, routes.shape[1]), 0)
    values = back[:, cap, 0:128]
    for k in range(2):
        spot = jnp.where(lane == slot[k], 1.0, 0.0).astype(BF16)
        found = jnp.where(hot[k], dot(values, spot, 1, 0), 0.0)
        found = jnp.sum(found, axis=0, keepdims=True)
        d_gate_ref[k : k + 1, :] = (found / gates[k : k + 1, :]).astype(BF16)


def local(tokens, gates, routes, cotangent, w_up, w_down):
    rows, feat = tokens.shape
    hidden = w_up.shape[1]
    groups = lax.axis_size("exp")
    mirrors = lax.axis_size("rep")
    cap = max(2, 3 * rows // groups)
    pad = (cap // 16 + 1) * 16
    half = groups // 2
    slots = half * pad
    share = hidden // mirrors
    routes_t, gates_t = routes.T, gates.T
    far = functools.partial(pltpu.with_memory_space_constraint, memory_space=pltpu.HBM)
    shape = jax.ShapeDtypeStruct
    unit = 2 * slots * feat
    disp_shape = shape((half, 2 * pad, feat), BF16)
    across = [(i, (i + half) % groups) for i in range(groups)]
    (packed,) = call(
        pack_kernel,
        "pack",
        [shape((2 * rows + 16, feat), BF16)],
        [far(a) for a in (routes_t, gates_t, tokens, cotangent)],
        [IN_HBM] * 4,
        [pltpu.VMEM((2, rows), jnp.int32), pltpu.VMEM((2, rows), BF16), DMA((4,))],
        0,
        0,
        SMALL,
    )
    partner = lax.ppermute(packed, "exp", across)

    (near_out,) = call(
        functools.partial(slots_kernel, rows),
        "near_slots",
        [disp_shape],
        [packed],
        [IN_VMEM],
        [],
        2 * unit * rows,
        0,
        SMALL,
    )
    halves = [list(range(half)), list(range(half, groups))]
    within = functools.partial(
        lax.all_to_all,
        axis_name="exp",
        split_axis=0,
        concat_axis=0,
        axis_index_groups=halves,
        tiled=True,
    )
    near = within(near_out)
    mirror_hops = [
        [(i, (i + shift) % mirrors) for i in range(mirrors)] for shift in range(1, mirrors)
    ]
    near_others = [lax.ppermute(near, "rep", hops) for hops in mirror_hops]
    (far_out,) = call(
        functools.partial(slots_kernel, rows),
        "far_slots",
        [disp_shape],
        [partner],
        [IN_VMEM],
        [],
        AHEAD,
        0,
        SMALL,
    )
    beyond = within(far_out)
    far_others = [lax.ppermute(beyond, "rep", hops) for hops in mirror_hops]

    block = min(512, hidden)
    scratch = [
        pltpu.VMEM((slots, feat), F32),
        pltpu.VMEM((slots, 128), F32),
        pltpu.VMEM((hidden, feat), BF16),
        pltpu.VMEM((hidden, feat), BF16),
        DMA((2 * hidden // block,)),
    ]
    near_back, pick = call(
        functools.partial(near_back_kernel, cap, block, rows),
        "near_backward",
        [shape((half, pad, feat), BF16), shape((groups * pad, rows), BF16)],
        [packed, near, far(w_up), far(w_down)],
        [IN_VMEM] * 2 + [IN_HBM] * 2,
        scratch,
        3 * unit * hidden,
        slots * hidden,
    )
    back = pl.pallas_call(
        functools.partial(far_back_kernel, cap, block),
        name="far_backward",
        out_shape=pltpu.HBM((2, half, pad, feat), BF16),
        in_specs=[IN_VMEM] * 2 + [IN_HBM] * 2,
        out_specs=IN_HBM,
        scratch_shapes=scratch + [pltpu.VMEM((half, pad, feat), BF16), DMA((2,))],
        compiler_params=pltpu.CompilerParams(vmem_limit_bytes=MEDIUM),
        cost_estimate=pl.CostEstimate(
            flops=AHEAD,
            bytes_accessed=4 * hidden * feat,
            transcendentals=slots * hidden,
        ),
    )(near_back, beyond, far(w_up), far(w_down))
    back = lax.all_to_all(
        back.reshape(groups, pad, feat), "exp", split_axis=0, concat_axis=0, tiled=True
    )

    part = min(512, share)
    total = shape((share, feat), F32)
    both_rows = [
        pltpu.VMEM((2 * slots, feat), BF16),
        pltpu.VMEM((2 * slots, feat), BF16),
        pltpu.VMEM((share, feat), BF16),
        pltpu.VMEM((share, feat), BF16),
        DMA((2 * share // part,)),
    ]
    up_sum, down_sum = call(
        functools.partial(own_weights_kernel, part, share),
        "own_weights",
        [total, total],
        [near, beyond, far(w_up), far(w_down)],
        [IN_VMEM] * 2 + [IN_HBM] * 2,
        both_rows,
        8 * unit * share,
        2 * slots * share,
        LARGE,
    )
    if mirrors == 1:
        grad_up, grad_down = up_sum.astype(BF16)[None], down_sum.astype(BF16)[None]
    else:
        others = [a for pair in zip(near_others, far_others) for a in pair]
        grad_up, grad_down = call(
            functools.partial(other_weights_kernel, part, share, mirrors),
            "other_weights",
            [shape((1, share, feat), BF16)] * 2,
            [*others, far(w_up), far(w_down), up_sum, down_sum],
            [IN_VMEM] * len(others) + [IN_HBM] * 2 + [IN_VMEM] * 2,
            both_rows,
            AHEAD,
            2 * slots * share,
            LARGE,
        )

    d_tokens, d_gates = call(
        functools.partial(combine_kernel, cap),
        "combine",
        [shape((rows, feat), BF16), shape((2, rows), BF16)],
        [routes_t, gates_t, pick, back],
        [IN_VMEM] * 4,
        [],
        2 * unit * rows,
    )
    return d_tokens, d_gates.T, grad_up, grad_down


def solution(mesh):
    by_both = P(("rep", "exp"), None)
    by_expert = P("exp", None, None)
    return jax.shard_map(
        local,
        mesh=mesh,
        in_specs=(by_both, by_both, by_both, by_both, by_expert, by_expert),
        out_specs=(by_both, by_both, P("exp", "rep", None), P("exp", "rep", None)),
        check_vma=False,
    )
```

```python
import functools
import itertools

import jax
import jax.numpy as jnp
from jax import lax
from jax.experimental import pallas as pl
from jax.experimental.pallas import tpu as pltpu
from jax.sharding import PartitionSpec as P

F32 = jnp.float32
BF16 = jnp.bfloat16
SMALL, MEDIUM, LARGE = 8 << 20, 12 << 20, 24 << 20
AHEAD = 10**11
IN_HBM = pl.BlockSpec(memory_space=pltpu.HBM)
IN_VMEM = pl.BlockSpec(memory_space=pltpu.VMEM)
DMA = pltpu.SemaphoreType.DMA


def dot(left, right, left_dim, right_dim):
    return lax.dot_general(
        left, right, (((left_dim,), (right_dim,)), ((), ())), preferred_element_type=F32
    )


def silu_parts(preact):
    sigma = 0.5 * jnp.tanh(0.5 * preact) + 0.5
    active = preact * sigma
    return active, sigma + active * (1.0 - sigma)


def call(body, name, outs, args, in_specs, scratch, flops, transcendentals=0, limit=MEDIUM):
    moved = sum(a.size * a.dtype.itemsize for a in (*args, *outs))
    return pl.pallas_call(
        body,
        name=name,
        out_shape=outs,
        in_specs=in_specs,
        out_specs=[IN_VMEM] * len(outs),
        scratch_shapes=scratch,
        compiler_params=pltpu.CompilerParams(vmem_limit_bytes=limit),
        cost_estimate=pl.CostEstimate(
            flops=flops, bytes_accessed=moved, transcendentals=transcendentals
        ),
    )(*args)


def paired(chips):
    return chips & (chips - 1) == 0


def hops_to(chips, k):
    if paired(chips):
        return [(2 * i + c, 2 * (i ^ k) + c) for i in range(chips) for c in range(2)]
    return [(2 * i + c, 2 * ((i + k) % chips) + c) for i in range(chips) for c in range(2)]


def pieces_of(experts, chips):
    me = lax.axis_index("exp")
    if paired(chips):
        return experts ^ me
    chip = (experts // 2 - me // 2 + chips) % chips
    return 2 * chip + (experts + me) % 2


def origin_of(k, core, chips):
    me = lax.axis_index("exp")
    if paired(chips):
        return me ^ (2 * k + core)
    return 2 * ((me // 2 - k + chips) % chips) + (me + core) % 2


def slots_of(pieces, number_of):
    rows = pieces.shape[1]
    number = lax.broadcasted_iota(jnp.int32, (number_of, rows), 0)
    hot = [number == pieces[k : k + 1, :] for k in range(2)]
    as_num = [jnp.where(h, 1.0, 0.0).astype(F32) for h in hot]
    before = jnp.where(
        lax.broadcasted_iota(jnp.int32, (rows, rows), 0)
        < lax.broadcasted_iota(jnp.int32, (rows, rows), 1),
        1.0,
        0.0,
    ).astype(BF16)
    count = dot(jnp.concatenate(as_num, axis=0).astype(BF16), before, 1, 0)
    total = jnp.sum(as_num[0], axis=1, keepdims=True)
    place = [count[:number_of], count[number_of:] + total]
    slot = [
        jnp.sum(jnp.where(h, p, 0.0), axis=0, keepdims=True).astype(jnp.int32)
        for h, p in zip(hot, place)
    ]
    return hot, slot


def picks_of(pieces, slot, number_of, pad):
    index = lax.broadcasted_iota(jnp.int32, (number_of * pad, pieces.shape[1]), 0)
    return [index == pieces[k : k + 1, :] * pad + slot[k] for k in range(2)]


def slots_kernel(pad, routes_hbm, gates_hbm, tok_hbm, cot_hbm, *refs):
    chips = len(refs) - 5
    out_refs, refs = refs[:chips], refs[chips:]
    routes_ref, gates_ref, tok_ref, cot_ref, sems = refs
    pairs = [
        (routes_hbm, routes_ref),
        (gates_hbm, gates_ref),
        (tok_hbm, tok_ref),
        (cot_hbm, cot_ref),
    ]
    copies = [
        pltpu.make_async_copy(src, dst, sems.at[i]) for i, (src, dst) in enumerate(pairs)
    ]
    for copy in copies:
        copy.start()
    copies[0].wait()
    copies[1].wait()
    pieces = pieces_of(routes_ref[...], chips)
    gates = gates_ref[...].astype(F32)
    _, slot = slots_of(pieces, 2 * chips)
    pick = picks_of(pieces, slot, 2 * chips, pad)
    plain = jnp.where(pick[0] | pick[1], 1.0, 0.0).astype(BF16)
    scaled = (
        jnp.where(pick[0], gates[0:1, :], 0.0) + jnp.where(pick[1], gates[1:2, :], 0.0)
    ).astype(BF16)
    copies[2].wait()
    copies[3].wait()
    rows = dot(plain, tok_ref[...], 1, 0).astype(BF16)
    grads = dot(scaled, cot_ref[...], 1, 0).astype(BF16)
    for k, out_ref in enumerate(out_refs):
        for i in range(2):
            here = slice((2 * k + i) * pad, (2 * k + i + 1) * pad)
            out_ref[2 * i * pad : (2 * i + 1) * pad, :] = rows[here, :]
            out_ref[(2 * i + 1) * pad : (2 * i + 2) * pad, :] = grads[here, :]


class Fetch:
    def __init__(self, up_hbm, down_hbm, up_ref, down_ref, sems, base, block):
        self.pairs = [(up_hbm, up_ref), (down_hbm, down_ref)]
        self.sems, self.base, self.block = sems, base, block
        self.steps = up_ref.shape[0] // block
        self.copies = []
        self.start()

    def start(self):
        step = len(self.copies)
        if step == self.steps:
            return
        to = pl.ds(step * self.block, self.block)
        of = pl.ds(pl.multiple_of(self.base + step * self.block, self.block), self.block)
        self.copies.append([
            pltpu.make_async_copy(src.at[0, of, :], dst.at[to, :], self.sems.at[2 * step + i])
            for i, (src, dst) in enumerate(self.pairs)
        ])
        for copy in self.copies[-1]:
            copy.start()

    def wait(self, step):
        self.start()
        for copy in self.copies[step]:
            copy.wait()


def gather_rows(pad, blocks, rows_ref, grads_ref):
    for i, (ref, at) in enumerate(blocks):
        here = slice(i * pad, (i + 1) * pad)
        rows_ref[here, :] = ref[at : at + pad, :]
        grads_ref[here, :] = ref[at + pad : at + 2 * pad, :]


def backward(cap, pad, block, blocks, weights, scratch, put):
    rows_ref, grads_ref, grad_acc, gate_acc, up_ref, down_ref, sems = scratch
    fetch = Fetch(*weights, up_ref, down_ref, sems, 0, block)
    gather_rows(pad, blocks, rows_ref, grads_ref)
    slots = rows_ref.shape[0]
    for step in range(up_ref.shape[0] // block):
        part = pl.ds(step * block, block)
        fetch.wait(step)
        up = up_ref[part, :]
        active, slope = silu_parts(dot(rows_ref[...], up, 1, 1))
        back = dot(grads_ref[...], down_ref[part, :], 1, 1)
        hid_grad = (back * slope).astype(BF16)
        gate = active.astype(BF16).astype(F32) * back
        gate = sum(gate[:, i : i + 128] for i in range(0, block, 128))
        in_grad = dot(hid_grad, up, 1, 0)
        if step == 0:
            grad_acc[...] = in_grad
            gate_acc[...] = gate
        else:
            grad_acc[...] += in_grad
            gate_acc[...] += gate
    gate = jnp.sum(gate_acc[...], axis=1, keepdims=True)
    spot = lax.broadcasted_iota(jnp.int32, (slots, 128), 0) % pad
    lane = lax.broadcasted_iota(jnp.int32, (slots, 128), 1)
    gate = jnp.where(spot == lane, gate, 0.0).reshape(len(blocks), pad, 128)
    gate = jnp.sum(gate, axis=1, keepdims=True)
    line = lax.broadcasted_iota(jnp.int32, (pad, 128), 0)
    for k in range(len(blocks)):
        here = slice(k * pad, (k + 1) * pad)
        first = jnp.where(line == cap, gate[k], grad_acc[here, 0:128])
        put(k, first.astype(BF16), grad_acc[here, 128:].astype(BF16))


def blocks_of(pad, direct_refs, sibling_refs):
    direct = [(ref, 0) for ref in direct_refs]
    sibling = [(r, at) for r in sibling_refs for at in range(0, r.shape[0], 2 * pad)]
    return direct, sibling


def direct_back_kernel(cap, pad, block, chips, *refs):
    pieces, (up_hbm, down_hbm, out_ref, *scratch) = refs[:chips], refs[chips:]

    def put(k, first, rest):
        out_ref[k, :, 0:128] = first
        out_ref[k, :, 128:] = rest

    direct, _ = blocks_of(pad, pieces, [])
    backward(cap, pad, block, direct, (up_hbm, down_hbm), scratch, put)


def sibling_back_kernel(cap, pad, block, order, *refs):
    sibling_ref, direct_ref, up_hbm, down_hbm, out_hbm, mine_ref, sems, *scratch = refs
    copies = []

    def send(i, core):
        ref = mine_ref if core else direct_ref
        to = out_hbm.at[origin_of(order[i], core, len(order))]
        copies.append(pltpu.make_async_copy(ref.at[i], to, sems.at[2 * i + core]))
        copies[-1].start()

    for i in range(len(order)):
        send(i, 0)

    def put(k, first, rest):
        mine_ref[k, :, 0:128] = first
        mine_ref[k, :, 128:] = rest
        send(k, 1)

    _, sibling = blocks_of(pad, [], [sibling_ref])
    backward(cap, pad, block, sibling, (up_hbm, down_hbm), scratch, put)
    for copy in copies:
        copy.wait()


def weights_kernel(pad, block, share, direct, sibling, begun, *refs):
    refs = list(refs)
    take = lambda number: [refs.pop(0) for _ in range(number)]
    direct_refs, sibling_refs, weights = take(direct), take(sibling), take(2)
    sums = take(2) if begun else None
    notes = None if begun else take(2)
    out_up, out_down = take(2)
    notes_out = None if begun else take(3)
    rows_ref, grads_ref, up_ref, down_ref, sems = refs
    fetch = Fetch(*weights, up_ref, down_ref, sems, lax.axis_index("rep") * share, block)
    blocks = sum(blocks_of(pad, direct_refs, sibling_refs), [])
    gather_rows(pad, blocks, rows_ref, grads_ref)
    for step in range(share // block):
        here = pl.ds(step * block, block)
        fetch.wait(step)
        active, slope = silu_parts(dot(up_ref[here, :], rows_ref[...], 1, 1))
        back = dot(down_ref[here, :], grads_ref[...], 1, 1)
        hid_grad = (back * slope).astype(BF16)
        up_part = dot(hid_grad, rows_ref[...], 1, 0)
        down_part = dot(active.astype(BF16), grads_ref[...], 1, 0)
        if begun:
            up_part += sums[0][0, here, :]
            down_part += sums[1][0, here, :]
        out_up[0, here, :] = up_part.astype(out_up.dtype)
        out_down[0, here, :] = down_part.astype(out_down.dtype)
    if not begun:
        note_routes(pad, *notes, *notes_out)


def note_routes(pad, routes_ref, gates_ref, pick_ref, hot_ref, spot_ref):
    routes = routes_ref[...]
    gates = gates_ref[...].astype(F32)
    groups = pick_ref.shape[0] // pad
    hot, slot = slots_of(routes, groups)
    pick = picks_of(routes, slot, groups, pad)
    pick_ref[...] = jnp.where(pick[0] | pick[1], 1.0, 0.0).astype(BF16)
    lane = lax.broadcasted_iota(jnp.int32, (128, routes.shape[1]), 0)
    for k in range(2):
        hot_ref[k] = jnp.where(hot[k], 1.0 / gates[k : k + 1, :], 0.0)
        spot_ref[k] = jnp.where(lane == slot[k], 1.0, 0.0).astype(BF16)


def combine_kernel(cap, pick_ref, hot_ref, spot_ref, back_ref, d_tok_ref, d_gate_ref):
    groups, pad, feat = back_ref.shape
    back = back_ref[...]
    d_tok_ref[...] = dot(pick_ref[...], back.reshape(groups * pad, feat), 0, 0).astype(BF16)
    values = back[:, cap, 0:128]
    for k in range(2):
        found = dot(values, spot_ref[k], 1, 0) * hot_ref[k]
        d_gate_ref[k : k + 1, :] = jnp.sum(found, axis=0, keepdims=True).astype(BF16)


def local(tokens, gates, routes, cotangent, w_up, w_down):
    rows, feat = tokens.shape
    hidden = w_up.shape[1]
    groups = lax.axis_size("exp")
    mirrors = lax.axis_size("rep")
    chips = groups // 2
    cap = max(2, 3 * rows // groups)
    pad = (cap // 16 + 1) * 16
    slots = chips * pad
    share = hidden // mirrors
    routes_t, gates_t = routes.T, gates.T
    hbm = functools.partial(pltpu.with_memory_space_constraint, memory_space=pltpu.HBM)
    shape = jax.ShapeDtypeStruct
    unit = 2 * slots * feat

    out = call(
        functools.partial(slots_kernel, pad),
        "slots",
        [shape((4 * pad, feat), BF16)] * chips,
        [hbm(a) for a in (routes_t, gates_t, tokens, cotangent)],
        [IN_HBM] * 4,
        [
            pltpu.VMEM((2, rows), jnp.int32),
            pltpu.VMEM((2, rows), BF16),
            pltpu.VMEM((rows, feat), BF16),
            pltpu.VMEM((rows, feat), BF16),
            DMA((4,)),
        ],
        4 * unit * rows,
    )
    near, far = list(range(1, chips // 2)), list(range(chips // 2, chips))
    order = near[:1] + far[:1]
    for pair in itertools.zip_longest(far[1:], near[1:]):
        order += [k for k in pair if k is not None]
    pieces = [out[0]] + [lax.ppermute(out[k], "exp", hops_to(chips, k)) for k in order]

    swap = [(i, i ^ 1) for i in range(groups)]
    around = [[(i, (i + s) % mirrors) for i in range(mirrors)] for s in range(1, mirrors)]
    handed = jnp.concatenate([piece[2 * pad :] for piece in pieces], axis=0)
    sibling = lax.ppermute(handed, "exp", swap)
    arrived = jnp.concatenate([piece[: 2 * pad] for piece in pieces], axis=0)
    others = [lax.ppermute(a, "rep", hops) for hops in around for a in (arrived, sibling)]

    w_up, w_down = hbm(w_up), hbm(w_down)
    block = min(512, hidden)
    scratch = [
        pltpu.VMEM((slots, feat), BF16),
        pltpu.VMEM((slots, feat), BF16),
        pltpu.VMEM((slots, feat), F32),
        pltpu.VMEM((slots, 128), F32),
        pltpu.VMEM((hidden, feat), BF16),
        pltpu.VMEM((hidden, feat), BF16),
        DMA((2 * hidden // block,)),
    ]
    results = (chips, pad, feat)
    (direct,) = call(
        functools.partial(direct_back_kernel, cap, pad, block, chips),
        "direct_backward",
        [shape(results, BF16)],
        [*pieces, w_up, w_down],
        [IN_VMEM] * chips + [IN_HBM] * 2,
        scratch,
        AHEAD,
        slots * hidden,
    )
    back = pl.pallas_call(
        functools.partial(sibling_back_kernel, cap, pad, block, [0, *order]),
        name="sibling_backward",
        out_shape=pltpu.HBM((groups, pad, feat), BF16),
        in_specs=[IN_VMEM] * 2 + [IN_HBM] * 2,
        out_specs=IN_HBM,
        scratch_shapes=[pltpu.VMEM(results, BF16), DMA((groups,)), *scratch],
        compiler_params=pltpu.CompilerParams(vmem_limit_bytes=MEDIUM),
        cost_estimate=pl.CostEstimate(
            flops=AHEAD, bytes_accessed=4 * hidden * feat, transcendentals=slots * hidden
        ),
    )(sibling, direct, w_up, w_down)
    back = lax.all_to_all(back, "exp", split_axis=0, concat_axis=0, tiled=True)

    part = min(512, share)

    def weights_call(name, direct_in, sibling_in, sums, ended, flops):
        begun = bool(sums)
        number = slots * (len(direct_in) // chips + len(sibling_in))
        notes = [] if begun else [
            shape((groups * pad, rows), BF16),
            shape((2, groups, rows), F32),
            shape((2, 128, rows), BF16),
        ]
        kept = BF16 if ended else F32
        return call(
            functools.partial(
                weights_kernel, pad, part, share, len(direct_in), len(sibling_in), begun
            ),
            name,
            [shape((1, share, feat), kept)] * 2 + notes,
            [*direct_in, *sibling_in, w_up, w_down, *(sums or [routes_t, gates_t])],
            [IN_VMEM] * (len(direct_in) + len(sibling_in)) + [IN_HBM] * 2 + [IN_VMEM] * 2,
            [
                pltpu.VMEM((number, feat), BF16),
                pltpu.VMEM((number, feat), BF16),
                pltpu.VMEM((share, feat), BF16),
                pltpu.VMEM((share, feat), BF16),
                DMA((2 * share // part,)),
            ],
            flops,
            number * share,
            LARGE,
        )

    *sums, pick, hot, spot = weights_call(
        "own_weights", pieces, [sibling], [], not others, 8 * unit * share
    )
    for i, other in enumerate(others):
        sums = weights_call("other_weights", [], [other], sums, i == len(others) - 1, AHEAD)
    grad_up, grad_down = sums

    d_tokens, d_gates = call(
        functools.partial(combine_kernel, cap),
        "combine",
        [shape((rows, feat), BF16), shape((2, rows), BF16)],
        [pick, hot, spot, back],
        [IN_VMEM] * 4,
        [],
        4 * unit * rows,
    )
    return d_tokens, d_gates.T, grad_up, grad_down


def solution(mesh):
    by_both = P(("rep", "exp"), None)
    by_expert = P("exp", None, None)
    return jax.shard_map(
        local,
        mesh=mesh,
        in_specs=(by_both, by_both, by_both, by_both, by_expert, by_expert),
        out_specs=(by_both, by_both, P("exp", "rep", None), P("exp", "rep", None)),
        check_vma=False,
    )
```

```python
import functools
import itertools

import jax
import jax.numpy as jnp
from jax import lax
from jax.experimental import pallas as pl
from jax.experimental.pallas import tpu as pltpu
from jax.sharding import PartitionSpec as P

F32 = jnp.float32
BF16 = jnp.bfloat16
SMALL, MEDIUM, LARGE = 8 << 20, 12 << 20, 24 << 20
AHEAD = 10**11
IN_HBM = pl.BlockSpec(memory_space=pltpu.HBM)
IN_VMEM = pl.BlockSpec(memory_space=pltpu.VMEM)
DMA = pltpu.SemaphoreType.DMA


def dot(left, right, left_dim, right_dim):
    return lax.dot_general(
        left, right, (((left_dim,), (right_dim,)), ((), ())), preferred_element_type=F32
    )


def silu_parts(preact):
    sigma = 0.5 * jnp.tanh(0.5 * preact) + 0.5
    active = preact * sigma
    return active, sigma + active * (1.0 - sigma)


def call(body, name, outs, args, in_specs, scratch, flops, transcendentals=0, limit=MEDIUM):
    moved = sum(a.size * a.dtype.itemsize for a in (*args, *outs)) if flops else 0
    return pl.pallas_call(
        body,
        name=name,
        out_shape=outs,
        in_specs=in_specs,
        out_specs=[IN_VMEM] * len(outs),
        scratch_shapes=scratch,
        compiler_params=pltpu.CompilerParams(vmem_limit_bytes=limit),
        cost_estimate=pl.CostEstimate(
            flops=flops, bytes_accessed=moved, transcendentals=transcendentals if flops else 0
        ),
    )(*args)


def paired(chips):
    return chips & (chips - 1) == 0


def hops_to(chips, k):
    if paired(chips):
        return [(2 * i + c, 2 * (i ^ k) + c) for i in range(chips) for c in range(2)]
    return [(2 * i + c, 2 * ((i + k) % chips) + c) for i in range(chips) for c in range(2)]


def pieces_of(experts, chips):
    me = lax.axis_index("exp")
    if paired(chips):
        return experts ^ me
    chip = (experts // 2 - me // 2 + chips) % chips
    return 2 * chip + (experts + me) % 2


def origin_of(k, core, chips):
    me = lax.axis_index("exp")
    if paired(chips):
        return me ^ (2 * k + core)
    return 2 * ((me // 2 - k + chips) % chips) + (me + core) % 2


def slots_of(pieces, number_of):
    rows = pieces.shape[1]
    number = lax.broadcasted_iota(jnp.int32, (number_of, rows), 0)
    hot = [number == pieces[k : k + 1, :] for k in range(2)]
    as_num = [jnp.where(h, 1.0, 0.0).astype(F32) for h in hot]
    before = jnp.where(
        lax.broadcasted_iota(jnp.int32, (rows, rows), 0)
        < lax.broadcasted_iota(jnp.int32, (rows, rows), 1),
        1.0,
        0.0,
    ).astype(BF16)
    count = dot(jnp.concatenate(as_num, axis=0).astype(BF16), before, 1, 0)
    total = jnp.sum(as_num[0], axis=1, keepdims=True)
    place = [count[:number_of], count[number_of:] + total]
    slot = [
        jnp.sum(jnp.where(h, p, 0.0), axis=0, keepdims=True).astype(jnp.int32)
        for h, p in zip(hot, place)
    ]
    return hot, slot


def picks_of(pieces, slot, number_of, pad):
    index = lax.broadcasted_iota(jnp.int32, (number_of * pad, pieces.shape[1]), 0)
    return [index == pieces[k : k + 1, :] * pad + slot[k] for k in range(2)]


def slots_kernel(pad, routes_hbm, gates_hbm, tok_hbm, cot_hbm, *refs):
    chips = len(refs) - 5
    out_refs, refs = refs[:chips], refs[chips:]
    routes_ref, gates_ref, tok_ref, cot_ref, sems = refs
    pairs = [
        (routes_hbm, routes_ref),
        (gates_hbm, gates_ref),
        (tok_hbm, tok_ref),
        (cot_hbm, cot_ref),
    ]
    copies = [
        pltpu.make_async_copy(src, dst, sems.at[i]) for i, (src, dst) in enumerate(pairs)
    ]
    for copy in copies:
        copy.start()
    copies[0].wait()
    copies[1].wait()
    pieces = pieces_of(routes_ref[...], chips)
    gates = gates_ref[...].astype(F32)
    _, slot = slots_of(pieces, 2 * chips)
    pick = picks_of(pieces, slot, 2 * chips, pad)
    plain = jnp.where(pick[0] | pick[1], 1.0, 0.0).astype(BF16)
    scaled = (
        jnp.where(pick[0], gates[0:1, :], 0.0) + jnp.where(pick[1], gates[1:2, :], 0.0)
    ).astype(BF16)
    copies[2].wait()
    copies[3].wait()
    rows = dot(plain, tok_ref[...], 1, 0).astype(BF16)
    grads = dot(scaled, cot_ref[...], 1, 0).astype(BF16)
    for k, out_ref in enumerate(out_refs):
        for i in range(2):
            here = slice((2 * k + i) * pad, (2 * k + i + 1) * pad)
            out_ref[2 * i * pad : (2 * i + 1) * pad, :] = rows[here, :]
            out_ref[(2 * i + 1) * pad : (2 * i + 2) * pad, :] = grads[here, :]


def steps_of(size, block):
    half = block // 2
    return [(0, half), (half, half)] + [(at, block) for at in range(block, size, block)]


class Fetch:
    def __init__(self, up_hbm, down_hbm, up_ref, down_ref, sems, base, steps):
        self.pairs = [(up_hbm, up_ref), (down_hbm, down_ref)]
        self.sems, self.base, self.steps = sems, base, steps
        self.copies = []
        self.start()
        self.start()

    def start(self):
        number = len(self.copies)
        if number == len(self.steps):
            return
        at, size = self.steps[number]
        to, of = pl.ds(at, size), pl.ds(pl.multiple_of(self.base + at, size), size)
        self.copies.append([
            pltpu.make_async_copy(src.at[0, of, :], dst.at[to, :], self.sems.at[2 * number + i])
            for i, (src, dst) in enumerate(self.pairs)
        ])
        for copy in self.copies[-1]:
            copy.start()

    def wait(self, number):
        for copy in self.copies[number]:
            copy.wait()
        self.start()


def fetch_kernel(up_hbm, down_hbm, up_ref, down_ref, sems):
    size = up_ref.shape[0]
    for copy in Fetch(up_hbm, down_hbm, up_ref, down_ref, sems, 0, [(0, size)]).copies[0]:
        copy.wait()


def hand_kernel(pad, at, *refs):
    piece_refs, out_ref = refs[:-2], refs[-1]
    for i, ref in enumerate(piece_refs):
        out_ref[2 * i * pad : 2 * (i + 1) * pad, :] = ref[at : at + 2 * pad, :]


def gather_rows(pad, blocks, rows_ref, grads_ref):
    for i, (ref, at) in enumerate(blocks):
        here = slice(i * pad, (i + 1) * pad)
        rows_ref[here, :] = ref[at : at + pad, :]
        grads_ref[here, :] = ref[at + pad : at + 2 * pad, :]


def backward(cap, pad, block, blocks, up_ref, down_ref, scratch, put):
    rows_ref, grads_ref, grad_acc, gate_acc = scratch
    gather_rows(pad, blocks, rows_ref, grads_ref)
    slots = rows_ref.shape[0]
    for step in range(up_ref.shape[0] // block):
        part = pl.ds(step * block, block)
        up = up_ref[part, :]
        active, slope = silu_parts(dot(rows_ref[...], up, 1, 1))
        back = dot(grads_ref[...], down_ref[part, :], 1, 1)
        hid_grad = (back * slope).astype(BF16)
        gate = active.astype(BF16).astype(F32) * back
        gate = sum(gate[:, i : i + 128] for i in range(0, block, 128))
        in_grad = dot(hid_grad, up, 1, 0)
        if step == 0:
            grad_acc[...] = in_grad
            gate_acc[...] = gate
        else:
            grad_acc[...] += in_grad
            gate_acc[...] += gate
    gate = jnp.sum(gate_acc[...], axis=1, keepdims=True)
    spot = lax.broadcasted_iota(jnp.int32, (slots, 128), 0) % pad
    lane = lax.broadcasted_iota(jnp.int32, (slots, 128), 1)
    gate = jnp.where(spot == lane, gate, 0.0).reshape(len(blocks), pad, 128)
    gate = jnp.sum(gate, axis=1, keepdims=True)
    line = lax.broadcasted_iota(jnp.int32, (pad, 128), 0)
    for k in range(len(blocks)):
        here = slice(k * pad, (k + 1) * pad)
        first = jnp.where(line == cap, gate[k], grad_acc[here, 0:128])
        put(k, first.astype(BF16), grad_acc[here, 128:].astype(BF16))


def blocks_of(pad, refs):
    return [(ref, at) for ref in refs for at in range(0, ref.shape[0], 2 * pad)]


def direct_back_kernel(cap, pad, block, chips, *refs):
    pieces, (up_ref, down_ref, out_ref, *scratch) = refs[:chips], refs[chips:]

    def put(k, first, rest):
        out_ref[k, :, 0:128] = first
        out_ref[k, :, 128:] = rest

    blocks = [(ref, 0) for ref in pieces]
    backward(cap, pad, block, blocks, up_ref, down_ref, scratch, put)


def sibling_back_kernel(cap, pad, block, order, *refs):
    sibling_ref, direct_ref, up_ref, down_ref, out_hbm, mine_ref, sems, *scratch = refs
    copies = []

    def send(i, core):
        ref = mine_ref if core else direct_ref
        to = out_hbm.at[origin_of(order[i], core, len(order))]
        copies.append(pltpu.make_async_copy(ref.at[i], to, sems.at[2 * i + core]))
        copies[-1].start()

    for i in range(len(order)):
        send(i, 0)

    def put(k, first, rest):
        mine_ref[k, :, 0:128] = first
        mine_ref[k, :, 128:] = rest
        send(k, 1)

    blocks = blocks_of(pad, [sibling_ref])
    backward(cap, pad, block, blocks, up_ref, down_ref, scratch, put)
    for copy in copies:
        copy.wait()


def weights_kernel(pad, block, share, number, begun, *refs):
    refs = list(refs)
    take = lambda number: [refs.pop(0) for _ in range(number)]
    row_refs, weights = take(number), take(2)
    sums = take(2) if begun else None
    notes = None if begun else take(2)
    out_up, out_down = take(2)
    notes_out = None if begun else take(3)
    rows_ref, grads_ref, up_ref, down_ref, sems = refs
    steps = steps_of(share, block)
    fetch = Fetch(*weights, up_ref, down_ref, sems, lax.axis_index("rep") * share, steps)
    gather_rows(pad, blocks_of(pad, row_refs), rows_ref, grads_ref)
    for step, (at, size) in enumerate(steps):
        here = pl.ds(at, size)
        fetch.wait(step)
        active, slope = silu_parts(dot(up_ref[here, :], rows_ref[...], 1, 1))
        back = dot(down_ref[here, :], grads_ref[...], 1, 1)
        hid_grad = (back * slope).astype(BF16)
        up_part = dot(hid_grad, rows_ref[...], 1, 0)
        down_part = dot(active.astype(BF16), grads_ref[...], 1, 0)
        if begun:
            up_part += sums[0][0, here, :]
            down_part += sums[1][0, here, :]
        out_up[0, here, :] = up_part.astype(out_up.dtype)
        out_down[0, here, :] = down_part.astype(out_down.dtype)
    if not begun:
        note_routes(pad, *notes, *notes_out)


def note_routes(pad, routes_ref, gates_ref, pick_ref, hot_ref, spot_ref):
    routes = routes_ref[...]
    gates = gates_ref[...].astype(F32)
    groups = pick_ref.shape[0] // pad
    hot, slot = slots_of(routes, groups)
    pick = picks_of(routes, slot, groups, pad)
    pick_ref[...] = jnp.where(pick[0] | pick[1], 1.0, 0.0).astype(BF16)
    lane = lax.broadcasted_iota(jnp.int32, (128, routes.shape[1]), 0)
    for k in range(2):
        hot_ref[k] = jnp.where(hot[k], 1.0 / gates[k : k + 1, :], 0.0)
        spot_ref[k] = jnp.where(lane == slot[k], 1.0, 0.0).astype(BF16)


def combine_kernel(cap, pick_ref, hot_ref, spot_ref, back_ref, d_tok_ref, d_gate_ref):
    groups, pad, feat = back_ref.shape
    back = back_ref[...]
    d_tok_ref[...] = dot(pick_ref[...], back.reshape(groups * pad, feat), 0, 0).astype(BF16)
    values = back[:, cap, 0:128]
    for k in range(2):
        found = dot(values, spot_ref[k], 1, 0) * hot_ref[k]
        d_gate_ref[k : k + 1, :] = jnp.sum(found, axis=0, keepdims=True).astype(BF16)


def local(tokens, gates, routes, cotangent, w_up, w_down):
    rows, feat = tokens.shape
    hidden = w_up.shape[1]
    groups = lax.axis_size("exp")
    mirrors = lax.axis_size("rep")
    chips = groups // 2
    cap = max(2, 3 * rows // groups)
    pad = (cap // 16 + 1) * 16
    slots = chips * pad
    share = hidden // mirrors
    routes_t, gates_t = routes.T, gates.T
    hbm = functools.partial(pltpu.with_memory_space_constraint, memory_space=pltpu.HBM)
    shape = jax.ShapeDtypeStruct
    unit = 2 * slots * feat

    out = call(
        functools.partial(slots_kernel, pad),
        "slots",
        [shape((4 * pad, feat), BF16)] * chips,
        [hbm(a) for a in (routes_t, gates_t, tokens, cotangent)],
        [IN_HBM] * 4,
        [
            pltpu.VMEM((2, rows), jnp.int32),
            pltpu.VMEM((2, rows), BF16),
            pltpu.VMEM((rows, feat), BF16),
            pltpu.VMEM((rows, feat), BF16),
            DMA((4,)),
        ],
        4 * unit * rows,
    )
    near, far = list(range(1, chips // 2)), list(range(chips // 2, chips))
    order = [k for pair in itertools.zip_longest(far[:-1], near[:-1]) for k in pair if k is not None]
    order += far[-1:] + near[-1:]
    pieces = [out[0]] + [lax.ppermute(out[k], "exp", hops_to(chips, k)) for k in order]

    swap = [(i, i ^ 1) for i in range(groups)]
    around = [[(i, (i + s) % mirrors) for i in range(mirrors)] for s in range(1, mirrors)]
    w_up, w_down = hbm(w_up), hbm(w_down)
    up_v, down_v = call(
        fetch_kernel,
        "fetch_weights",
        [shape((hidden, feat), BF16)] * 2,
        [w_up, w_down],
        [IN_HBM] * 2,
        [DMA((2,))],
        0,
        0,
        SMALL,
    )
    (handed,), (arrived,) = [
        call(
            functools.partial(hand_kernel, pad, at),
            name,
            [shape((2 * slots, feat), BF16)],
            [*pieces, up_v],
            [IN_VMEM] * (chips + 1),
            [],
            0,
            0,
            SMALL,
        )
        for at, name in [(2 * pad, "hand_on"), (0, "arrived_rows")]
    ]
    sibling = lax.ppermute(handed, "exp", swap)
    others = [lax.ppermute(a, "rep", hops) for hops in around for a in (arrived, sibling)]

    block = min(512, hidden)
    scratch = [
        pltpu.VMEM((slots, feat), BF16),
        pltpu.VMEM((slots, feat), BF16),
        pltpu.VMEM((slots, feat), F32),
        pltpu.VMEM((slots, 128), F32),
    ]
    results = (chips, pad, feat)
    (direct,) = call(
        functools.partial(direct_back_kernel, cap, pad, block, chips),
        "direct_backward",
        [shape(results, BF16)],
        [*pieces, up_v, down_v],
        [IN_VMEM] * (chips + 2),
        scratch,
        AHEAD,
        slots * hidden,
    )
    back = pl.pallas_call(
        functools.partial(sibling_back_kernel, cap, pad, block, [0, *order]),
        name="sibling_backward",
        out_shape=pltpu.HBM((groups, pad, feat), BF16),
        in_specs=[IN_VMEM] * 4,
        out_specs=IN_HBM,
        scratch_shapes=[pltpu.VMEM(results, BF16), DMA((groups,)), *scratch],
        compiler_params=pltpu.CompilerParams(vmem_limit_bytes=MEDIUM),
        cost_estimate=pl.CostEstimate(
            flops=AHEAD, bytes_accessed=4 * hidden * feat, transcendentals=slots * hidden
        ),
    )(sibling, direct, up_v, down_v)
    back = lax.all_to_all(back, "exp", split_axis=0, concat_axis=0, tiled=True)

    part = min(512, share)

    def weights_call(name, row_ins, sums, ended, flops):
        begun = bool(sums)
        number = slots * len(row_ins)
        notes = [] if begun else [
            shape((groups * pad, rows), BF16),
            shape((2, groups, rows), F32),
            shape((2, 128, rows), BF16),
        ]
        kept = BF16 if ended else F32
        return call(
            functools.partial(weights_kernel, pad, part, share, len(row_ins), begun),
            name,
            [shape((1, share, feat), kept)] * 2 + notes,
            [*row_ins, w_up, w_down, *(sums or [routes_t, gates_t])],
            [IN_VMEM] * len(row_ins) + [IN_HBM] * 2 + [IN_VMEM] * 2,
            [
                pltpu.VMEM((number, feat), BF16),
                pltpu.VMEM((number, feat), BF16),
                pltpu.VMEM((share, feat), BF16),
                pltpu.VMEM((share, feat), BF16),
                DMA((2 * share // part + 2,)),
            ],
            flops,
            number * share,
            LARGE,
        )

    *sums, pick, hot, spot = weights_call("own_weights", [arrived, sibling], [], not others, 0)
    for i, other in enumerate(others):
        ended = i == len(others) - 1
        sums = weights_call("other_weights", [other], sums, ended, AHEAD if ended else 0)
    grad_up, grad_down = sums

    d_tokens, d_gates = call(
        functools.partial(combine_kernel, cap),
        "combine",
        [shape((rows, feat), BF16), shape((2, rows), BF16)],
        [pick, hot, spot, back],
        [IN_VMEM] * 4,
        [],
        4 * unit * rows,
        0,
        SMALL,
    )
    return d_tokens, d_gates.T, grad_up, grad_down


def solution(mesh):
    by_both = P(("rep", "exp"), None)
    by_expert = P("exp", None, None)
    return jax.shard_map(
        local,
        mesh=mesh,
        in_specs=(by_both, by_both, by_both, by_both, by_expert, by_expert),
        out_specs=(by_both, by_both, P("exp", "rep", None), P("exp", "rep", None)),
        check_vma=False,
    )
```

```python
import functools
import math

import jax
import jax.numpy as jnp
from jax import lax
from jax.experimental import pallas as pl
from jax.experimental.pallas import tpu as pltpu
from jax.sharding import PartitionSpec as P

F32 = jnp.float32
BF16 = jnp.bfloat16
SMALL, MEDIUM, LARGE = 8 << 20, 12 << 20, 24 << 20
AHEAD = 10**11
IN_HBM = pl.BlockSpec(memory_space=pltpu.HBM)
IN_VMEM = pl.BlockSpec(memory_space=pltpu.VMEM)
DMA = pltpu.SemaphoreType.DMA


def dot(left, right, left_dim, right_dim):
    return lax.dot_general(
        left, right, (((left_dim,), (right_dim,)), ((), ())), preferred_element_type=F32
    )


def silu_parts(preact):
    sigma = 0.5 * jnp.tanh(0.5 * preact) + 0.5
    active = preact * sigma
    return active, sigma + active * (1.0 - sigma)


def call(body, name, outs, args, in_specs, scratch, flops, transcendentals=0, limit=MEDIUM, out_specs=None):
    moved = sum(math.prod(a.shape) * a.dtype.itemsize for a in (*args, *outs)) if flops else 0
    return pl.pallas_call(
        body,
        name=name,
        out_shape=outs,
        in_specs=in_specs,
        out_specs=out_specs or [IN_VMEM] * len(outs),
        scratch_shapes=scratch,
        compiler_params=pltpu.CompilerParams(vmem_limit_bytes=limit),
        cost_estimate=pl.CostEstimate(
            flops=flops, bytes_accessed=moved, transcendentals=transcendentals if flops else 0
        ),
    )(*args)


def paired(chips):
    return chips & (chips - 1) == 0


def hops_to(chips, k):
    if paired(chips):
        return [(2 * i + c, 2 * (i ^ k) + c) for i in range(chips) for c in range(2)]
    return [(2 * i + c, 2 * ((i + k) % chips) + c) for i in range(chips) for c in range(2)]


def pieces_of(experts, chips):
    me = lax.axis_index("exp")
    if paired(chips):
        return experts ^ me
    chip = (experts // 2 - me // 2 + chips) % chips
    return 2 * chip + (experts + me) % 2


def origin_of(k, core, chips):
    me = lax.axis_index("exp")
    if paired(chips):
        return me ^ (2 * k + core)
    return 2 * ((me // 2 - k + chips) % chips) + (me + core) % 2


def slots_of(pieces, number_of):
    rows = pieces.shape[1]
    number = lax.broadcasted_iota(jnp.int32, (number_of, rows), 0)
    hot = [number == pieces[k : k + 1, :] for k in range(2)]
    as_num = [jnp.where(h, 1.0, 0.0).astype(F32) for h in hot]
    before = jnp.where(
        lax.broadcasted_iota(jnp.int32, (rows, rows), 0)
        < lax.broadcasted_iota(jnp.int32, (rows, rows), 1),
        1.0,
        0.0,
    ).astype(BF16)
    count = dot(jnp.concatenate(as_num, axis=0).astype(BF16), before, 1, 0)
    total = jnp.sum(as_num[0], axis=1, keepdims=True)
    place = [count[:number_of], count[number_of:] + total]
    slot = [
        jnp.sum(jnp.where(h, p, 0.0), axis=0, keepdims=True).astype(jnp.int32)
        for h, p in zip(hot, place)
    ]
    return hot, slot


def picks_of(pieces, slot, number_of, pad):
    index = lax.broadcasted_iota(jnp.int32, (number_of * pad, pieces.shape[1]), 0)
    return [index == pieces[k : k + 1, :] * pad + slot[k] for k in range(2)]


def slots_kernel(pad, chips, twice, routes_hbm, gates_hbm, tok_hbm, cot_hbm, *refs):
    order = [*range(chips), *twice]
    out_refs, refs = refs[: len(order)], refs[len(order) :]
    routes_ref, gates_ref, tok_ref, cot_ref, sems = refs
    pairs = [
        (routes_hbm, routes_ref),
        (gates_hbm, gates_ref),
        (tok_hbm, tok_ref),
        (cot_hbm, cot_ref),
    ]
    copies = [
        pltpu.make_async_copy(src, dst, sems.at[i]) for i, (src, dst) in enumerate(pairs)
    ]
    for copy in copies:
        copy.start()
    copies[0].wait()
    copies[1].wait()
    pieces = pieces_of(routes_ref[...], chips)
    gates = gates_ref[...].astype(F32)
    _, slot = slots_of(pieces, 2 * chips)
    pick = picks_of(pieces, slot, 2 * chips, pad)
    plain = jnp.where(pick[0] | pick[1], 1.0, 0.0).astype(BF16)
    scaled = (
        jnp.where(pick[0], gates[0:1, :], 0.0) + jnp.where(pick[1], gates[1:2, :], 0.0)
    ).astype(BF16)
    copies[2].wait()
    copies[3].wait()
    rows = dot(plain, tok_ref[...], 1, 0).astype(BF16)
    grads = dot(scaled, cot_ref[...], 1, 0).astype(BF16)
    for k, out_ref in zip(order, out_refs):
        for i in range(2):
            here = slice((2 * k + i) * pad, (2 * k + i + 1) * pad)
            out_ref[2 * i * pad : (2 * i + 1) * pad, :] = rows[here, :]
            out_ref[(2 * i + 1) * pad : (2 * i + 2) * pad, :] = grads[here, :]


def steps_of(size, block):
    half = block // 2
    return [(0, half), (half, half)] + [(at, block) for at in range(block, size, block)]


class Fetch:
    def __init__(self, up_hbm, down_hbm, up_ref, down_ref, sems, base, steps):
        self.pairs = [(up_hbm, up_ref), (down_hbm, down_ref)]
        self.sems, self.base, self.steps = sems, base, steps
        self.copies = []
        self.start()
        self.start()

    def start(self):
        number = len(self.copies)
        if number == len(self.steps):
            return
        at, size = self.steps[number]
        to, of = pl.ds(at, size), pl.ds(pl.multiple_of(self.base + at, size), size)
        self.copies.append([
            pltpu.make_async_copy(src.at[0, of, :], dst.at[to, :], self.sems.at[2 * number + i])
            for i, (src, dst) in enumerate(self.pairs)
        ])
        for copy in self.copies[-1]:
            copy.start()

    def wait(self, number):
        for copy in self.copies[number]:
            copy.wait()
        self.start()


def fetch_kernel(up_hbm, down_hbm, up_ref, down_ref, sems):
    size = up_ref.shape[0]
    for copy in Fetch(up_hbm, down_hbm, up_ref, down_ref, sems, 0, [(0, size)]).copies[0]:
        copy.wait()


def join_kernel(size, lists, *refs):
    out_refs = refs[len(refs) - len(lists) :]
    for blocks, out_ref in zip(lists, out_refs):
        for i, (number, at) in enumerate(blocks):
            out_ref[i * size : (i + 1) * size, :] = refs[number][at : at + size, :]


def gather_rows(pad, blocks, rows_ref, grads_ref):
    for i, (ref, at) in enumerate(blocks):
        here = slice(i * pad, (i + 1) * pad)
        rows_ref[here, :] = ref[at : at + pad, :]
        grads_ref[here, :] = ref[at + pad : at + 2 * pad, :]


def backward(cap, pad, block, blocks, up_ref, down_ref, scratch, put):
    rows_ref, grads_ref, grad_acc, gate_acc = scratch
    gather_rows(pad, blocks, rows_ref, grads_ref)
    slots = rows_ref.shape[0]
    for step in range(up_ref.shape[0] // block):
        part = pl.ds(step * block, block)
        up = up_ref[part, :]
        active, slope = silu_parts(dot(rows_ref[...], up, 1, 1))
        back = dot(grads_ref[...], down_ref[part, :], 1, 1)
        hid_grad = (back * slope).astype(BF16)
        gate = active.astype(BF16).astype(F32) * back
        gate = sum(gate[:, i : i + 128] for i in range(0, block, 128))
        in_grad = dot(hid_grad, up, 1, 0)
        if step == 0:
            grad_acc[...] = in_grad
            gate_acc[...] = gate
        else:
            grad_acc[...] += in_grad
            gate_acc[...] += gate
    gate = jnp.sum(gate_acc[...], axis=1, keepdims=True)
    spot = lax.broadcasted_iota(jnp.int32, (slots, 128), 0) % pad
    lane = lax.broadcasted_iota(jnp.int32, (slots, 128), 1)
    gate = jnp.where(spot == lane, gate, 0.0).reshape(len(blocks), pad, 128)
    gate = jnp.sum(gate, axis=1, keepdims=True)
    line = lax.broadcasted_iota(jnp.int32, (pad, 128), 0)
    for k in range(len(blocks)):
        here = slice(k * pad, (k + 1) * pad)
        first = jnp.where(line == cap, gate[k], grad_acc[here, 0:128])
        put(k, first.astype(BF16), grad_acc[here, 128:].astype(BF16))


def blocks_of(pad, refs):
    return [(ref, at) for ref in refs for at in range(0, ref.shape[0], 2 * pad)]


def direct_back_kernel(cap, pad, block, chips, *refs):
    pieces, (up_ref, down_ref, out_ref, *scratch) = refs[:chips], refs[chips:]

    def put(k, first, rest):
        out_ref[k, :, 0:128] = first
        out_ref[k, :, 128:] = rest

    blocks = [(ref, 0) for ref in pieces]
    backward(cap, pad, block, blocks, up_ref, down_ref, scratch, put)


def sibling_back_kernel(cap, pad, block, order, *refs):
    sibling_ref, direct_ref, up_ref, down_ref, out_hbm, mine_ref, sems, *scratch = refs
    copies = []

    def send(i, core):
        ref = mine_ref if core else direct_ref
        to = out_hbm.at[origin_of(order[i], core, len(order))]
        copies.append(pltpu.make_async_copy(ref.at[i], to, sems.at[2 * i + core]))
        copies[-1].start()

    for i in range(len(order)):
        send(i, 0)

    def put(k, first, rest):
        mine_ref[k, :, 0:128] = first
        mine_ref[k, :, 128:] = rest
        send(k, 1)

    blocks = blocks_of(pad, [sibling_ref])
    backward(cap, pad, block, blocks, up_ref, down_ref, scratch, put)
    for copy in copies:
        copy.wait()


def weights_kernel(pad, block, share, number, places, begun, ended, *refs):
    refs = list(refs)
    take = lambda number: [refs.pop(0) for _ in range(number)]
    row_refs, weights = take(number), take(2)
    sums = take(2) if begun else None
    notes = None if begun else take(2)
    outs = take(2)
    notes_out = None if begun else take(3)
    rows_ref, grads_ref, up_ref, down_ref, sems, *kept = refs
    steps = steps_of(share, block)
    fetch = Fetch(*weights, up_ref, down_ref, sems, lax.axis_index("rep") * share, steps)
    gather_rows(pad, [(row_refs[i], at) for i, at in places], rows_ref, grads_ref)
    copies = []
    for step, (at, size) in enumerate(steps):
        here = pl.ds(at, size)
        fetch.wait(step)
        active, slope = silu_parts(dot(up_ref[here, :], rows_ref[...], 1, 1))
        back = dot(down_ref[here, :], grads_ref[...], 1, 1)
        hid_grad = (back * slope).astype(BF16)
        parts = [dot(hid_grad, rows_ref[...], 1, 0), dot(active.astype(BF16), grads_ref[...], 1, 0)]
        for i, part in enumerate(parts):
            if begun:
                part += sums[i][0, here, :]
            if not ended:
                outs[i][0, here, :] = part
                continue
            kept[i][here, :] = part.astype(BF16)
            sem = kept[2].at[2 * step + i]
            copies.append(pltpu.make_async_copy(kept[i].at[here, :], outs[i].at[0, here, :], sem))
            copies[-1].start()
    if not begun:
        note_routes(pad, *notes, *notes_out)
    for copy in copies:
        copy.wait()


def note_routes(pad, routes_ref, gates_ref, pick_ref, hot_ref, spot_ref):
    routes = routes_ref[...]
    gates = gates_ref[...].astype(F32)
    groups = pick_ref.shape[0] // pad
    hot, slot = slots_of(routes, groups)
    pick = picks_of(routes, slot, groups, pad)
    pick_ref[...] = jnp.where(pick[0] | pick[1], 1.0, 0.0).astype(BF16)
    lane = lax.broadcasted_iota(jnp.int32, (128, routes.shape[1]), 0)
    for k in range(2):
        hot_ref[k] = jnp.where(hot[k], 1.0 / gates[k : k + 1, :], 0.0)
        spot_ref[k] = jnp.where(lane == slot[k], 1.0, 0.0).astype(BF16)


def combine_kernel(cap, pick_ref, hot_ref, spot_ref, back_ref, d_tok_ref, d_gate_ref):
    groups, pad, feat = back_ref.shape
    back = back_ref[...]
    d_tok_ref[...] = dot(pick_ref[...], back.reshape(groups * pad, feat), 0, 0).astype(BF16)
    values = back[:, cap, 0:128]
    for k in range(2):
        found = dot(values, spot_ref[k], 1, 0) * hot_ref[k]
        d_gate_ref[k : k + 1, :] = jnp.sum(found, axis=0, keepdims=True).astype(BF16)


def local(tokens, gates, routes, cotangent, w_up, w_down):
    rows, feat = tokens.shape
    hidden = w_up.shape[1]
    groups = lax.axis_size("exp")
    mirrors = lax.axis_size("rep")
    chips = groups // 2
    cap = max(2, 3 * rows // groups)
    pad = (cap // 16 + 1) * 16
    slots = chips * pad
    share = hidden // mirrors
    routes_t, gates_t = routes.T, gates.T
    hbm = functools.partial(pltpu.with_memory_space_constraint, memory_space=pltpu.HBM)
    shape = jax.ShapeDtypeStruct
    unit = 2 * slots * feat

    near, far = list(range(1, chips // 2)), list(range(chips // 2, chips))
    order = near[:1] + far + near[1:]
    twice = [0, order[0]] if mirrors > 1 else []
    out = call(
        functools.partial(slots_kernel, pad, chips, twice),
        "slots",
        [shape((4 * pad, feat), BF16)] * (chips + len(twice)),
        [hbm(a) for a in (routes_t, gates_t, tokens, cotangent)],
        [IN_HBM] * 4,
        [
            pltpu.VMEM((2, rows), jnp.int32),
            pltpu.VMEM((2, rows), BF16),
            pltpu.VMEM((rows, feat), BF16),
            pltpu.VMEM((rows, feat), BF16),
            DMA((4,)),
        ],
        4 * unit * rows,
    )
    pieces = [out[0]] + [lax.ppermute(out[k], "exp", hops_to(chips, k)) for k in order]
    swap = [(i, i ^ 1) for i in range(groups)]
    around = [[(i, (i + s) % mirrors) for i in range(mirrors)] for s in range(1, mirrors)]

    def crossed(piece, k, hops):
        moves = hops_to(chips, k) if k else [(i, i) for i in range(groups)]
        pairs = [(m * groups + i, n * groups + j) for m, n in hops for i, j in moves]
        return lax.ppermute(piece, ("rep", "exp"), pairs)

    doubles = list(zip(out[chips:], twice))
    straight = [[crossed(piece, k, hops) for hops in around] for piece, k in doubles]
    arrivals = [*pieces[:2], *sum(straight[:1], []), *pieces[2:], *sum(straight[1:], [])]

    w_up, w_down = hbm(w_up), hbm(w_down)
    up_v, down_v = call(
        fetch_kernel,
        "fetch_weights",
        [shape((hidden, feat), BF16)] * 2,
        [w_up, w_down],
        [IN_HBM] * 2,
        [DMA((2,))],
        0,
        0,
        SMALL,
    )
    whole = 2 * pad

    def join(name, arrays, *lists):
        return call(
            functools.partial(join_kernel, whole, lists),
            name,
            [shape((len(blocks) * whole, feat), BF16) for blocks in lists],
            arrays,
            [IN_VMEM] * len(arrays),
            [],
            0,
            0,
            SMALL,
        )

    def places_in(arrays):
        return [next(i for i, a in enumerate(arrivals) if a is array) for array in arrays]

    own, flat = places_in(pieces), places_in(sum(straight, []))
    (handed,) = join("hand_on", [*arrivals, up_v], [(i, whole) for i in own])
    sibling = lax.ppermute(handed, "exp", swap)
    lists = [[(i, 0) for i in own[2:]], [(i, 0) for i in own[:2] + flat]]
    if flat:
        lists.append([(i, whole) for i in flat])
    arrived, early, *mirrored = join("arrived_rows", [*arrivals, handed], *lists)
    firsts = [lax.ppermute(arrived, "rep", hops) for hops in around]
    later = range(2, chips)
    (passed,) = join("sibling_rows", [sibling], [(0, i * whole) for i in later])
    seconds = [lax.ppermute(passed, "rep", hops) for hops in around]
    seconds += [lax.ppermute(a, "exp", swap) for a in mirrored]

    block = min(512, hidden)
    scratch = [
        pltpu.VMEM((slots, feat), BF16),
        pltpu.VMEM((slots, feat), BF16),
        pltpu.VMEM((slots, feat), F32),
        pltpu.VMEM((slots, 128), F32),
    ]
    results = (chips, pad, feat)
    (direct,) = call(
        functools.partial(direct_back_kernel, cap, pad, block, chips),
        "direct_backward",
        [shape(results, BF16)],
        [*pieces, up_v, down_v],
        [IN_VMEM] * (chips + 2),
        scratch,
        AHEAD,
        slots * hidden,
    )
    back = pl.pallas_call(
        functools.partial(sibling_back_kernel, cap, pad, block, [0, *order]),
        name="sibling_backward",
        out_shape=pltpu.HBM((groups, pad, feat), BF16),
        in_specs=[IN_VMEM] * 4,
        out_specs=IN_HBM,
        scratch_shapes=[pltpu.VMEM(results, BF16), DMA((groups,)), *scratch],
        compiler_params=pltpu.CompilerParams(vmem_limit_bytes=MEDIUM),
        cost_estimate=pl.CostEstimate(
            flops=AHEAD, bytes_accessed=4 * hidden * feat, transcendentals=slots * hidden
        ),
    )(sibling, direct, up_v, down_v)
    back = lax.all_to_all(back, "exp", split_axis=0, concat_axis=0, tiled=True)

    part = min(512, share)

    def weights_call(name, arrays, places, sums, ended, flops):
        begun = bool(sums)
        number = len(places) * pad
        notes = [] if begun else [
            shape((groups * pad, rows), BF16),
            shape((2, groups, rows), F32),
            shape((2, 128, rows), BF16),
        ]
        grad = pltpu.HBM((1, share, feat), BF16) if ended else shape((1, share, feat), F32)
        steps = len(steps_of(share, part))
        scratch = [
            pltpu.VMEM((number, feat), BF16),
            pltpu.VMEM((number, feat), BF16),
            pltpu.VMEM((share, feat), BF16),
            pltpu.VMEM((share, feat), BF16),
            DMA((2 * steps,)),
        ]
        if ended:
            scratch += [pltpu.VMEM((share, feat), BF16)] * 2 + [DMA((2 * steps,))]
        return call(
            functools.partial(
                weights_kernel, pad, part, share, len(arrays), places, begun, ended
            ),
            name,
            [grad] * 2 + notes,
            [*arrays, w_up, w_down, *(sums or [routes_t, gates_t])],
            [IN_VMEM] * len(arrays) + [IN_HBM] * 2 + [IN_VMEM] * 2,
            scratch,
            flops,
            number * share,
            LARGE,
            [IN_HBM if ended else IN_VMEM] * 2 + [IN_VMEM] * len(notes),
        )

    def places_of(arrays, first=0):
        return [
            (first + i, at) for i, a in enumerate(arrays) for at in range(0, a.shape[0], whole)
        ]

    joined = [sibling, arrived, early, *firsts]
    *sums, pick, hot, spot = weights_call(
        "first_weights", joined, places_of(joined), [], not seconds, 0
    )
    if seconds:
        sums = weights_call("last_weights", seconds, places_of(seconds), sums, True, AHEAD)
    grad_up, grad_down = sums

    d_tokens, d_gates = call(
        functools.partial(combine_kernel, cap),
        "combine",
        [shape((rows, feat), BF16), shape((2, rows), BF16)],
        [pick, hot, spot, back],
        [IN_VMEM] * 4,
        [],
        4 * unit * rows,
        0,
        SMALL,
    )
    return d_tokens, d_gates.T, grad_up, grad_down


def solution(mesh):
    by_both = P(("rep", "exp"), None)
    by_expert = P("exp", None, None)
    return jax.shard_map(
        local,
        mesh=mesh,
        in_specs=(by_both, by_both, by_both, by_both, by_expert, by_expert),
        out_specs=(by_both, by_both, P("exp", "rep", None), P("exp", "rep", None)),
        check_vma=False,
    )
```

```python
import functools
import math

import jax
import jax.numpy as jnp
from jax import lax
from jax.experimental import pallas as pl
from jax.experimental.pallas import tpu as pltpu
from jax.sharding import PartitionSpec as P

F32 = jnp.float32
BF16 = jnp.bfloat16
SMALL, MEDIUM, LARGE = 8 << 20, 12 << 20, 24 << 20
AHEAD = 10**11
IN_HBM = pl.BlockSpec(memory_space=pltpu.HBM)
IN_VMEM = pl.BlockSpec(memory_space=pltpu.VMEM)
DMA = pltpu.SemaphoreType.DMA


def dot(left, right, left_dim, right_dim):
    return lax.dot_general(
        left, right, (((left_dim,), (right_dim,)), ((), ())), preferred_element_type=F32
    )


def silu_parts(preact):
    sigma = 0.5 * jnp.tanh(0.5 * preact) + 0.5
    active = preact * sigma
    return active, sigma + active * (1.0 - sigma)


def call(body, name, outs, args, in_specs, scratch, flops, transcendentals=0, limit=MEDIUM, out_specs=None):
    moved = sum(math.prod(a.shape) * a.dtype.itemsize for a in (*args, *outs)) if flops else 0
    return pl.pallas_call(
        body,
        name=name,
        out_shape=outs,
        in_specs=in_specs,
        out_specs=out_specs or [IN_VMEM] * len(outs),
        scratch_shapes=scratch,
        compiler_params=pltpu.CompilerParams(vmem_limit_bytes=limit),
        cost_estimate=pl.CostEstimate(
            flops=flops, bytes_accessed=moved, transcendentals=transcendentals if flops else 0
        ),
    )(*args)


def paired(chips):
    return chips & (chips - 1) == 0


def hops_to(chips, k):
    if paired(chips):
        return [(2 * i + c, 2 * (i ^ k) + c) for i in range(chips) for c in range(2)]
    return [(2 * i + c, 2 * ((i + k) % chips) + c) for i in range(chips) for c in range(2)]


def pieces_of(experts, chips):
    me = lax.axis_index("exp")
    if paired(chips):
        return experts ^ me
    chip = (experts // 2 - me // 2 + chips) % chips
    return 2 * chip + (experts + me) % 2


def origin_of(k, core, chips):
    me = lax.axis_index("exp")
    if paired(chips):
        return me ^ (2 * k + core)
    return 2 * ((me // 2 - k + chips) % chips) + (me + core) % 2


def slots_of(pieces, number_of):
    rows = pieces.shape[1]
    number = lax.broadcasted_iota(jnp.int32, (number_of, rows), 0)
    hot = [number == pieces[k : k + 1, :] for k in range(2)]
    as_num = [jnp.where(h, 1.0, 0.0).astype(F32) for h in hot]
    before = jnp.where(
        lax.broadcasted_iota(jnp.int32, (rows, rows), 0)
        < lax.broadcasted_iota(jnp.int32, (rows, rows), 1),
        1.0,
        0.0,
    ).astype(BF16)
    count = dot(jnp.concatenate(as_num, axis=0).astype(BF16), before, 1, 0)
    total = jnp.sum(as_num[0], axis=1, keepdims=True)
    place = [count[:number_of], count[number_of:] + total]
    slot = [
        jnp.sum(jnp.where(h, p, 0.0), axis=0, keepdims=True).astype(jnp.int32)
        for h, p in zip(hot, place)
    ]
    return hot, slot


def picks_of(pieces, slot, number_of, pad):
    index = lax.broadcasted_iota(jnp.int32, (number_of * pad, pieces.shape[1]), 0)
    return [index == pieces[k : k + 1, :] * pad + slot[k] for k in range(2)]


def slots_kernel(pad, chips, twice, routes_hbm, gates_hbm, tok_hbm, cot_hbm, *refs):
    order = [*range(chips), *twice]
    out_refs, refs = refs[: len(order)], refs[len(order) :]
    routes_ref, gates_ref, tok_ref, cot_ref, sems = refs
    pairs = [
        (routes_hbm, routes_ref),
        (gates_hbm, gates_ref),
        (tok_hbm, tok_ref),
        (cot_hbm, cot_ref),
    ]
    copies = [
        pltpu.make_async_copy(src, dst, sems.at[i]) for i, (src, dst) in enumerate(pairs)
    ]
    for copy in copies:
        copy.start()
    copies[0].wait()
    copies[1].wait()
    pieces = pieces_of(routes_ref[...], chips)
    gates = gates_ref[...].astype(F32)
    _, slot = slots_of(pieces, 2 * chips)
    pick = picks_of(pieces, slot, 2 * chips, pad)
    plain = jnp.where(pick[0] | pick[1], 1.0, 0.0).astype(BF16)
    scaled = (
        jnp.where(pick[0], gates[0:1, :], 0.0) + jnp.where(pick[1], gates[1:2, :], 0.0)
    ).astype(BF16)
    copies[2].wait()
    copies[3].wait()
    rows = dot(plain, tok_ref[...], 1, 0).astype(BF16)
    grads = dot(scaled, cot_ref[...], 1, 0).astype(BF16)
    for k, out_ref in zip(order, out_refs):
        for i in range(2):
            here = slice((2 * k + i) * pad, (2 * k + i + 1) * pad)
            out_ref[2 * i * pad : (2 * i + 1) * pad, :] = rows[here, :]
            out_ref[(2 * i + 1) * pad : (2 * i + 2) * pad, :] = grads[here, :]


def steps_of(size, block):
    half = block // 2
    return [(0, half), (half, half)] + [(at, block) for at in range(block, size, block)]


class Fetch:
    def __init__(self, up_hbm, down_hbm, up_ref, down_ref, sems, base, steps):
        self.pairs = [(up_hbm, up_ref), (down_hbm, down_ref)]
        self.sems, self.base, self.steps = sems, base, steps
        self.copies = []
        self.start()
        self.start()

    def start(self):
        number = len(self.copies)
        if number == len(self.steps):
            return
        at, size = self.steps[number]
        to, of = pl.ds(at, size), pl.ds(pl.multiple_of(self.base + at, size), size)
        self.copies.append([
            pltpu.make_async_copy(src.at[0, of, :], dst.at[to, :], self.sems.at[2 * number + i])
            for i, (src, dst) in enumerate(self.pairs)
        ])
        for copy in self.copies[-1]:
            copy.start()

    def wait(self, number):
        for copy in self.copies[number]:
            copy.wait()
        self.start()


def fetch_kernel(up_hbm, down_hbm, up_ref, down_ref, sems):
    size = up_ref.shape[0]
    for copy in Fetch(up_hbm, down_hbm, up_ref, down_ref, sems, 0, [(0, size)]).copies[0]:
        copy.wait()


def join_kernel(size, lists, *refs):
    out_refs = refs[len(refs) - len(lists) :]
    for blocks, out_ref in zip(lists, out_refs):
        for i, (number, at) in enumerate(blocks):
            out_ref[i * size : (i + 1) * size, :] = refs[number][at : at + size, :]


def gather_rows(pad, blocks, rows_ref, grads_ref):
    for i, (ref, at) in enumerate(blocks):
        here = slice(i * pad, (i + 1) * pad)
        rows_ref[here, :] = ref[at : at + pad, :]
        grads_ref[here, :] = ref[at + pad : at + 2 * pad, :]


def backward(cap, pad, block, blocks, up_ref, down_ref, scratch, put):
    rows_ref, grads_ref, grad_acc, gate_acc = scratch
    gather_rows(pad, blocks, rows_ref, grads_ref)
    slots = rows_ref.shape[0]
    for step in range(up_ref.shape[0] // block):
        part = pl.ds(step * block, block)
        up = up_ref[part, :]
        active, slope = silu_parts(dot(rows_ref[...], up, 1, 1))
        back = dot(grads_ref[...], down_ref[part, :], 1, 1)
        hid_grad = (back * slope).astype(BF16)
        gate = active.astype(BF16).astype(F32) * back
        gate = sum(gate[:, i : i + 128] for i in range(0, block, 128))
        in_grad = dot(hid_grad, up, 1, 0)
        if step == 0:
            grad_acc[...] = in_grad
            gate_acc[...] = gate
        else:
            grad_acc[...] += in_grad
            gate_acc[...] += gate
    gate = jnp.sum(gate_acc[...], axis=1, keepdims=True)
    spot = lax.broadcasted_iota(jnp.int32, (slots, 128), 0) % pad
    lane = lax.broadcasted_iota(jnp.int32, (slots, 128), 1)
    gate = jnp.where(spot == lane, gate, 0.0).reshape(len(blocks), pad, 128)
    gate = jnp.sum(gate, axis=1, keepdims=True)
    line = lax.broadcasted_iota(jnp.int32, (pad, 128), 0)
    for k in range(len(blocks)):
        here = slice(k * pad, (k + 1) * pad)
        first = jnp.where(line == cap, gate[k], grad_acc[here, 0:128])
        put(k, first.astype(BF16), grad_acc[here, 128:].astype(BF16))


def blocks_of(pad, refs):
    return [(ref, at) for ref in refs for at in range(0, ref.shape[0], 2 * pad)]


def direct_back_kernel(cap, pad, block, chips, *refs):
    pieces, (up_ref, down_ref, out_ref, *scratch) = refs[:chips], refs[chips:]

    def put(k, first, rest):
        out_ref[k, :, 0:128] = first
        out_ref[k, :, 128:] = rest

    blocks = [(ref, 0) for ref in pieces]
    backward(cap, pad, block, blocks, up_ref, down_ref, scratch, put)


def sibling_back_kernel(cap, pad, block, order, *refs):
    sibling_ref, direct_ref, up_ref, down_ref, out_hbm, mine_ref, sems, *scratch = refs
    copies = []

    def send(i, core):
        ref = mine_ref if core else direct_ref
        to = out_hbm.at[origin_of(order[i], core, len(order))]
        copies.append(pltpu.make_async_copy(ref.at[i], to, sems.at[2 * i + core]))
        copies[-1].start()

    for i in range(len(order)):
        send(i, 0)

    def put(k, first, rest):
        mine_ref[k, :, 0:128] = first
        mine_ref[k, :, 128:] = rest
        send(k, 1)

    blocks = blocks_of(pad, [sibling_ref])
    backward(cap, pad, block, blocks, up_ref, down_ref, scratch, put)
    for copy in copies:
        copy.wait()


def weights_kernel(pad, block, share, number, places, begun, ended, *refs):
    refs = list(refs)
    take = lambda number: [refs.pop(0) for _ in range(number)]
    row_refs, weights = take(number), take(2)
    sums = take(2) if begun else None
    notes = None if begun else take(2)
    outs = take(2)
    notes_out = None if begun else take(3)
    rows_ref, grads_ref, up_ref, down_ref, sems, *kept = refs
    steps = steps_of(share, block)
    fetch = Fetch(*weights, up_ref, down_ref, sems, lax.axis_index("rep") * share, steps)
    gather_rows(pad, [(row_refs[i], at) for i, at in places], rows_ref, grads_ref)
    copies = []
    for step, (at, size) in enumerate(steps):
        here = pl.ds(at, size)
        fetch.wait(step)
        active, slope = silu_parts(dot(up_ref[here, :], rows_ref[...], 1, 1))
        back = dot(down_ref[here, :], grads_ref[...], 1, 1)
        hid_grad = (back * slope).astype(BF16)
        parts = [dot(hid_grad, rows_ref[...], 1, 0), dot(active.astype(BF16), grads_ref[...], 1, 0)]
        for i, part in enumerate(parts):
            if begun:
                part += sums[i][0, here, :]
            if not ended:
                outs[i][0, here, :] = part
                continue
            kept[i][here, :] = part.astype(BF16)
            sem = kept[2].at[2 * step + i]
            copies.append(pltpu.make_async_copy(kept[i].at[here, :], outs[i].at[0, here, :], sem))
            copies[-1].start()
    if not begun:
        note_routes(pad, *notes, *notes_out)
    for copy in copies:
        copy.wait()


def note_routes(pad, routes_ref, gates_ref, pick_ref, hot_ref, spot_ref):
    routes = routes_ref[...]
    gates = gates_ref[...].astype(F32)
    groups = pick_ref.shape[0] // pad
    hot, slot = slots_of(routes, groups)
    pick = picks_of(routes, slot, groups, pad)
    pick_ref[...] = jnp.where(pick[0] | pick[1], 1.0, 0.0).astype(BF16)
    lane = lax.broadcasted_iota(jnp.int32, (128, routes.shape[1]), 0)
    for k in range(2):
        hot_ref[k] = jnp.where(hot[k], 1.0 / gates[k : k + 1, :], 0.0)
        spot_ref[k] = jnp.where(lane == slot[k], 1.0, 0.0).astype(BF16)


def combine_kernel(cap, pick_ref, hot_ref, spot_ref, back_ref, d_tok_ref, d_gate_ref):
    groups, pad, feat = back_ref.shape
    back = back_ref[...]
    d_tok_ref[...] = dot(pick_ref[...], back.reshape(groups * pad, feat), 0, 0).astype(BF16)
    values = back[:, cap, 0:128]
    for k in range(2):
        found = dot(values, spot_ref[k], 1, 0) * hot_ref[k]
        d_gate_ref[k : k + 1, :] = jnp.sum(found, axis=0, keepdims=True).astype(BF16)


def local(tokens, gates, routes, cotangent, w_up, w_down):
    rows, feat = tokens.shape
    hidden = w_up.shape[1]
    groups = lax.axis_size("exp")
    mirrors = lax.axis_size("rep")
    chips = groups // 2
    cap = max(2, 3 * rows // groups)
    pad = (cap // 16 + 1) * 16
    slots = chips * pad
    share = hidden // mirrors
    routes_t, gates_t = routes.T, gates.T
    hbm = functools.partial(pltpu.with_memory_space_constraint, memory_space=pltpu.HBM)
    shape = jax.ShapeDtypeStruct
    unit = 2 * slots * feat

    near, far = list(range(1, chips // 2)), list(range(chips // 2, chips))
    order = near[:1] + far + near[1:]
    twice = [0] if mirrors > 1 else []
    out = call(
        functools.partial(slots_kernel, pad, chips, twice),
        "slots",
        [shape((4 * pad, feat), BF16)] * (chips + len(twice)),
        [hbm(a) for a in (routes_t, gates_t, tokens, cotangent)],
        [IN_HBM] * 4,
        [
            pltpu.VMEM((2, rows), jnp.int32),
            pltpu.VMEM((2, rows), BF16),
            pltpu.VMEM((rows, feat), BF16),
            pltpu.VMEM((rows, feat), BF16),
            DMA((4,)),
        ],
        4 * unit * rows,
    )
    pieces = [out[0]] + [lax.ppermute(out[k], "exp", hops_to(chips, k)) for k in order]
    swap = [(i, i ^ 1) for i in range(groups)]
    around = [[(i, (i + s) % mirrors) for i in range(mirrors)] for s in range(1, mirrors)]

    def crossed(piece, k, hops):
        moves = hops_to(chips, k) if k else [(i, i) for i in range(groups)]
        pairs = [(m * groups + i, n * groups + j) for m, n in hops for i, j in moves]
        return lax.ppermute(piece, ("rep", "exp"), pairs)

    doubles = list(zip(out[chips:], twice))
    straight = [[crossed(piece, k, hops) for hops in around] for piece, k in doubles]
    arrivals = [*pieces, *sum(straight, [])]

    w_up, w_down = hbm(w_up), hbm(w_down)
    up_v, down_v = call(
        fetch_kernel,
        "fetch_weights",
        [shape((hidden, feat), BF16)] * 2,
        [w_up, w_down],
        [IN_HBM] * 2,
        [DMA((2,))],
        0,
        0,
        SMALL,
    )
    whole = 2 * pad

    def join(name, arrays, *lists):
        return call(
            functools.partial(join_kernel, whole, lists),
            name,
            [shape((len(blocks) * whole, feat), BF16) for blocks in lists],
            arrays,
            [IN_VMEM] * len(arrays),
            [],
            0,
            0,
            SMALL,
        )

    def places_in(arrays):
        return [next(i for i, a in enumerate(arrivals) if a is array) for array in arrays]

    own, flat = places_in(pieces), places_in(sum(straight, []))
    (handed,) = join("hand_on", [*arrivals, up_v], [(i, whole) for i in own])
    sibling = lax.ppermute(handed, "exp", swap)
    lists = [[(i, 0) for i in own[1:]], [(i, 0) for i in own[:1] + flat]]
    arrived, early = join("arrived_rows", [*arrivals, handed], *lists)
    firsts = [lax.ppermute(arrived, "rep", hops) for hops in around]
    later = range(1, chips)
    (passed,) = join("sibling_rows", [sibling], [(0, i * whole) for i in later])
    seconds = [lax.ppermute(passed, "rep", hops) for hops in around]

    block = min(512, hidden)
    scratch = [
        pltpu.VMEM((slots, feat), BF16),
        pltpu.VMEM((slots, feat), BF16),
        pltpu.VMEM((slots, feat), F32),
        pltpu.VMEM((slots, 128), F32),
    ]
    results = (chips, pad, feat)
    (direct,) = call(
        functools.partial(direct_back_kernel, cap, pad, block, chips),
        "direct_backward",
        [shape(results, BF16)],
        [*pieces, up_v, down_v],
        [IN_VMEM] * (chips + 2),
        scratch,
        AHEAD,
        slots * hidden,
    )
    back = pl.pallas_call(
        functools.partial(sibling_back_kernel, cap, pad, block, [0, *order]),
        name="sibling_backward",
        out_shape=pltpu.HBM((groups, pad, feat), BF16),
        in_specs=[IN_VMEM] * 4,
        out_specs=IN_HBM,
        scratch_shapes=[pltpu.VMEM(results, BF16), DMA((groups,)), *scratch],
        compiler_params=pltpu.CompilerParams(vmem_limit_bytes=MEDIUM),
        cost_estimate=pl.CostEstimate(
            flops=AHEAD, bytes_accessed=4 * hidden * feat, transcendentals=slots * hidden
        ),
    )(sibling, direct, up_v, down_v)
    back = lax.all_to_all(back, "exp", split_axis=0, concat_axis=0, tiled=True)

    if flat:
        crossers = sum(straight, [])
        blocks = [(i, whole) for i in range(len(crossers))]
        (mirrored,) = join("hand_on_mirror", [*crossers, direct], blocks)
        seconds.append(lax.ppermute(mirrored, "exp", swap))

    part = min(512, share)

    def weights_call(name, arrays, places, sums, ended, flops):
        begun = bool(sums)
        number = len(places) * pad
        notes = [] if begun else [
            shape((groups * pad, rows), BF16),
            shape((2, groups, rows), F32),
            shape((2, 128, rows), BF16),
        ]
        grad = pltpu.HBM((1, share, feat), BF16) if ended else shape((1, share, feat), F32)
        steps = len(steps_of(share, part))
        scratch = [
            pltpu.VMEM((number, feat), BF16),
            pltpu.VMEM((number, feat), BF16),
            pltpu.VMEM((share, feat), BF16),
            pltpu.VMEM((share, feat), BF16),
            DMA((2 * steps,)),
        ]
        if ended:
            scratch += [pltpu.VMEM((share, feat), BF16)] * 2 + [DMA((2 * steps,))]
        return call(
            functools.partial(
                weights_kernel, pad, part, share, len(arrays), places, begun, ended
            ),
            name,
            [grad] * 2 + notes,
            [*arrays, w_up, w_down, *(sums or [routes_t, gates_t])],
            [IN_VMEM] * len(arrays) + [IN_HBM] * 2 + [IN_VMEM] * 2,
            scratch,
            flops,
            number * share,
            LARGE,
            [IN_HBM if ended else IN_VMEM] * 2 + [IN_VMEM] * len(notes),
        )

    def places_of(arrays, first=0):
        return [
            (first + i, at) for i, a in enumerate(arrays) for at in range(0, a.shape[0], whole)
        ]

    joined = [sibling, arrived, early, *firsts]
    *sums, pick, hot, spot = weights_call(
        "first_weights", joined, places_of(joined), [], not seconds, 0
    )
    if seconds:
        sums = weights_call("last_weights", seconds, places_of(seconds), sums, True, AHEAD)
    grad_up, grad_down = sums

    d_tokens, d_gates = call(
        functools.partial(combine_kernel, cap),
        "combine",
        [shape((rows, feat), BF16), shape((2, rows), BF16)],
        [pick, hot, spot, back],
        [IN_VMEM] * 4,
        [],
        4 * unit * rows,
        0,
        SMALL,
    )
    return d_tokens, d_gates.T, grad_up, grad_down


def solution(mesh):
    by_both = P(("rep", "exp"), None)
    by_expert = P("exp", None, None)
    return jax.shard_map(
        local,
        mesh=mesh,
        in_specs=(by_both, by_both, by_both, by_both, by_expert, by_expert),
        out_specs=(by_both, by_both, P("exp", "rep", None), P("exp", "rep", None)),
        check_vma=False,
    )
```

```python
import functools
import math

import jax
import jax.numpy as jnp
from jax import lax
from jax.experimental import pallas as pl
from jax.experimental.pallas import tpu as pltpu
from jax.sharding import PartitionSpec as P

F32 = jnp.float32
BF16 = jnp.bfloat16
SMALL, MEDIUM, LARGE = 8 << 20, 12 << 20, 24 << 20
AHEAD = 10**11
IN_HBM = pl.BlockSpec(memory_space=pltpu.HBM)
IN_VMEM = pl.BlockSpec(memory_space=pltpu.VMEM)
ANYWHERE = pl.BlockSpec(memory_space=pl.ANY)
DMA = pltpu.SemaphoreType.DMA


def dot(left, right, left_dim, right_dim):
    return lax.dot_general(
        left, right, (((left_dim,), (right_dim,)), ((), ())), preferred_element_type=F32
    )


def silu_parts(preact):
    sigma = 0.5 * jnp.tanh(0.5 * preact) + 0.5
    active = preact * sigma
    return active, sigma + active * (1.0 - sigma)


def call(body, name, outs, args, in_specs, scratch, flops, transcendentals=0, limit=MEDIUM, out_specs=None):
    moved = sum(math.prod(a.shape) * a.dtype.itemsize for a in (*args, *outs)) if flops else 0
    return pl.pallas_call(
        body,
        name=name,
        out_shape=outs,
        in_specs=in_specs,
        out_specs=out_specs or [IN_VMEM] * len(outs),
        scratch_shapes=scratch,
        compiler_params=pltpu.CompilerParams(vmem_limit_bytes=limit),
        cost_estimate=pl.CostEstimate(
            flops=flops, bytes_accessed=moved, transcendentals=transcendentals if flops else 0
        ),
    )(*args)


def paired(chips):
    return chips & (chips - 1) == 0


def hops_to(chips, k):
    if paired(chips):
        return [(2 * i + c, 2 * (i ^ k) + c) for i in range(chips) for c in range(2)]
    return [(2 * i + c, 2 * ((i + k) % chips) + c) for i in range(chips) for c in range(2)]


def pieces_of(experts, chips):
    me = lax.axis_index("exp")
    if paired(chips):
        return experts ^ me
    chip = (experts // 2 - me // 2 + chips) % chips
    return 2 * chip + (experts + me) % 2


def origin_of(k, core, chips):
    me = lax.axis_index("exp")
    if paired(chips):
        return me ^ (2 * k + core)
    return 2 * ((me // 2 - k + chips) % chips) + (me + core) % 2


def slots_of(pieces, number_of):
    rows = pieces.shape[1]
    number = lax.broadcasted_iota(jnp.int32, (number_of, rows), 0)
    hot = [number == pieces[k : k + 1, :] for k in range(2)]
    as_num = [jnp.where(h, 1.0, 0.0).astype(F32) for h in hot]
    before = jnp.where(
        lax.broadcasted_iota(jnp.int32, (rows, rows), 0)
        < lax.broadcasted_iota(jnp.int32, (rows, rows), 1),
        1.0,
        0.0,
    ).astype(BF16)
    count = dot(jnp.concatenate(as_num, axis=0).astype(BF16), before, 1, 0)
    total = jnp.sum(as_num[0], axis=1, keepdims=True)
    place = [count[:number_of], count[number_of:] + total]
    slot = [
        jnp.sum(jnp.where(h, p, 0.0), axis=0, keepdims=True).astype(jnp.int32)
        for h, p in zip(hot, place)
    ]
    return hot, slot


def picks_of(pieces, slot, number_of, pad):
    index = lax.broadcasted_iota(jnp.int32, (number_of * pad, pieces.shape[1]), 0)
    return [index == pieces[k : k + 1, :] * pad + slot[k] for k in range(2)]


def slots_kernel(pad, chips, twice, routes_hbm, gates_hbm, tok_hbm, cot_hbm, *refs):
    order = [*range(chips), *twice]
    out_refs, refs = refs[: len(order)], refs[len(order) :]
    routes_ref, gates_ref, tok_ref, cot_ref, sems = refs
    pairs = [
        (routes_hbm, routes_ref),
        (gates_hbm, gates_ref),
        (tok_hbm, tok_ref),
        (cot_hbm, cot_ref),
    ]
    copies = [
        pltpu.make_async_copy(src, dst, sems.at[i]) for i, (src, dst) in enumerate(pairs)
    ]
    for copy in copies:
        copy.start()
    copies[0].wait()
    copies[1].wait()
    pieces = pieces_of(routes_ref[...], chips)
    gates = gates_ref[...].astype(F32)
    _, slot = slots_of(pieces, 2 * chips)
    pick = picks_of(pieces, slot, 2 * chips, pad)
    plain = jnp.where(pick[0] | pick[1], 1.0, 0.0).astype(BF16)
    scaled = (
        jnp.where(pick[0], gates[0:1, :], 0.0) + jnp.where(pick[1], gates[1:2, :], 0.0)
    ).astype(BF16)
    copies[2].wait()
    copies[3].wait()
    rows = dot(plain, tok_ref[...], 1, 0).astype(BF16)
    grads = dot(scaled, cot_ref[...], 1, 0).astype(BF16)
    for k, out_ref in zip(order, out_refs):
        for i in range(2):
            here = slice((2 * k + i) * pad, (2 * k + i + 1) * pad)
            out_ref[2 * i * pad : (2 * i + 1) * pad, :] = rows[here, :]
            out_ref[(2 * i + 1) * pad : (2 * i + 2) * pad, :] = grads[here, :]


def steps_of(size, block):
    half = block // 2
    return [(0, half)] + [(at, block) for at in range(half, size - half, block)] + [(size - half, half)]


class Fetch:
    def __init__(self, up_hbm, down_hbm, up_ref, down_ref, sems, base, steps):
        self.pairs = [(up_hbm, up_ref), (down_hbm, down_ref)]
        self.sems, self.base, self.steps = sems, base, steps
        self.copies = []
        self.start()
        self.start()

    def start(self):
        number = len(self.copies)
        if number == len(self.steps):
            return
        at, size = self.steps[number]
        to, of = pl.ds(at, size), pl.ds(pl.multiple_of(self.base + at, size), size)
        self.copies.append([
            pltpu.make_async_copy(src.at[0, of, :], dst.at[to, :], self.sems.at[2 * number + i])
            for i, (src, dst) in enumerate(self.pairs)
        ])
        for copy in self.copies[-1]:
            copy.start()

    def wait(self, number):
        for copy in self.copies[number]:
            copy.wait()
        self.start()


def fetch_kernel(up_hbm, down_hbm, up_ref, down_ref, sems):
    size = up_ref.shape[0]
    for copy in Fetch(up_hbm, down_hbm, up_ref, down_ref, sems, 0, [(0, size)]).copies[0]:
        copy.wait()


def join_kernel(size, lists, *refs):
    out_refs = refs[len(refs) - len(lists) :]
    for blocks, out_ref in zip(lists, out_refs):
        for i, (number, at) in enumerate(blocks):
            out_ref[i * size : (i + 1) * size, :] = refs[number][at : at + size, :]


def gather_rows(pad, blocks, rows_ref, grads_ref):
    for i, (ref, at) in enumerate(blocks):
        here = slice(i * pad, (i + 1) * pad)
        rows_ref[here, :] = ref[at : at + pad, :]
        grads_ref[here, :] = ref[at + pad : at + 2 * pad, :]


def backward(cap, pad, block, blocks, up_ref, down_ref, scratch, put):
    rows_ref, grads_ref, grad_acc, gate_acc = scratch
    gather_rows(pad, blocks, rows_ref, grads_ref)
    slots = rows_ref.shape[0]
    for step in range(up_ref.shape[0] // block):
        part = pl.ds(step * block, block)
        up = up_ref[part, :]
        active, slope = silu_parts(dot(rows_ref[...], up, 1, 1))
        back = dot(grads_ref[...], down_ref[part, :], 1, 1)
        hid_grad = (back * slope).astype(BF16)
        gate = active.astype(BF16).astype(F32) * back
        gate = sum(gate[:, i : i + 128] for i in range(0, block, 128))
        in_grad = dot(hid_grad, up, 1, 0)
        if step == 0:
            grad_acc[...] = in_grad
            gate_acc[...] = gate
        else:
            grad_acc[...] += in_grad
            gate_acc[...] += gate
    gate = jnp.sum(gate_acc[...], axis=1, keepdims=True)
    spot = lax.broadcasted_iota(jnp.int32, (slots, 128), 0) % pad
    lane = lax.broadcasted_iota(jnp.int32, (slots, 128), 1)
    gate = jnp.where(spot == lane, gate, 0.0).reshape(len(blocks), pad, 128)
    gate = jnp.sum(gate, axis=1, keepdims=True)
    line = lax.broadcasted_iota(jnp.int32, (pad, 128), 0)
    for k in range(len(blocks)):
        here = slice(k * pad, (k + 1) * pad)
        first = jnp.where(line == cap, gate[k], grad_acc[here, 0:128])
        put(k, first.astype(BF16), grad_acc[here, 128:].astype(BF16))


def blocks_of(pad, refs):
    return [(ref, at) for ref in refs for at in range(0, ref.shape[0], 2 * pad)]


def direct_back_kernel(cap, pad, block, chips, *refs):
    pieces, (up_ref, down_ref, _, out_ref, *scratch) = refs[:chips], refs[chips:]

    def put(k, first, rest):
        out_ref[k, :, 0:128] = first
        out_ref[k, :, 128:] = rest

    blocks = [(ref, 0) for ref in pieces]
    backward(cap, pad, block, blocks, up_ref, down_ref, scratch, put)


def sibling_back_kernel(cap, pad, block, order, *refs):
    sibling_ref, direct_ref, up_ref, down_ref, out_hbm, mine_ref, sems, *scratch = refs
    copies = []

    def send(i, core):
        ref = mine_ref if core else direct_ref
        to = out_hbm.at[origin_of(order[i], core, len(order))]
        copies.append(pltpu.make_async_copy(ref.at[i], to, sems.at[2 * i + core]))
        copies[-1].start()

    for i in range(len(order)):
        send(i, 0)

    def put(k, first, rest):
        mine_ref[k, :, 0:128] = first
        mine_ref[k, :, 128:] = rest
        send(k, 1)

    blocks = blocks_of(pad, [sibling_ref])
    backward(cap, pad, block, blocks, up_ref, down_ref, scratch, put)
    for copy in copies:
        copy.wait()


def weights_kernel(pad, block, share, number, places, begun, ended, *refs):
    refs = list(refs)
    take = lambda number: [refs.pop(0) for _ in range(number)]
    row_refs, weights = take(number), take(2)
    sums = take(2) if begun else None
    notes = None if begun else take(2)
    take(1)
    outs = take(2)
    notes_out = None if begun else take(3)
    up_ref, down_ref = weights if begun else take(2)
    rows_ref, grads_ref, sems, *kept = refs
    steps = steps_of(share, block)
    if not begun:
        fetch = Fetch(*weights, up_ref, down_ref, sems, lax.axis_index("rep") * share, steps)
    gather_rows(pad, [(row_refs[i], at) for i, at in places], rows_ref, grads_ref)
    copies = []
    for step, (at, size) in enumerate(steps):
        here = pl.ds(at, size)
        if not begun:
            fetch.wait(step)
        active, slope = silu_parts(dot(up_ref[here, :], rows_ref[...], 1, 1))
        back = dot(down_ref[here, :], grads_ref[...], 1, 1)
        hid_grad = (back * slope).astype(BF16)
        parts = [dot(hid_grad, rows_ref[...], 1, 0), dot(active.astype(BF16), grads_ref[...], 1, 0)]
        for i, part in enumerate(parts):
            if begun:
                part += sums[i][0, here, :]
            if not ended:
                outs[i][0, here, :] = part
                continue
            kept[i][here, :] = part.astype(BF16)
            sem = kept[2].at[2 * step + i]
            copies.append(pltpu.make_async_copy(kept[i].at[here, :], outs[i].at[0, here, :], sem))
            copies[-1].start()
    if not begun:
        note_routes(pad, *notes, *notes_out)
    for copy in copies:
        copy.wait()


def note_routes(pad, routes_ref, gates_ref, pick_ref, hot_ref, spot_ref):
    routes = routes_ref[...]
    gates = gates_ref[...].astype(F32)
    groups = pick_ref.shape[0] // pad
    hot, slot = slots_of(routes, groups)
    pick = picks_of(routes, slot, groups, pad)
    pick_ref[...] = jnp.where(pick[0] | pick[1], 1.0, 0.0).astype(BF16)
    lane = lax.broadcasted_iota(jnp.int32, (128, routes.shape[1]), 0)
    for k in range(2):
        hot_ref[k] = jnp.where(hot[k], 1.0 / gates[k : k + 1, :], 0.0)
        spot_ref[k] = jnp.where(lane == slot[k], 1.0, 0.0).astype(BF16)


def combine_kernel(cap, pick_ref, hot_ref, spot_ref, back_ref, d_tok_ref, d_gate_ref):
    groups, pad, feat = back_ref.shape
    back = back_ref[...]
    d_tok_ref[...] = dot(pick_ref[...], back.reshape(groups * pad, feat), 0, 0).astype(BF16)
    values = back[:, cap, 0:128]
    for k in range(2):
        found = dot(values, spot_ref[k], 1, 0) * hot_ref[k]
        d_gate_ref[k : k + 1, :] = jnp.sum(found, axis=0, keepdims=True).astype(BF16)


def local(tokens, gates, routes, cotangent, w_up, w_down):
    rows, feat = tokens.shape
    hidden = w_up.shape[1]
    groups = lax.axis_size("exp")
    mirrors = lax.axis_size("rep")
    chips = groups // 2
    cap = max(2, 3 * rows // groups)
    pad = (cap // 16 + 1) * 16
    slots = chips * pad
    share = hidden // mirrors
    routes_t, gates_t = routes.T, gates.T
    hbm = functools.partial(pltpu.with_memory_space_constraint, memory_space=pltpu.HBM)
    shape = jax.ShapeDtypeStruct
    unit = 2 * slots * feat

    near, far = list(range(1, chips // 2)), list(range(chips // 2, chips))
    order = far[:2] + near[:1] + far[2:] + near[1:]
    twice = [0] if mirrors > 1 else []
    out = call(
        functools.partial(slots_kernel, pad, chips, twice),
        "slots",
        [shape((4 * pad, feat), BF16)] * (chips + len(twice)),
        [hbm(a) for a in (routes_t, gates_t, tokens, cotangent)],
        [IN_HBM] * 4,
        [
            pltpu.VMEM((2, rows), jnp.int32),
            pltpu.VMEM((2, rows), BF16),
            pltpu.VMEM((rows, feat), BF16),
            pltpu.VMEM((rows, feat), BF16),
            DMA((4,)),
        ],
        4 * unit * rows,
    )
    pieces = [out[0]] + [lax.ppermute(out[k], "exp", hops_to(chips, k)) for k in order]
    swap = [(i, i ^ 1) for i in range(groups)]
    around = [[(i, (i + s) % mirrors) for i in range(mirrors)] for s in range(1, mirrors)]

    def crossed(piece, k, hops):
        moves = hops_to(chips, k) if k else [(i, i) for i in range(groups)]
        pairs = [(m * groups + i, n * groups + j) for m, n in hops for i, j in moves]
        return lax.ppermute(piece, ("rep", "exp"), pairs)

    doubles = list(zip(out[chips:], twice))
    straight = [[crossed(piece, k, hops) for hops in around] for piece, k in doubles]
    arrivals = [*pieces[:2], *sum(straight, []), *pieces[2:]]

    w_up, w_down = hbm(w_up), hbm(w_down)
    up_v, down_v = call(
        fetch_kernel,
        "fetch_weights",
        [shape((hidden, feat), BF16)] * 2,
        [w_up, w_down],
        [IN_HBM] * 2,
        [DMA((2,))],
        0,
        0,
        SMALL,
    )
    whole = 2 * pad

    def join(name, arrays, *lists, after=()):
        return call(
            functools.partial(join_kernel, whole, lists),
            name,
            [shape((len(blocks) * whole, feat), BF16) for blocks in lists],
            [*arrays, *after],
            [IN_VMEM] * len(arrays) + [ANYWHERE] * len(after),
            [],
            0,
            0,
            SMALL,
        )

    def places_in(arrays):
        return [next(i for i, a in enumerate(arrivals) if a is array) for array in arrays]

    own, flat = places_in(pieces), places_in(sum(straight, []))
    (handed,) = join("hand_on", [*arrivals, up_v], [(i, whole) for i in own])
    sibling = lax.ppermute(handed, "exp", swap)
    lists = [[(i, 0) for i in own[1:]], [(i, 0) for i in own[:1] + flat]]
    arrived, early = join("arrived_rows", [*arrivals, handed], *lists)
    firsts = [lax.ppermute(arrived, "rep", hops) for hops in around]
    later = range(1, chips)
    (passed,) = join("sibling_rows", [sibling], [(0, i * whole) for i in later])
    seconds = [lax.ppermute(passed, "rep", hops) for hops in around]

    block = min(512, hidden)
    scratch = [
        pltpu.VMEM((slots, feat), BF16),
        pltpu.VMEM((slots, feat), BF16),
        pltpu.VMEM((slots, feat), F32),
        pltpu.VMEM((slots, 128), F32),
    ]
    results = (chips, pad, feat)
    (direct,) = call(
        functools.partial(direct_back_kernel, cap, pad, block, chips),
        "direct_backward",
        [shape(results, BF16)],
        [*pieces, up_v, down_v, arrived],
        [IN_VMEM] * (chips + 2) + [ANYWHERE],
        scratch,
        AHEAD,
        slots * hidden,
    )
    back = pl.pallas_call(
        functools.partial(sibling_back_kernel, cap, pad, block, [0, *order]),
        name="sibling_backward",
        out_shape=pltpu.HBM((groups, pad, feat), BF16),
        in_specs=[IN_VMEM] * 4,
        out_specs=IN_HBM,
        scratch_shapes=[pltpu.VMEM(results, BF16), DMA((groups,)), *scratch],
        compiler_params=pltpu.CompilerParams(vmem_limit_bytes=MEDIUM),
        cost_estimate=pl.CostEstimate(
            flops=AHEAD, bytes_accessed=4 * hidden * feat, transcendentals=slots * hidden
        ),
    )(sibling, direct, up_v, down_v)
    results_out = hbm(back)
    back = lax.all_to_all(back, "exp", split_axis=0, concat_axis=0, tiled=True)

    part = min(512, share)

    def weights_call(name, arrays, places, weights, sums, ended, flops):
        begun = bool(sums)
        number = len(places) * pad
        notes = [] if begun else [
            shape((groups * pad, rows), BF16),
            shape((2, groups, rows), F32),
            shape((2, 128, rows), BF16),
            shape((share, feat), BF16),
            shape((share, feat), BF16),
        ]
        grad = pltpu.HBM((1, share, feat), BF16) if ended else shape((1, share, feat), F32)
        steps = len(steps_of(share, part))
        scratch = [
            pltpu.VMEM((number, feat), BF16),
            pltpu.VMEM((number, feat), BF16),
            DMA((2 * steps,)),
        ]
        if ended:
            scratch += [pltpu.VMEM((share, feat), BF16)] * 2 + [DMA((2 * steps,))]
        return call(
            functools.partial(
                weights_kernel, pad, part, share, len(arrays), places, begun, ended
            ),
            name,
            [grad] * 2 + notes,
            [*arrays, *weights, *(sums or [routes_t, gates_t]), results_out],
            [IN_VMEM] * len(arrays)
            + [IN_VMEM if begun else IN_HBM] * 2
            + [IN_VMEM] * 2
            + [IN_HBM],
            scratch,
            flops,
            number * share,
            LARGE,
            [IN_HBM if ended else IN_VMEM] * 2 + [IN_VMEM] * len(notes),
        )

    def places_of(arrays, first=0):
        return [
            (first + i, at) for i, a in enumerate(arrays) for at in range(0, a.shape[0], whole)
        ]

    joined = [sibling, arrived, early, *firsts]
    *sums, pick, hot, spot, up_v, down_v = weights_call(
        "first_weights", joined, places_of(joined), [w_up, w_down], [], not seconds, 0
    )
    if flat:
        crossers = sum(straight, [])
        blocks = [(i, whole) for i in range(len(crossers))]
        (mirrored,) = join("hand_on_mirror", crossers, blocks, after=sums[:1])
        seconds.append(lax.ppermute(mirrored, "exp", swap))
    if seconds:
        sums = weights_call(
            "last_weights", seconds, places_of(seconds), [up_v, down_v], sums, True, AHEAD
        )
    grad_up, grad_down = sums

    d_tokens, d_gates = call(
        functools.partial(combine_kernel, cap),
        "combine",
        [shape((rows, feat), BF16), shape((2, rows), BF16)],
        [pick, hot, spot, back],
        [IN_VMEM] * 4,
        [],
        4 * unit * rows,
        0,
        SMALL,
    )
    return d_tokens, d_gates.T, grad_up, grad_down


def solution(mesh):
    by_both = P(("rep", "exp"), None)
    by_expert = P("exp", None, None)
    return jax.shard_map(
        local,
        mesh=mesh,
        in_specs=(by_both, by_both, by_both, by_both, by_expert, by_expert),
        out_specs=(by_both, by_both, P("exp", "rep", None), P("exp", "rep", None)),
        check_vma=False,
    )
```

```python
import functools
import itertools
import math

import jax
import jax.numpy as jnp
from jax import lax
from jax.experimental import pallas as pl
from jax.experimental.pallas import tpu as pltpu
from jax.sharding import PartitionSpec as P

F32 = jnp.float32
BF16 = jnp.bfloat16
SMALL, MEDIUM, LARGE = 8 << 20, 12 << 20, 24 << 20
AHEAD = 10**11
IN_HBM = pl.BlockSpec(memory_space=pltpu.HBM)
IN_VMEM = pl.BlockSpec(memory_space=pltpu.VMEM)
ANYWHERE = pl.BlockSpec(memory_space=pl.ANY)
DMA = pltpu.SemaphoreType.DMA


def dot(left, right, left_dim, right_dim):
    return lax.dot_general(
        left, right, (((left_dim,), (right_dim,)), ((), ())), preferred_element_type=F32
    )


def silu_parts(preact):
    sigma = 0.5 * jnp.tanh(0.5 * preact) + 0.5
    active = preact * sigma
    return active, sigma + active * (1.0 - sigma)


def call(body, name, outs, args, in_specs, scratch, flops, transcendentals=0, limit=MEDIUM, out_specs=None):
    moved = sum(math.prod(a.shape) * a.dtype.itemsize for a in (*args, *outs)) if flops else 0
    return pl.pallas_call(
        body,
        name=name,
        out_shape=outs,
        in_specs=in_specs,
        out_specs=out_specs or [IN_VMEM] * len(outs),
        scratch_shapes=scratch,
        compiler_params=pltpu.CompilerParams(vmem_limit_bytes=limit),
        cost_estimate=pl.CostEstimate(
            flops=flops, bytes_accessed=moved, transcendentals=transcendentals if flops else 0
        ),
    )(*args)


def paired(chips):
    return chips & (chips - 1) == 0


def hops_to(chips, k):
    if paired(chips):
        return [(2 * i + c, 2 * (i ^ k) + c) for i in range(chips) for c in range(2)]
    return [(2 * i + c, 2 * ((i + k) % chips) + c) for i in range(chips) for c in range(2)]


def pieces_of(experts, chips):
    me = lax.axis_index("exp")
    if paired(chips):
        return experts ^ me
    chip = (experts // 2 - me // 2 + chips) % chips
    return 2 * chip + (experts + me) % 2


def origin_of(k, core, chips):
    me = lax.axis_index("exp")
    if paired(chips):
        return me ^ (2 * k + core)
    return 2 * ((me // 2 - k + chips) % chips) + (me + core) % 2


def slots_of(pieces, number_of):
    rows = pieces.shape[1]
    number = lax.broadcasted_iota(jnp.int32, (number_of, rows), 0)
    hot = [number == pieces[k : k + 1, :] for k in range(2)]
    as_num = [jnp.where(h, 1.0, 0.0).astype(F32) for h in hot]
    before = jnp.where(
        lax.broadcasted_iota(jnp.int32, (rows, rows), 0)
        < lax.broadcasted_iota(jnp.int32, (rows, rows), 1),
        1.0,
        0.0,
    ).astype(BF16)
    count = dot(jnp.concatenate(as_num, axis=0).astype(BF16), before, 1, 0)
    total = jnp.sum(as_num[0], axis=1, keepdims=True)
    place = [count[:number_of], count[number_of:] + total]
    slot = [
        jnp.sum(jnp.where(h, p, 0.0), axis=0, keepdims=True).astype(jnp.int32)
        for h, p in zip(hot, place)
    ]
    return hot, slot


def picks_of(pieces, slot, number_of, pad):
    index = lax.broadcasted_iota(jnp.int32, (number_of * pad, pieces.shape[1]), 0)
    return [index == pieces[k : k + 1, :] * pad + slot[k] for k in range(2)]


def slots_kernel(pad, routes_hbm, gates_hbm, tok_hbm, cot_hbm, *refs):
    chips = len(refs) - 5
    out_refs, refs = refs[:chips], refs[chips:]
    routes_ref, gates_ref, tok_ref, cot_ref, sems = refs
    pairs = [
        (routes_hbm, routes_ref),
        (gates_hbm, gates_ref),
        (tok_hbm, tok_ref),
        (cot_hbm, cot_ref),
    ]
    copies = [
        pltpu.make_async_copy(src, dst, sems.at[i]) for i, (src, dst) in enumerate(pairs)
    ]
    for copy in copies:
        copy.start()
    copies[0].wait()
    copies[1].wait()
    pieces = pieces_of(routes_ref[...], chips)
    gates = gates_ref[...].astype(F32)
    _, slot = slots_of(pieces, 2 * chips)
    pick = picks_of(pieces, slot, 2 * chips, pad)
    plain = jnp.where(pick[0] | pick[1], 1.0, 0.0).astype(BF16)
    scaled = (
        jnp.where(pick[0], gates[0:1, :], 0.0) + jnp.where(pick[1], gates[1:2, :], 0.0)
    ).astype(BF16)
    copies[2].wait()
    copies[3].wait()
    rows = dot(plain, tok_ref[...], 1, 0).astype(BF16)
    grads = dot(scaled, cot_ref[...], 1, 0).astype(BF16)
    for k, out_ref in enumerate(out_refs):
        for i in range(2):
            here = slice((2 * k + i) * pad, (2 * k + i + 1) * pad)
            out_ref[2 * i * pad : (2 * i + 1) * pad, :] = rows[here, :]
            out_ref[(2 * i + 1) * pad : (2 * i + 2) * pad, :] = grads[here, :]


def steps_of(size, block):
    half = block // 2
    return [(0, half)] + [(at, block) for at in range(half, size - half, block)] + [(size - half, half)]


class Fetch:
    def __init__(self, up_hbm, down_hbm, up_ref, down_ref, sems, base, steps):
        self.pairs = [(up_hbm, up_ref), (down_hbm, down_ref)]
        self.sems, self.base, self.steps = sems, base, steps
        self.copies = []
        self.start()
        self.start()

    def start(self):
        number = len(self.copies)
        if number == len(self.steps):
            return
        at, size = self.steps[number]
        to, of = pl.ds(at, size), pl.ds(pl.multiple_of(self.base + at, size), size)
        self.copies.append([
            pltpu.make_async_copy(src.at[0, of, :], dst.at[to, :], self.sems.at[2 * number + i])
            for i, (src, dst) in enumerate(self.pairs)
        ])
        for copy in self.copies[-1]:
            copy.start()

    def wait(self, number):
        for copy in self.copies[number]:
            copy.wait()
        self.start()


def fetch_kernel(up_hbm, down_hbm, up_ref, down_ref, sems):
    size = up_ref.shape[0]
    for copy in Fetch(up_hbm, down_hbm, up_ref, down_ref, sems, 0, [(0, size)]).copies[0]:
        copy.wait()


def join_kernel(size, lists, *refs):
    out_refs = refs[len(refs) - len(lists) :]
    for blocks, out_ref in zip(lists, out_refs):
        for i, (number, at) in enumerate(blocks):
            out_ref[i * size : (i + 1) * size, :] = refs[number][at : at + size, :]


def gather_rows(pad, blocks, rows_ref, grads_ref):
    for i, (ref, at) in enumerate(blocks):
        here = slice(i * pad, (i + 1) * pad)
        rows_ref[here, :] = ref[at : at + pad, :]
        grads_ref[here, :] = ref[at + pad : at + 2 * pad, :]


def backward(cap, pad, block, blocks, up_ref, down_ref, scratch, put):
    rows_ref, grads_ref, grad_acc, gate_acc = scratch
    gather_rows(pad, blocks, rows_ref, grads_ref)
    slots = rows_ref.shape[0]
    for step in range(up_ref.shape[0] // block):
        part = pl.ds(step * block, block)
        up = up_ref[part, :]
        active, slope = silu_parts(dot(rows_ref[...], up, 1, 1))
        back = dot(grads_ref[...], down_ref[part, :], 1, 1)
        hid_grad = (back * slope).astype(BF16)
        gate = active.astype(BF16).astype(F32) * back
        gate = sum(gate[:, i : i + 128] for i in range(0, block, 128))
        in_grad = dot(hid_grad, up, 1, 0)
        if step == 0:
            grad_acc[...] = in_grad
            gate_acc[...] = gate
        else:
            grad_acc[...] += in_grad
            gate_acc[...] += gate
    gate = jnp.sum(gate_acc[...], axis=1, keepdims=True)
    spot = lax.broadcasted_iota(jnp.int32, (slots, 128), 0) % pad
    lane = lax.broadcasted_iota(jnp.int32, (slots, 128), 1)
    gate = jnp.where(spot == lane, gate, 0.0).reshape(len(blocks), pad, 128)
    gate = jnp.sum(gate, axis=1, keepdims=True)
    line = lax.broadcasted_iota(jnp.int32, (pad, 128), 0)
    for k in range(len(blocks)):
        here = slice(k * pad, (k + 1) * pad)
        first = jnp.where(line == cap, gate[k], grad_acc[here, 0:128])
        put(k, first.astype(BF16), grad_acc[here, 128:].astype(BF16))


def blocks_of(pad, refs):
    return [(ref, at) for ref in refs for at in range(0, ref.shape[0], 2 * pad)]


def direct_back_kernel(cap, pad, block, chips, *refs):
    pieces, (up_ref, down_ref, _, out_ref, *scratch) = refs[:chips], refs[chips:]

    def put(k, first, rest):
        out_ref[k, :, 0:128] = first
        out_ref[k, :, 128:] = rest

    blocks = [(ref, 0) for ref in pieces]
    backward(cap, pad, block, blocks, up_ref, down_ref, scratch, put)


def sibling_back_kernel(cap, pad, block, order, *refs):
    sibling_ref, direct_ref, up_ref, down_ref, out_hbm, mine_ref, sems, *scratch = refs
    copies = []

    def send(i, core):
        ref = mine_ref if core else direct_ref
        to = out_hbm.at[origin_of(order[i], core, len(order))]
        copies.append(pltpu.make_async_copy(ref.at[i], to, sems.at[2 * i + core]))
        copies[-1].start()

    for i in range(len(order)):
        send(i, 0)

    def put(k, first, rest):
        mine_ref[k, :, 0:128] = first
        mine_ref[k, :, 128:] = rest
        send(k, 1)

    blocks = blocks_of(pad, [sibling_ref])
    backward(cap, pad, block, blocks, up_ref, down_ref, scratch, put)
    for copy in copies:
        copy.wait()


def weights_kernel(pad, block, share, number, places, begun, ended, *refs):
    refs = list(refs)
    take = lambda number: [refs.pop(0) for _ in range(number)]
    row_refs, weights = take(number), take(2)
    sums = take(2) if begun else None
    notes = None if begun else take(2)
    outs = take(2)
    notes_out = None if begun else take(3)
    up_ref, down_ref = weights if begun else take(2)
    rows_ref, grads_ref, sems, *kept = refs
    steps = steps_of(share, block)
    if not begun:
        fetch = Fetch(*weights, up_ref, down_ref, sems, lax.axis_index("rep") * share, steps)
    gather_rows(pad, [(row_refs[i], at) for i, at in places], rows_ref, grads_ref)
    copies = []
    for step, (at, size) in enumerate(steps):
        here = pl.ds(at, size)
        if not begun:
            fetch.wait(step)
        active, slope = silu_parts(dot(up_ref[here, :], rows_ref[...], 1, 1))
        back = dot(down_ref[here, :], grads_ref[...], 1, 1)
        hid_grad = (back * slope).astype(BF16)
        parts = [dot(hid_grad, rows_ref[...], 1, 0), dot(active.astype(BF16), grads_ref[...], 1, 0)]
        for i, part in enumerate(parts):
            if begun:
                part += sums[i][0, here, :]
            if not ended:
                outs[i][0, here, :] = part
                continue
            kept[i][here, :] = part.astype(BF16)
            sem = kept[2].at[2 * step + i]
            copies.append(pltpu.make_async_copy(kept[i].at[here, :], outs[i].at[0, here, :], sem))
            copies[-1].start()
    if not begun:
        note_routes(pad, *notes, *notes_out)
    for copy in copies:
        copy.wait()


def note_routes(pad, routes_ref, gates_ref, pick_ref, hot_ref, spot_ref):
    routes = routes_ref[...]
    gates = gates_ref[...].astype(F32)
    groups = pick_ref.shape[0] // pad
    hot, slot = slots_of(routes, groups)
    pick = picks_of(routes, slot, groups, pad)
    pick_ref[...] = jnp.where(pick[0] | pick[1], 1.0, 0.0).astype(BF16)
    lane = lax.broadcasted_iota(jnp.int32, (128, routes.shape[1]), 0)
    for k in range(2):
        hot_ref[k] = jnp.where(hot[k], 1.0 / gates[k : k + 1, :], 0.0)
        spot_ref[k] = jnp.where(lane == slot[k], 1.0, 0.0).astype(BF16)


def combine_kernel(cap, pick_ref, hot_ref, spot_ref, back_ref, d_tok_ref, d_gate_ref):
    groups, pad, feat = back_ref.shape
    back = back_ref[...]
    d_tok_ref[...] = dot(pick_ref[...], back.reshape(groups * pad, feat), 0, 0).astype(BF16)
    values = back[:, cap, 0:128]
    for k in range(2):
        found = dot(values, spot_ref[k], 1, 0) * hot_ref[k]
        d_gate_ref[k : k + 1, :] = jnp.sum(found, axis=0, keepdims=True).astype(BF16)


def local(tokens, gates, routes, cotangent, w_up, w_down):
    rows, feat = tokens.shape
    hidden = w_up.shape[1]
    groups = lax.axis_size("exp")
    mirrors = lax.axis_size("rep")
    chips = groups // 2
    cap = max(2, 3 * rows // groups)
    pad = (cap // 16 + 1) * 16
    slots = chips * pad
    share = hidden // mirrors
    routes_t, gates_t = routes.T, gates.T
    hbm = functools.partial(pltpu.with_memory_space_constraint, memory_space=pltpu.HBM)
    shape = jax.ShapeDtypeStruct
    unit = 2 * slots * feat

    near, far = list(range(1, chips // 2)), list(range(chips // 2, chips))
    order = [k for pair in itertools.zip_longest(far[:-1], near[:-1]) for k in pair if k is not None]
    order += far[-1:] + near[-1:]
    out = call(
        functools.partial(slots_kernel, pad),
        "slots",
        [shape((4 * pad, feat), BF16)] * chips,
        [hbm(a) for a in (routes_t, gates_t, tokens, cotangent)],
        [IN_HBM] * 4,
        [
            pltpu.VMEM((2, rows), jnp.int32),
            pltpu.VMEM((2, rows), BF16),
            pltpu.VMEM((rows, feat), BF16),
            pltpu.VMEM((rows, feat), BF16),
            DMA((4,)),
        ],
        4 * unit * rows,
    )
    pieces = [out[0]] + [lax.ppermute(out[k], "exp", hops_to(chips, k)) for k in order]
    swap = [(i, i ^ 1) for i in range(groups)]
    around = [[(i, (i + s) % mirrors) for i in range(mirrors)] for s in range(1, mirrors)]

    w_up, w_down = hbm(w_up), hbm(w_down)
    up_v, down_v = call(
        fetch_kernel,
        "fetch_weights",
        [shape((hidden, feat), BF16)] * 2,
        [w_up, w_down],
        [IN_HBM] * 2,
        [DMA((2,))],
        0,
        0,
        SMALL,
    )
    whole = 2 * pad

    def join(name, arrays, *lists):
        return call(
            functools.partial(join_kernel, whole, lists),
            name,
            [shape((len(blocks) * whole, feat), BF16) for blocks in lists],
            arrays,
            [IN_VMEM] * len(arrays),
            [],
            0,
            0,
            SMALL,
        )

    (handed,) = join("hand_on", [*pieces, up_v], [(i, whole) for i in range(chips)])
    sibling = lax.ppermute(handed, "exp", swap)
    (arrived,) = join("arrived_rows", [*pieces, handed], [(i, 0) for i in range(chips)])
    firsts = [lax.ppermute(arrived, "rep", hops) for hops in around]
    seconds = [lax.ppermute(sibling, "rep", hops) for hops in around]

    block = min(512, hidden)
    scratch = [
        pltpu.VMEM((slots, feat), BF16),
        pltpu.VMEM((slots, feat), BF16),
        pltpu.VMEM((slots, feat), F32),
        pltpu.VMEM((slots, 128), F32),
    ]
    results = (chips, pad, feat)
    (direct,) = call(
        functools.partial(direct_back_kernel, cap, pad, block, chips),
        "direct_backward",
        [shape(results, BF16)],
        [*pieces, up_v, down_v, arrived],
        [IN_VMEM] * (chips + 2) + [ANYWHERE],
        scratch,
        AHEAD,
        slots * hidden,
    )
    back = pl.pallas_call(
        functools.partial(sibling_back_kernel, cap, pad, block, [0, *order]),
        name="sibling_backward",
        out_shape=pltpu.HBM((groups, pad, feat), BF16),
        in_specs=[IN_VMEM] * 4,
        out_specs=IN_HBM,
        scratch_shapes=[pltpu.VMEM(results, BF16), DMA((groups,)), *scratch],
        compiler_params=pltpu.CompilerParams(vmem_limit_bytes=MEDIUM),
        cost_estimate=pl.CostEstimate(
            flops=AHEAD, bytes_accessed=4 * hidden * feat, transcendentals=slots * hidden
        ),
    )(sibling, direct, up_v, down_v)
    back = lax.all_to_all(back, "exp", split_axis=0, concat_axis=0, tiled=True)

    part = min(512, share)

    def weights_call(name, arrays, places, weights, sums, ended, flops):
        begun = bool(sums)
        number = len(places) * pad
        notes = [] if begun else [
            shape((groups * pad, rows), BF16),
            shape((2, groups, rows), F32),
            shape((2, 128, rows), BF16),
            shape((share, feat), BF16),
            shape((share, feat), BF16),
        ]
        grad = pltpu.HBM((1, share, feat), BF16) if ended else shape((1, share, feat), F32)
        steps = len(steps_of(share, part))
        scratch = [
            pltpu.VMEM((number, feat), BF16),
            pltpu.VMEM((number, feat), BF16),
            DMA((2 * steps,)),
        ]
        if ended:
            scratch += [pltpu.VMEM((share, feat), BF16)] * 2 + [DMA((2 * steps,))]
        return call(
            functools.partial(
                weights_kernel, pad, part, share, len(arrays), places, begun, ended
            ),
            name,
            [grad] * 2 + notes,
            [*arrays, *weights, *(sums or [routes_t, gates_t])],
            [IN_VMEM] * len(arrays) + [IN_VMEM if begun else IN_HBM] * 2 + [IN_VMEM] * 2,
            scratch,
            flops,
            number * share,
            LARGE,
            [IN_HBM if ended else IN_VMEM] * 2 + [IN_VMEM] * len(notes),
        )

    def places_of(arrays, first=0):
        return [
            (first + i, at) for i, a in enumerate(arrays) for at in range(0, a.shape[0], whole)
        ]

    joined = [sibling, arrived, *firsts]
    *sums, pick, hot, spot, up_v, down_v = weights_call(
        "first_weights", joined, places_of(joined), [w_up, w_down], [], not seconds, 0
    )
    if seconds:
        sums = weights_call(
            "last_weights", seconds, places_of(seconds), [up_v, down_v], sums, True, AHEAD
        )
    grad_up, grad_down = sums

    d_tokens, d_gates = call(
        functools.partial(combine_kernel, cap),
        "combine",
        [shape((rows, feat), BF16), shape((2, rows), BF16)],
        [pick, hot, spot, back],
        [IN_VMEM] * 4,
        [],
        4 * unit * rows,
        0,
        SMALL,
    )
    return d_tokens, d_gates.T, grad_up, grad_down


def solution(mesh):
    by_both = P(("rep", "exp"), None)
    by_expert = P("exp", None, None)
    return jax.shard_map(
        local,
        mesh=mesh,
        in_specs=(by_both, by_both, by_both, by_both, by_expert, by_expert),
        out_specs=(by_both, by_both, P("exp", "rep", None), P("exp", "rep", None)),
        check_vma=False,
    )
```

```python
import functools
import itertools
import math

import jax
import jax.numpy as jnp
from jax import lax
from jax.experimental import pallas as pl
from jax.experimental.pallas import tpu as pltpu
from jax.sharding import PartitionSpec as P

F32 = jnp.float32
BF16 = jnp.bfloat16
SMALL, MEDIUM, LARGE = 8 << 20, 12 << 20, 24 << 20
AHEAD = 10**11
IN_HBM = pl.BlockSpec(memory_space=pltpu.HBM)
IN_VMEM = pl.BlockSpec(memory_space=pltpu.VMEM)
ANYWHERE = pl.BlockSpec(memory_space=pl.ANY)
DMA = pltpu.SemaphoreType.DMA


def dot(left, right, left_dim, right_dim):
    return lax.dot_general(
        left, right, (((left_dim,), (right_dim,)), ((), ())), preferred_element_type=F32
    )


def silu_parts(preact):
    sigma = 0.5 * jnp.tanh(0.5 * preact) + 0.5
    active = preact * sigma
    return active, sigma + active * (1.0 - sigma)


def call(body, name, outs, args, in_specs, scratch, flops, transcendentals=0, limit=MEDIUM, out_specs=None):
    moved = sum(math.prod(a.shape) * a.dtype.itemsize for a in (*args, *outs)) if flops else 0
    return pl.pallas_call(
        body,
        name=name,
        out_shape=outs,
        in_specs=in_specs,
        out_specs=out_specs or [IN_VMEM] * len(outs),
        scratch_shapes=scratch,
        compiler_params=pltpu.CompilerParams(vmem_limit_bytes=limit),
        cost_estimate=pl.CostEstimate(
            flops=flops, bytes_accessed=moved, transcendentals=transcendentals if flops else 0
        ),
    )(*args)


def paired(chips):
    return chips & (chips - 1) == 0


def hops_to(chips, k):
    if paired(chips):
        return [(2 * i + c, 2 * (i ^ k) + c) for i in range(chips) for c in range(2)]
    return [(2 * i + c, 2 * ((i + k) % chips) + c) for i in range(chips) for c in range(2)]


def pieces_of(experts, chips):
    me = lax.axis_index("exp")
    if paired(chips):
        return experts ^ me
    chip = (experts // 2 - me // 2 + chips) % chips
    return 2 * chip + (experts + me) % 2


def origin_of(k, core, chips):
    me = lax.axis_index("exp")
    if paired(chips):
        return me ^ (2 * k + core)
    return 2 * ((me // 2 - k + chips) % chips) + (me + core) % 2


def slots_of(pieces, number_of):
    rows = pieces.shape[1]
    number = lax.broadcasted_iota(jnp.int32, (number_of, rows), 0)
    hot = [number == pieces[k : k + 1, :] for k in range(2)]
    as_num = [jnp.where(h, 1.0, 0.0).astype(F32) for h in hot]
    before = jnp.where(
        lax.broadcasted_iota(jnp.int32, (rows, rows), 0)
        < lax.broadcasted_iota(jnp.int32, (rows, rows), 1),
        1.0,
        0.0,
    ).astype(BF16)
    count = dot(jnp.concatenate(as_num, axis=0).astype(BF16), before, 1, 0)
    total = jnp.sum(as_num[0], axis=1, keepdims=True)
    place = [count[:number_of], count[number_of:] + total]
    slot = [
        jnp.sum(jnp.where(h, p, 0.0), axis=0, keepdims=True).astype(jnp.int32)
        for h, p in zip(hot, place)
    ]
    return hot, slot


def picks_of(pieces, slot, number_of, pad):
    index = lax.broadcasted_iota(jnp.int32, (number_of * pad, pieces.shape[1]), 0)
    return [index == pieces[k : k + 1, :] * pad + slot[k] for k in range(2)]


def slots_kernel(pad, tight, routes_hbm, gates_hbm, tok_hbm, cot_hbm, *refs):
    chips = len(refs) - 5
    out_refs, refs = refs[:chips], refs[chips:]
    routes_ref, gates_ref, tok_ref, cot_ref, sems = refs
    pairs = [
        (routes_hbm, routes_ref),
        (gates_hbm, gates_ref),
        (tok_hbm, tok_ref),
        (cot_hbm, cot_ref),
    ]
    copies = [
        pltpu.make_async_copy(src, dst, sems.at[i]) for i, (src, dst) in enumerate(pairs)
    ]
    for copy in copies:
        copy.start()
    copies[0].wait()
    copies[1].wait()
    pieces = pieces_of(routes_ref[...], chips)
    gates = gates_ref[...].astype(F32)
    _, slot = slots_of(pieces, 2 * chips)
    pick = picks_of(pieces, slot, 2 * chips, pad)
    plain = jnp.where(pick[0] | pick[1], 1.0, 0.0).astype(BF16)
    scaled = (
        jnp.where(pick[0], gates[0:1, :], 0.0) + jnp.where(pick[1], gates[1:2, :], 0.0)
    ).astype(BF16)
    copies[2].wait()
    copies[3].wait()
    rows = dot(plain, tok_ref[...], 1, 0).astype(BF16)
    grads = dot(scaled, cot_ref[...], 1, 0).astype(BF16)
    for k, out_ref in enumerate(out_refs):
        for i in range(2):
            here = slice((2 * k + i) * pad, (2 * k + i) * pad + tight)
            out_ref[2 * i * tight : (2 * i + 1) * tight, :] = rows[here, :]
            out_ref[(2 * i + 1) * tight : (2 * i + 2) * tight, :] = grads[here, :]


def steps_of(size, block):
    half = block // 2
    return [(0, half)] + [(at, block) for at in range(half, size - half, block)] + [(size - half, half)]


class Fetch:
    def __init__(self, up_hbm, down_hbm, up_ref, down_ref, sems, base, steps):
        self.pairs = [(up_hbm, up_ref), (down_hbm, down_ref)]
        self.sems, self.base, self.steps = sems, base, steps
        self.copies = []
        self.start()
        self.start()

    def start(self):
        number = len(self.copies)
        if number == len(self.steps):
            return
        at, size = self.steps[number]
        to, of = pl.ds(at, size), pl.ds(pl.multiple_of(self.base + at, size), size)
        self.copies.append([
            pltpu.make_async_copy(src.at[0, of, :], dst.at[to, :], self.sems.at[2 * number + i])
            for i, (src, dst) in enumerate(self.pairs)
        ])
        for copy in self.copies[-1]:
            copy.start()

    def wait(self, number):
        for copy in self.copies[number]:
            copy.wait()
        self.start()


def fetch_kernel(up_hbm, down_hbm, up_ref, down_ref, sems):
    size = up_ref.shape[0]
    for copy in Fetch(up_hbm, down_hbm, up_ref, down_ref, sems, 0, [(0, size)]).copies[0]:
        copy.wait()


def join_kernel(size, lists, *refs):
    out_refs = refs[len(refs) - len(lists) :]
    for blocks, out_ref in zip(lists, out_refs):
        for i, (number, at) in enumerate(blocks):
            out_ref[i * size : (i + 1) * size, :] = refs[number][at : at + size, :]


def spread_rows(pad, tight, blocks, rows_ref, grads_ref):
    feat = rows_ref.shape[1]
    for i, (ref, row_at, grad_at) in enumerate(blocks):
        for to_ref, at in [(rows_ref, row_at), (grads_ref, grad_at)]:
            to_ref[i * pad : i * pad + tight, :] = ref[at : at + tight, :]
            to_ref[i * pad + tight : (i + 1) * pad, :] = jnp.zeros((pad - tight, feat), BF16)


def backward(cap, pad, tight, block, blocks, up_ref, down_ref, scratch, put):
    rows_ref, grads_ref, grad_acc, gate_acc = scratch
    spread_rows(pad, tight, blocks, rows_ref, grads_ref)
    slots = rows_ref.shape[0]
    for step in range(up_ref.shape[0] // block):
        part = pl.ds(step * block, block)
        up = up_ref[part, :]
        active, slope = silu_parts(dot(rows_ref[...], up, 1, 1))
        back = dot(grads_ref[...], down_ref[part, :], 1, 1)
        hid_grad = (back * slope).astype(BF16)
        gate = active.astype(BF16).astype(F32) * back
        gate = sum(gate[:, i : i + 128] for i in range(0, block, 128))
        in_grad = dot(hid_grad, up, 1, 0)
        if step == 0:
            grad_acc[...] = in_grad
            gate_acc[...] = gate
        else:
            grad_acc[...] += in_grad
            gate_acc[...] += gate
    gate = jnp.sum(gate_acc[...], axis=1, keepdims=True)
    spot = lax.broadcasted_iota(jnp.int32, (slots, 128), 0) % pad
    lane = lax.broadcasted_iota(jnp.int32, (slots, 128), 1)
    gate = jnp.where(spot == lane, gate, 0.0).reshape(len(blocks), pad, 128)
    gate = jnp.sum(gate, axis=1, keepdims=True)
    line = lax.broadcasted_iota(jnp.int32, (pad, 128), 0)
    for k in range(len(blocks)):
        here = slice(k * pad, (k + 1) * pad)
        first = jnp.where(line == cap, gate[k], grad_acc[here, 0:128])
        put(k, first.astype(BF16), grad_acc[here, 128:].astype(BF16))


def direct_back_kernel(cap, pad, tight, block, chips, *refs):
    pieces, (up_ref, down_ref, _, out_ref, *scratch) = refs[:chips], refs[chips:]

    def put(k, first, rest):
        out_ref[k, :, 0:128] = first
        out_ref[k, :, 128:] = rest

    blocks = [(ref, 0, tight) for ref in pieces]
    backward(cap, pad, tight, block, blocks, up_ref, down_ref, scratch, put)


def sibling_back_kernel(cap, pad, tight, block, order, *refs):
    sibling_ref, direct_ref, up_ref, down_ref, out_hbm, mine_ref, sems, *scratch = refs
    copies = []

    def send(i, core):
        ref = mine_ref if core else direct_ref
        to = out_hbm.at[origin_of(order[i], core, len(order))]
        copies.append(pltpu.make_async_copy(ref.at[i], to, sems.at[2 * i + core]))
        copies[-1].start()

    for i in range(len(order)):
        send(i, 0)

    def put(k, first, rest):
        mine_ref[k, :, 0:128] = first
        mine_ref[k, :, 128:] = rest
        send(k, 1)

    chips = len(order)
    blocks = [(sibling_ref, k * tight, (chips + k) * tight) for k in range(chips)]
    backward(cap, pad, tight, block, blocks, up_ref, down_ref, scratch, put)
    for copy in copies:
        copy.wait()


def weights_kernel(pad, block, share, number, begun, ended, *refs):
    refs = list(refs)
    take = lambda number: [refs.pop(0) for _ in range(number)]
    row_refs, weights = take(number), take(2)
    sums = take(2) if begun else None
    notes = None if begun else take(2)
    outs = take(2)
    notes_out = None if begun else take(3)
    up_ref, down_ref = weights if begun else take(2)
    rows_ref, grads_ref, sems, *kept = refs
    steps = steps_of(share, block)
    if not begun:
        fetch = Fetch(*weights, up_ref, down_ref, sems, lax.axis_index("rep") * share, steps)
    for i, ref in enumerate(row_refs):
        size = ref.shape[0] // 2
        rows_ref[i * size : (i + 1) * size, :] = ref[:size, :]
        grads_ref[i * size : (i + 1) * size, :] = ref[size:, :]
    copies = []
    for step, (at, size) in enumerate(steps):
        here = pl.ds(at, size)
        if not begun:
            fetch.wait(step)
        active, slope = silu_parts(dot(up_ref[here, :], rows_ref[...], 1, 1))
        back = dot(down_ref[here, :], grads_ref[...], 1, 1)
        hid_grad = (back * slope).astype(BF16)
        parts = [dot(hid_grad, rows_ref[...], 1, 0), dot(active.astype(BF16), grads_ref[...], 1, 0)]
        for i, part in enumerate(parts):
            if begun:
                part += sums[i][0, here, :]
            if not ended:
                outs[i][0, here, :] = part
                continue
            kept[i][here, :] = part.astype(BF16)
            sem = kept[2].at[2 * step + i]
            copies.append(pltpu.make_async_copy(kept[i].at[here, :], outs[i].at[0, here, :], sem))
            copies[-1].start()
    if not begun:
        note_routes(pad, *notes, *notes_out)
    for copy in copies:
        copy.wait()


def note_routes(pad, routes_ref, gates_ref, pick_ref, hot_ref, spot_ref):
    routes = routes_ref[...]
    gates = gates_ref[...].astype(F32)
    groups = pick_ref.shape[0] // pad
    hot, slot = slots_of(routes, groups)
    pick = picks_of(routes, slot, groups, pad)
    pick_ref[...] = jnp.where(pick[0] | pick[1], 1.0, 0.0).astype(BF16)
    lane = lax.broadcasted_iota(jnp.int32, (128, routes.shape[1]), 0)
    for k in range(2):
        hot_ref[k] = jnp.where(hot[k], 1.0 / gates[k : k + 1, :], 0.0)
        spot_ref[k] = jnp.where(lane == slot[k], 1.0, 0.0).astype(BF16)


def combine_kernel(cap, pick_ref, hot_ref, spot_ref, back_ref, d_tok_ref, d_gate_ref):
    groups, pad, feat = back_ref.shape
    back = back_ref[...]
    d_tok_ref[...] = dot(pick_ref[...], back.reshape(groups * pad, feat), 0, 0).astype(BF16)
    values = back[:, cap, 0:128]
    for k in range(2):
        found = dot(values, spot_ref[k], 1, 0) * hot_ref[k]
        d_gate_ref[k : k + 1, :] = jnp.sum(found, axis=0, keepdims=True).astype(BF16)


def local(tokens, gates, routes, cotangent, w_up, w_down):
    rows, feat = tokens.shape
    hidden = w_up.shape[1]
    groups = lax.axis_size("exp")
    mirrors = lax.axis_size("rep")
    chips = groups // 2
    cap = max(2, 3 * rows // groups)
    pad = (cap // 16 + 1) * 16
    tight = cap + cap % 2
    slots = chips * pad
    share = hidden // mirrors
    routes_t, gates_t = routes.T, gates.T
    hbm = functools.partial(pltpu.with_memory_space_constraint, memory_space=pltpu.HBM)
    shape = jax.ShapeDtypeStruct
    unit = 2 * slots * feat

    near, far = list(range(1, chips // 2)), list(range(chips // 2, chips))
    order = [k for pair in itertools.zip_longest(far[:-1], near[:-1]) for k in pair if k is not None]
    order += far[-1:] + near[-1:]
    out = call(
        functools.partial(slots_kernel, pad, tight),
        "slots",
        [shape((4 * tight, feat), BF16)] * chips,
        [hbm(a) for a in (routes_t, gates_t, tokens, cotangent)],
        [IN_HBM] * 4,
        [
            pltpu.VMEM((2, rows), jnp.int32),
            pltpu.VMEM((2, rows), BF16),
            pltpu.VMEM((rows, feat), BF16),
            pltpu.VMEM((rows, feat), BF16),
            DMA((4,)),
        ],
        4 * unit * rows,
    )
    pieces = [out[0]] + [lax.ppermute(out[k], "exp", hops_to(chips, k)) for k in order]
    swap = [(i, i ^ 1) for i in range(groups)]
    around = [[(i, (i + s) % mirrors) for i in range(mirrors)] for s in range(1, mirrors)]

    w_up, w_down = hbm(w_up), hbm(w_down)
    up_v, down_v = call(
        fetch_kernel,
        "fetch_weights",
        [shape((hidden, feat), BF16)] * 2,
        [w_up, w_down],
        [IN_HBM] * 2,
        [DMA((2,))],
        0,
        0,
        SMALL,
    )
    def join(name, arrays, *lists):
        return call(
            functools.partial(join_kernel, tight, lists),
            name,
            [shape((len(blocks) * tight, feat), BF16) for blocks in lists],
            arrays,
            [IN_VMEM] * len(arrays),
            [],
            0,
            0,
            SMALL,
        )

    (handed,) = join("hand_on", [*pieces, up_v], [(i, at) for at in (2 * tight, 3 * tight) for i in range(chips)])
    sibling = lax.ppermute(handed, "exp", swap)
    (arrived,) = join("arrived_rows", [*pieces, handed], [(i, at) for at in (0, tight) for i in range(chips)])
    firsts = [lax.ppermute(arrived, "rep", hops) for hops in around]
    seconds = [lax.ppermute(sibling, "rep", hops) for hops in around]

    block = min(512, hidden)
    scratch = [
        pltpu.VMEM((slots, feat), BF16),
        pltpu.VMEM((slots, feat), BF16),
        pltpu.VMEM((slots, feat), F32),
        pltpu.VMEM((slots, 128), F32),
    ]
    results = (chips, pad, feat)
    (direct,) = call(
        functools.partial(direct_back_kernel, cap, pad, tight, block, chips),
        "direct_backward",
        [shape(results, BF16)],
        [*pieces, up_v, down_v, arrived],
        [IN_VMEM] * (chips + 2) + [ANYWHERE],
        scratch,
        AHEAD,
        slots * hidden,
    )
    back = pl.pallas_call(
        functools.partial(sibling_back_kernel, cap, pad, tight, block, [0, *order]),
        name="sibling_backward",
        out_shape=pltpu.HBM((groups, pad, feat), BF16),
        in_specs=[IN_VMEM] * 4,
        out_specs=IN_HBM,
        scratch_shapes=[pltpu.VMEM(results, BF16), DMA((groups,)), *scratch],
        compiler_params=pltpu.CompilerParams(vmem_limit_bytes=MEDIUM),
        cost_estimate=pl.CostEstimate(
            flops=AHEAD, bytes_accessed=4 * hidden * feat, transcendentals=slots * hidden
        ),
    )(sibling, direct, up_v, down_v)
    back = lax.all_to_all(back, "exp", split_axis=0, concat_axis=0, tiled=True)

    part = min(512, share)

    def weights_call(name, arrays, weights, sums, ended, flops):
        begun = bool(sums)
        number = len(arrays) * chips * tight
        notes = [] if begun else [
            shape((groups * pad, rows), BF16),
            shape((2, groups, rows), F32),
            shape((2, 128, rows), BF16),
            shape((share, feat), BF16),
            shape((share, feat), BF16),
        ]
        grad = pltpu.HBM((1, share, feat), BF16) if ended else shape((1, share, feat), F32)
        steps = len(steps_of(share, part))
        scratch = [
            pltpu.VMEM((number, feat), BF16),
            pltpu.VMEM((number, feat), BF16),
            DMA((2 * steps,)),
        ]
        if ended:
            scratch += [pltpu.VMEM((share, feat), BF16)] * 2 + [DMA((2 * steps,))]
        return call(
            functools.partial(weights_kernel, pad, part, share, len(arrays), begun, ended),
            name,
            [grad] * 2 + notes,
            [*arrays, *weights, *(sums or [routes_t, gates_t])],
            [IN_VMEM] * len(arrays) + [IN_VMEM if begun else IN_HBM] * 2 + [IN_VMEM] * 2,
            scratch,
            flops,
            number * share,
            LARGE,
            [IN_HBM if ended else IN_VMEM] * 2 + [IN_VMEM] * len(notes),
        )

    joined = [sibling, arrived, *firsts]
    *sums, pick, hot, spot, up_v, down_v = weights_call(
        "first_weights", joined, [w_up, w_down], [], not seconds, 0
    )
    if seconds:
        sums = weights_call(
            "last_weights", seconds, [up_v, down_v], sums, True, AHEAD
        )
    grad_up, grad_down = sums

    d_tokens, d_gates = call(
        functools.partial(combine_kernel, cap),
        "combine",
        [shape((rows, feat), BF16), shape((2, rows), BF16)],
        [pick, hot, spot, back],
        [IN_VMEM] * 4,
        [],
        4 * unit * rows,
        0,
        SMALL,
    )
    return d_tokens, d_gates.T, grad_up, grad_down


def solution(mesh):
    by_both = P(("rep", "exp"), None)
    by_expert = P("exp", None, None)
    return jax.shard_map(
        local,
        mesh=mesh,
        in_specs=(by_both, by_both, by_both, by_both, by_expert, by_expert),
        out_specs=(by_both, by_both, P("exp", "rep", None), P("exp", "rep", None)),
        check_vma=False,
    )
```

```python
import functools
import itertools
import math

import jax
import jax.numpy as jnp
from jax import lax
from jax.experimental import pallas as pl
from jax.experimental.pallas import tpu as pltpu
from jax.sharding import PartitionSpec as P

F32 = jnp.float32
BF16 = jnp.bfloat16
SMALL, MEDIUM, LARGE = 8 << 20, 12 << 20, 24 << 20
AHEAD = 10**11
IN_HBM = pl.BlockSpec(memory_space=pltpu.HBM)
IN_VMEM = pl.BlockSpec(memory_space=pltpu.VMEM)
ANYWHERE = pl.BlockSpec(memory_space=pl.ANY)
DMA = pltpu.SemaphoreType.DMA


def dot(left, right, left_dim, right_dim):
    return lax.dot_general(
        left, right, (((left_dim,), (right_dim,)), ((), ())), preferred_element_type=F32
    )


def silu_parts(preact):
    sigma = 0.5 * jnp.tanh(0.5 * preact) + 0.5
    active = preact * sigma
    return active, sigma + active * (1.0 - sigma)


def call(body, name, outs, args, in_specs, scratch, flops, transcendentals=0, limit=MEDIUM, out_specs=None):
    moved = sum(math.prod(a.shape) * a.dtype.itemsize for a in (*args, *outs)) if flops else 0
    return pl.pallas_call(
        body,
        name=name,
        out_shape=outs,
        in_specs=in_specs,
        out_specs=out_specs or [IN_VMEM] * len(outs),
        scratch_shapes=scratch,
        compiler_params=pltpu.CompilerParams(vmem_limit_bytes=limit),
        cost_estimate=pl.CostEstimate(
            flops=flops, bytes_accessed=moved, transcendentals=transcendentals if flops else 0
        ),
    )(*args)


def paired(chips):
    return chips & (chips - 1) == 0


def hops_to(chips, k):
    if paired(chips):
        return [(2 * i + c, 2 * (i ^ k) + c) for i in range(chips) for c in range(2)]
    return [(2 * i + c, 2 * ((i + k) % chips) + c) for i in range(chips) for c in range(2)]


def pieces_of(experts, chips):
    me = lax.axis_index("exp")
    if paired(chips):
        return experts ^ me
    chip = (experts // 2 - me // 2 + chips) % chips
    return 2 * chip + (experts + me) % 2


def origin_of(k, core, chips):
    me = lax.axis_index("exp")
    if paired(chips):
        return me ^ (2 * k + core)
    return 2 * ((me // 2 - k + chips) % chips) + (me + core) % 2


def slots_of(pieces, number_of):
    rows = pieces.shape[1]
    number = lax.broadcasted_iota(jnp.int32, (number_of, rows), 0)
    hot = [number == pieces[k : k + 1, :] for k in range(2)]
    as_num = [jnp.where(h, 1.0, 0.0).astype(F32) for h in hot]
    before = jnp.where(
        lax.broadcasted_iota(jnp.int32, (rows, rows), 0)
        < lax.broadcasted_iota(jnp.int32, (rows, rows), 1),
        1.0,
        0.0,
    ).astype(BF16)
    count = dot(jnp.concatenate(as_num, axis=0).astype(BF16), before, 1, 0)
    total = jnp.sum(as_num[0], axis=1, keepdims=True)
    place = [count[:number_of], count[number_of:] + total]
    slot = [
        jnp.sum(jnp.where(h, p, 0.0), axis=0, keepdims=True).astype(jnp.int32)
        for h, p in zip(hot, place)
    ]
    return hot, slot


def picks_of(pieces, slot, number_of, pad):
    index = lax.broadcasted_iota(jnp.int32, (number_of * pad, pieces.shape[1]), 0)
    return [index == pieces[k : k + 1, :] * pad + slot[k] for k in range(2)]


def slots_kernel(pad, tight, routes_hbm, gates_hbm, tok_hbm, cot_hbm, *refs):
    chips = len(refs) - 5
    out_refs, refs = refs[:chips], refs[chips:]
    routes_ref, gates_ref, tok_ref, cot_ref, sems = refs
    pairs = [
        (routes_hbm, routes_ref),
        (gates_hbm, gates_ref),
        (tok_hbm, tok_ref),
        (cot_hbm, cot_ref),
    ]
    copies = [
        pltpu.make_async_copy(src, dst, sems.at[i]) for i, (src, dst) in enumerate(pairs)
    ]
    for copy in copies:
        copy.start()
    copies[0].wait()
    copies[1].wait()
    pieces = pieces_of(routes_ref[...], chips)
    gates = gates_ref[...].astype(F32)
    _, slot = slots_of(pieces, 2 * chips)
    pick = picks_of(pieces, slot, 2 * chips, pad)
    plain = jnp.where(pick[0] | pick[1], 1.0, 0.0).astype(BF16)
    scaled = (
        jnp.where(pick[0], gates[0:1, :], 0.0) + jnp.where(pick[1], gates[1:2, :], 0.0)
    ).astype(BF16)
    copies[2].wait()
    copies[3].wait()
    rows = dot(plain, tok_ref[...], 1, 0).astype(BF16)
    grads = dot(scaled, cot_ref[...], 1, 0).astype(BF16)
    for k, out_ref in enumerate(out_refs):
        for i in range(2):
            here = slice((2 * k + i) * pad, (2 * k + i) * pad + tight)
            out_ref[2 * i * tight : (2 * i + 1) * tight, :] = rows[here, :]
            out_ref[(2 * i + 1) * tight : (2 * i + 2) * tight, :] = grads[here, :]


def steps_of(size, block):
    half = block // 2
    return [(0, half)] + [(at, block) for at in range(half, size - half, block)] + [(size - half, half)]


class Fetch:
    def __init__(self, up_hbm, down_hbm, up_ref, down_ref, sems, base, steps):
        self.pairs = [(up_hbm, up_ref), (down_hbm, down_ref)]
        self.sems, self.base, self.steps = sems, base, steps
        self.copies = []
        self.start()
        self.start()

    def start(self):
        number = len(self.copies)
        if number == len(self.steps):
            return
        at, size = self.steps[number]
        to, of = pl.ds(at, size), pl.ds(pl.multiple_of(self.base + at, size), size)
        self.copies.append([
            pltpu.make_async_copy(src.at[0, of, :], dst.at[to, :], self.sems.at[2 * number + i])
            for i, (src, dst) in enumerate(self.pairs)
        ])
        for copy in self.copies[-1]:
            copy.start()

    def wait(self, number):
        for copy in self.copies[number]:
            copy.wait()
        self.start()


def fetch_kernel(up_hbm, down_hbm, up_ref, down_ref, sems):
    size = up_ref.shape[0]
    for copy in Fetch(up_hbm, down_hbm, up_ref, down_ref, sems, 0, [(0, size)]).copies[0]:
        copy.wait()


def join_kernel(size, lists, *refs):
    out_refs = refs[len(refs) - len(lists) :]
    for blocks, out_ref in zip(lists, out_refs):
        for i, (number, at) in enumerate(blocks):
            out_ref[i * size : (i + 1) * size, :] = refs[number][at : at + size, :]


def spread_rows(pad, tight, blocks, rows_ref, grads_ref):
    feat = rows_ref.shape[1]
    for i, (ref, row_at, grad_at) in enumerate(blocks):
        for to_ref, at in [(rows_ref, row_at), (grads_ref, grad_at)]:
            to_ref[i * pad : i * pad + tight, :] = ref[at : at + tight, :]
            to_ref[i * pad + tight : (i + 1) * pad, :] = jnp.zeros((pad - tight, feat), BF16)


def backward(cap, pad, tight, block, blocks, up_ref, down_ref, scratch, put):
    rows_ref, grads_ref, grad_acc, gate_acc = scratch
    spread_rows(pad, tight, blocks, rows_ref, grads_ref)
    slots = rows_ref.shape[0]
    for step in range(up_ref.shape[0] // block):
        part = pl.ds(step * block, block)
        up = up_ref[part, :]
        active, slope = silu_parts(dot(rows_ref[...], up, 1, 1))
        back = dot(grads_ref[...], down_ref[part, :], 1, 1)
        hid_grad = (back * slope).astype(BF16)
        gate = active.astype(BF16).astype(F32) * back
        gate = sum(gate[:, i : i + 128] for i in range(0, block, 128))
        in_grad = dot(hid_grad, up, 1, 0)
        if step == 0:
            grad_acc[...] = in_grad
            gate_acc[...] = gate
        else:
            grad_acc[...] += in_grad
            gate_acc[...] += gate
    gate = jnp.sum(gate_acc[...], axis=1, keepdims=True)
    spot = lax.broadcasted_iota(jnp.int32, (slots, 128), 0) % pad
    lane = lax.broadcasted_iota(jnp.int32, (slots, 128), 1)
    gate = jnp.where(spot == lane, gate, 0.0).reshape(len(blocks), pad, 128)
    gate = jnp.sum(gate, axis=1, keepdims=True)
    line = lax.broadcasted_iota(jnp.int32, (pad, 128), 0)
    for k in range(len(blocks)):
        here = slice(k * pad, (k + 1) * pad)
        first = jnp.where(line == cap, gate[k], grad_acc[here, 0:128])
        put(k, first.astype(BF16), grad_acc[here, 128:].astype(BF16))


def early_back_kernel(cap, pad, tight, block, number, *refs):
    pieces, (up_ref, down_ref, out_ref, *scratch) = refs[:number], refs[number:]

    def put(k, first, rest):
        out_ref[k, :, 0:128] = first
        out_ref[k, :, 128:] = rest

    blocks = [(ref, 0, tight) for ref in pieces]
    backward(cap, pad, tight, block, blocks, up_ref, down_ref, scratch, put)


def late_back_kernel(cap, pad, tight, block, order, number, *refs):
    pieces, refs = refs[:number], refs[number:]
    sibling_ref, early_ref, up_ref, down_ref, _, out_hbm, late_ref, sems, *scratch = refs
    chips = len(order)
    begun = chips - number
    copies = []

    def send(ref, k, core):
        to = out_hbm.at[origin_of(order[k], core, chips)]
        copies.append(pltpu.make_async_copy(ref, to, sems.at[2 * k + core]))
        copies[-1].start()

    for k in range(begun):
        send(early_ref.at[k], k, 0)

    def put(i, first, rest):
        late_ref[i, :, 0:128] = first
        late_ref[i, :, 128:] = rest
        if i < number:
            send(late_ref.at[i], begun + i, 0)
        else:
            send(late_ref.at[i], i - number, 1)

    blocks = [(ref, 0, tight) for ref in pieces]
    blocks += [(sibling_ref, k * tight, (chips + k) * tight) for k in range(chips)]
    backward(cap, pad, tight, block, blocks, up_ref, down_ref, scratch, put)
    for copy in copies:
        copy.wait()


def weights_kernel(pad, block, share, number, begun, ended, *refs):
    refs = list(refs)
    take = lambda number: [refs.pop(0) for _ in range(number)]
    row_refs, weights = take(number), take(2)
    sums = take(2) if begun else None
    notes = None if begun else take(2)
    outs = take(2)
    notes_out = None if begun else take(3)
    up_ref, down_ref = weights if begun else take(2)
    rows_ref, grads_ref, sems, *kept = refs
    steps = steps_of(share, block)
    if not begun:
        fetch = Fetch(*weights, up_ref, down_ref, sems, lax.axis_index("rep") * share, steps)
    for i, ref in enumerate(row_refs):
        size = ref.shape[0] // 2
        rows_ref[i * size : (i + 1) * size, :] = ref[:size, :]
        grads_ref[i * size : (i + 1) * size, :] = ref[size:, :]
    copies = []
    for step, (at, size) in enumerate(steps):
        here = pl.ds(at, size)
        if not begun:
            fetch.wait(step)
        active, slope = silu_parts(dot(up_ref[here, :], rows_ref[...], 1, 1))
        back = dot(down_ref[here, :], grads_ref[...], 1, 1)
        hid_grad = (back * slope).astype(BF16)
        parts = [dot(hid_grad, rows_ref[...], 1, 0), dot(active.astype(BF16), grads_ref[...], 1, 0)]
        for i, part in enumerate(parts):
            if begun:
                part += sums[i][0, here, :]
            if not ended:
                outs[i][0, here, :] = part
                continue
            kept[i][here, :] = part.astype(BF16)
            sem = kept[2].at[2 * step + i]
            copies.append(pltpu.make_async_copy(kept[i].at[here, :], outs[i].at[0, here, :], sem))
            copies[-1].start()
    if not begun:
        note_routes(pad, *notes, *notes_out)
    for copy in copies:
        copy.wait()


def note_routes(pad, routes_ref, gates_ref, pick_ref, hot_ref, spot_ref):
    routes = routes_ref[...]
    gates = gates_ref[...].astype(F32)
    rows, slots = pick_ref.shape
    groups = slots // pad
    hot, slot = slots_of(routes, groups)
    same = lax.broadcasted_iota(jnp.int32, (rows, rows), 0) == lax.broadcasted_iota(
        jnp.int32, (rows, rows), 1
    )
    along = jnp.concatenate([routes, *slot, jnp.zeros((4, rows), jnp.int32)], axis=0)
    down = dot(jnp.where(same, 1.0, 0.0).astype(BF16), along.astype(F32).astype(BF16), 1, 1)
    index = lax.broadcasted_iota(jnp.int32, (rows, slots), 1)
    target = [(down[:, k : k + 1] * pad + down[:, 2 + k : 3 + k]).astype(jnp.int32) for k in (0, 1)]
    pick_ref[...] = jnp.where((index == target[0]) | (index == target[1]), 1.0, 0.0).astype(BF16)
    lane = lax.broadcasted_iota(jnp.int32, (128, routes.shape[1]), 0)
    for k in range(2):
        hot_ref[k] = jnp.where(hot[k], 1.0 / gates[k : k + 1, :], 0.0)
        spot_ref[k] = jnp.where(lane == slot[k], 1.0, 0.0).astype(BF16)


def combine_kernel(cap, pick_ref, hot_ref, spot_ref, back_ref, d_tok_ref, d_gate_ref):
    groups, pad, feat = back_ref.shape
    back = back_ref[...]
    d_tok_ref[...] = dot(pick_ref[...], back.reshape(groups * pad, feat), 1, 0).astype(BF16)
    values = back[:, cap, 0:128]
    for k in range(2):
        found = dot(values, spot_ref[k], 1, 0) * hot_ref[k]
        d_gate_ref[k : k + 1, :] = jnp.sum(found, axis=0, keepdims=True).astype(BF16)


def local(tokens, gates, routes, cotangent, w_up, w_down):
    rows, feat = tokens.shape
    hidden = w_up.shape[1]
    groups = lax.axis_size("exp")
    mirrors = lax.axis_size("rep")
    chips = groups // 2
    cap = max(2, 3 * rows // groups)
    pad = (cap // 16 + 1) * 16
    tight = cap + cap % 2
    slots = chips * pad
    share = hidden // mirrors
    routes_t, gates_t = routes.T, gates.T
    hbm = functools.partial(pltpu.with_memory_space_constraint, memory_space=pltpu.HBM)
    shape = jax.ShapeDtypeStruct
    unit = 2 * slots * feat

    near, far = list(range(1, chips // 2)), list(range(chips // 2, chips))
    order = [k for pair in itertools.zip_longest(far[:-1], near[:-1]) for k in pair if k is not None]
    order += far[-1:] + near[-1:]
    out = call(
        functools.partial(slots_kernel, pad, tight),
        "slots",
        [shape((4 * tight, feat), BF16)] * chips,
        [hbm(a) for a in (routes_t, gates_t, tokens, cotangent)],
        [IN_HBM] * 4,
        [
            pltpu.VMEM((2, rows), jnp.int32),
            pltpu.VMEM((2, rows), BF16),
            pltpu.VMEM((rows, feat), BF16),
            pltpu.VMEM((rows, feat), BF16),
            DMA((4,)),
        ],
        4 * unit * rows,
    )
    pieces = [out[0]] + [lax.ppermute(out[k], "exp", hops_to(chips, k)) for k in order]
    swap = [(i, i ^ 1) for i in range(groups)]
    around = [[(i, (i + s) % mirrors) for i in range(mirrors)] for s in range(1, mirrors)]

    w_up, w_down = hbm(w_up), hbm(w_down)
    up_v, down_v = call(
        fetch_kernel,
        "fetch_weights",
        [shape((hidden, feat), BF16)] * 2,
        [w_up, w_down],
        [IN_HBM] * 2,
        [DMA((2,))],
        0,
        0,
        SMALL,
    )
    block = min(512, hidden)
    late = min(3, chips // 2)

    def scratch(number):
        return [
            pltpu.VMEM((number * pad, feat), BF16),
            pltpu.VMEM((number * pad, feat), BF16),
            pltpu.VMEM((number * pad, feat), F32),
            pltpu.VMEM((number * pad, 128), F32),
        ]

    (early,) = call(
        functools.partial(early_back_kernel, cap, pad, tight, block, chips - late),
        "early_backward",
        [shape((chips - late, pad, feat), BF16)],
        [*pieces[:-late], up_v, down_v],
        [IN_VMEM] * (chips - late + 2),
        scratch(chips - late),
        3 * unit * hidden,
        slots * hidden,
    )

    def join(name, arrays, *lists):
        return call(
            functools.partial(join_kernel, tight, lists),
            name,
            [shape((len(blocks) * tight, feat), BF16) for blocks in lists],
            arrays,
            [IN_VMEM] * len(arrays),
            [],
            0,
            0,
            SMALL,
        )

    (handed,) = join("hand_on", [*pieces, early], [(i, at) for at in (2 * tight, 3 * tight) for i in range(chips)])
    sibling = lax.ppermute(handed, "exp", swap)
    (arrived,) = join("arrived_rows", [*pieces, handed], [(i, at) for at in (0, tight) for i in range(chips)])
    firsts = [lax.ppermute(arrived, "rep", hops) for hops in around]
    seconds = [lax.ppermute(sibling, "rep", hops) for hops in around]

    back = pl.pallas_call(
        functools.partial(late_back_kernel, cap, pad, tight, block, [0, *order], late),
        name="late_backward",
        out_shape=pltpu.HBM((groups, pad, feat), BF16),
        in_specs=[IN_VMEM] * (late + 4) + [ANYWHERE],
        out_specs=IN_HBM,
        scratch_shapes=[
            pltpu.VMEM((late + chips, pad, feat), BF16),
            DMA((groups,)),
            *scratch(late + chips),
        ],
        compiler_params=pltpu.CompilerParams(vmem_limit_bytes=MEDIUM),
        cost_estimate=pl.CostEstimate(
            flops=AHEAD, bytes_accessed=4 * hidden * feat, transcendentals=slots * hidden
        ),
    )(*pieces[-late:], sibling, early, up_v, down_v, arrived)
    back = lax.all_to_all(back, "exp", split_axis=0, concat_axis=0, tiled=True)

    part = min(512, share)

    def weights_call(name, arrays, weights, sums, ended, flops):
        begun = bool(sums)
        number = len(arrays) * chips * tight
        notes = [] if begun else [
            shape((rows, groups * pad), BF16),
            shape((2, groups, rows), F32),
            shape((2, 128, rows), BF16),
            shape((share, feat), BF16),
            shape((share, feat), BF16),
        ]
        grad = pltpu.HBM((1, share, feat), BF16) if ended else shape((1, share, feat), F32)
        steps = len(steps_of(share, part))
        scratch = [
            pltpu.VMEM((number, feat), BF16),
            pltpu.VMEM((number, feat), BF16),
            DMA((2 * steps,)),
        ]
        if ended:
            scratch += [pltpu.VMEM((share, feat), BF16)] * 2 + [DMA((2 * steps,))]
        return call(
            functools.partial(weights_kernel, pad, part, share, len(arrays), begun, ended),
            name,
            [grad] * 2 + notes,
            [*arrays, *weights, *(sums or [routes_t, gates_t])],
            [IN_VMEM] * len(arrays) + [IN_VMEM if begun else IN_HBM] * 2 + [IN_VMEM] * 2,
            scratch,
            flops,
            number * share,
            LARGE,
            [IN_HBM if ended else IN_VMEM] * 2 + [IN_VMEM] * len(notes),
        )

    joined = [sibling, arrived, *firsts]
    *sums, pick, hot, spot, up_v, down_v = weights_call(
        "first_weights", joined, [w_up, w_down], [], not seconds, 0
    )
    if seconds:
        sums = weights_call(
            "last_weights", seconds, [up_v, down_v], sums, True, AHEAD
        )
    grad_up, grad_down = sums

    d_tokens, d_gates = call(
        functools.partial(combine_kernel, cap),
        "combine",
        [shape((rows, feat), BF16), shape((2, rows), BF16)],
        [pick, hot, spot, back],
        [IN_VMEM] * 4,
        [],
        4 * unit * rows,
        0,
        SMALL,
    )
    return d_tokens, d_gates.T, grad_up, grad_down


def solution(mesh):
    by_both = P(("rep", "exp"), None)
    by_expert = P("exp", None, None)
    return jax.shard_map(
        local,
        mesh=mesh,
        in_specs=(by_both, by_both, by_both, by_both, by_expert, by_expert),
        out_specs=(by_both, by_both, P("exp", "rep", None), P("exp", "rep", None)),
        check_vma=False,
    )
```

```python
import functools
import itertools
import math

import jax
import jax.numpy as jnp
from jax import lax
from jax.experimental import pallas as pl
from jax.experimental.pallas import tpu as pltpu
from jax.sharding import PartitionSpec as P

F32 = jnp.float32
BF16 = jnp.bfloat16
SMALL, MEDIUM, LARGE = 8 << 20, 12 << 20, 24 << 20
AHEAD = 10**11
IN_HBM = pl.BlockSpec(memory_space=pltpu.HBM)
IN_VMEM = pl.BlockSpec(memory_space=pltpu.VMEM)
ANYWHERE = pl.BlockSpec(memory_space=pl.ANY)
DMA = pltpu.SemaphoreType.DMA


def dot(left, right, left_dim, right_dim):
    return lax.dot_general(
        left, right, (((left_dim,), (right_dim,)), ((), ())), preferred_element_type=F32
    )


def silu_parts(preact):
    sigma = 0.5 * jnp.tanh(0.5 * preact) + 0.5
    active = preact * sigma
    return active, sigma + active * (1.0 - sigma)


def call(body, name, outs, args, in_specs, scratch, flops, transcendentals=0, limit=MEDIUM, out_specs=None):
    moved = sum(math.prod(a.shape) * a.dtype.itemsize for a in (*args, *outs)) if flops else 0
    return pl.pallas_call(
        body,
        name=name,
        out_shape=outs,
        in_specs=in_specs,
        out_specs=out_specs or [IN_VMEM] * len(outs),
        scratch_shapes=scratch,
        compiler_params=pltpu.CompilerParams(vmem_limit_bytes=limit),
        cost_estimate=pl.CostEstimate(
            flops=flops, bytes_accessed=moved, transcendentals=transcendentals if flops else 0
        ),
    )(*args)


def paired(chips):
    return chips & (chips - 1) == 0


def hops_to(chips, k):
    if paired(chips):
        return [(2 * i + c, 2 * (i ^ k) + c) for i in range(chips) for c in range(2)]
    return [(2 * i + c, 2 * ((i + k) % chips) + c) for i in range(chips) for c in range(2)]


def pieces_of(experts, chips):
    me = lax.axis_index("exp")
    if paired(chips):
        return experts ^ me
    chip = (experts // 2 - me // 2 + chips) % chips
    return 2 * chip + (experts + me) % 2


def origin_of(k, core, chips):
    me = lax.axis_index("exp")
    if paired(chips):
        return me ^ (2 * k + core)
    return 2 * ((me // 2 - k + chips) % chips) + (me + core) % 2


def slots_of(pieces, number_of):
    rows = pieces.shape[1]
    number = lax.broadcasted_iota(jnp.int32, (number_of, rows), 0)
    hot = [number == pieces[k : k + 1, :] for k in range(2)]
    as_num = [jnp.where(h, 1.0, 0.0).astype(F32) for h in hot]
    before = jnp.where(
        lax.broadcasted_iota(jnp.int32, (rows, rows), 0)
        < lax.broadcasted_iota(jnp.int32, (rows, rows), 1),
        1.0,
        0.0,
    ).astype(BF16)
    count = dot(jnp.concatenate(as_num, axis=0).astype(BF16), before, 1, 0)
    total = jnp.sum(as_num[0], axis=1, keepdims=True)
    place = [count[:number_of], count[number_of:] + total]
    slot = [
        jnp.sum(jnp.where(h, p, 0.0), axis=0, keepdims=True).astype(jnp.int32)
        for h, p in zip(hot, place)
    ]
    return hot, slot


def picks_of(pieces, slot, number_of, pad):
    index = lax.broadcasted_iota(jnp.int32, (number_of * pad, pieces.shape[1]), 0)
    return [index == pieces[k : k + 1, :] * pad + slot[k] for k in range(2)]


def slots_kernel(pad, tight, routes_hbm, gates_hbm, tok_hbm, cot_hbm, *refs):
    chips = len(refs) - 5
    out_refs, refs = refs[:chips], refs[chips:]
    routes_ref, gates_ref, tok_ref, cot_ref, sems = refs
    pairs = [
        (routes_hbm, routes_ref),
        (gates_hbm, gates_ref),
        (tok_hbm, tok_ref),
        (cot_hbm, cot_ref),
    ]
    copies = [
        pltpu.make_async_copy(src, dst, sems.at[i]) for i, (src, dst) in enumerate(pairs)
    ]
    for copy in copies:
        copy.start()
    copies[0].wait()
    copies[1].wait()
    pieces = pieces_of(routes_ref[...], chips)
    gates = gates_ref[...].astype(F32)
    _, slot = slots_of(pieces, 2 * chips)
    pick = picks_of(pieces, slot, 2 * chips, pad)
    plain = jnp.where(pick[0] | pick[1], 1.0, 0.0).astype(BF16)
    scaled = (
        jnp.where(pick[0], gates[0:1, :], 0.0) + jnp.where(pick[1], gates[1:2, :], 0.0)
    ).astype(BF16)
    copies[2].wait()
    copies[3].wait()
    rows = dot(plain, tok_ref[...], 1, 0).astype(BF16)
    grads = dot(scaled, cot_ref[...], 1, 0).astype(BF16)
    for k, out_ref in enumerate(out_refs):
        for i in range(2):
            here = slice((2 * k + i) * pad, (2 * k + i) * pad + tight)
            out_ref[2 * i * tight : (2 * i + 1) * tight, :] = rows[here, :]
            out_ref[(2 * i + 1) * tight : (2 * i + 2) * tight, :] = grads[here, :]


def steps_of(size, block):
    half = block // 2
    return [(0, half)] + [(at, block) for at in range(half, size - half, block)] + [(size - half, half)]


class Fetch:
    def __init__(self, up_hbm, down_hbm, up_ref, down_ref, sems, base, steps):
        self.pairs = [(up_hbm, up_ref), (down_hbm, down_ref)]
        self.sems, self.base, self.steps = sems, base, steps
        self.copies = []
        self.start()
        self.start()

    def start(self):
        number = len(self.copies)
        if number == len(self.steps):
            return
        at, size = self.steps[number]
        to, of = pl.ds(at, size), pl.ds(pl.multiple_of(self.base + at, size), size)
        self.copies.append([
            pltpu.make_async_copy(src.at[0, of, :], dst.at[to, :], self.sems.at[2 * number + i])
            for i, (src, dst) in enumerate(self.pairs)
        ])
        for copy in self.copies[-1]:
            copy.start()

    def wait(self, number):
        for copy in self.copies[number]:
            copy.wait()
        self.start()


def fetch_kernel(up_hbm, down_hbm, up_ref, down_ref, sems):
    size = up_ref.shape[0]
    for copy in Fetch(up_hbm, down_hbm, up_ref, down_ref, sems, 0, [(0, size)]).copies[0]:
        copy.wait()


def join_kernel(size, lists, *refs):
    out_refs = refs[len(refs) - len(lists) :]
    for blocks, out_ref in zip(lists, out_refs):
        for i, (number, at) in enumerate(blocks):
            out_ref[i * size : (i + 1) * size, :] = refs[number][at : at + size, :]


def spread_rows(pad, tight, blocks, rows_ref, grads_ref):
    feat = rows_ref.shape[1]
    for i, (ref, row_at, grad_at) in enumerate(blocks):
        for to_ref, at in [(rows_ref, row_at), (grads_ref, grad_at)]:
            to_ref[i * pad : i * pad + tight, :] = ref[at : at + tight, :]
            to_ref[i * pad + tight : (i + 1) * pad, :] = jnp.zeros((pad - tight, feat), BF16)


def backward(cap, pad, tight, block, blocks, up_ref, down_ref, scratch, put):
    rows_ref, grads_ref, grad_acc, gate_acc = scratch
    spread_rows(pad, tight, blocks, rows_ref, grads_ref)
    slots = rows_ref.shape[0]
    for step in range(up_ref.shape[0] // block):
        part = pl.ds(step * block, block)
        up = up_ref[part, :]
        active, slope = silu_parts(dot(rows_ref[...], up, 1, 1))
        back = dot(grads_ref[...], down_ref[part, :], 1, 1)
        hid_grad = (back * slope).astype(BF16)
        gate = active.astype(BF16).astype(F32) * back
        gate = sum(gate[:, i : i + 128] for i in range(0, block, 128))
        in_grad = dot(hid_grad, up, 1, 0)
        if step == 0:
            grad_acc[...] = in_grad
            gate_acc[...] = gate
        else:
            grad_acc[...] += in_grad
            gate_acc[...] += gate
    gate = jnp.sum(gate_acc[...], axis=1, keepdims=True)
    spot = lax.broadcasted_iota(jnp.int32, (slots, 128), 0) % pad
    lane = lax.broadcasted_iota(jnp.int32, (slots, 128), 1)
    gate = jnp.where(spot == lane, gate, 0.0).reshape(len(blocks), pad, 128)
    gate = jnp.sum(gate, axis=1, keepdims=True)
    line = lax.broadcasted_iota(jnp.int32, (pad, 128), 0)
    for k in range(len(blocks)):
        here = slice(k * pad, (k + 1) * pad)
        first = jnp.where(line == cap, gate[k], grad_acc[here, 0:128])
        put(k, first.astype(BF16), grad_acc[here, 128:].astype(BF16))


def early_back_kernel(cap, pad, tight, block, number, *refs):
    pieces, (up_ref, down_ref, out_ref, *scratch) = refs[:number], refs[number:]

    def put(k, first, rest):
        out_ref[k, :, 0:128] = first
        out_ref[k, :, 128:] = rest

    blocks = [(ref, 0, tight) for ref in pieces]
    backward(cap, pad, tight, block, blocks, up_ref, down_ref, scratch, put)


def late_back_kernel(cap, pad, tight, block, order, number, *refs):
    pieces, refs = refs[:number], refs[number:]
    sibling_ref, early_ref, up_ref, down_ref, _, out_hbm, late_ref, sems, *scratch = refs
    chips = len(order)
    begun = chips - number
    copies = []

    def send(ref, k, core):
        to = out_hbm.at[origin_of(order[k], core, chips)]
        copies.append(pltpu.make_async_copy(ref, to, sems.at[2 * k + core]))
        copies[-1].start()

    for k in range(begun):
        send(early_ref.at[k], k, 0)

    def put(i, first, rest):
        late_ref[i, :, 0:128] = first
        late_ref[i, :, 128:] = rest
        if i < number:
            send(late_ref.at[i], begun + i, 0)
        else:
            send(late_ref.at[i], i - number, 1)

    blocks = [(ref, 0, tight) for ref in pieces]
    blocks += [(sibling_ref, k * tight, (chips + k) * tight) for k in range(chips)]
    backward(cap, pad, tight, block, blocks, up_ref, down_ref, scratch, put)
    for copy in copies:
        copy.wait()


def weights_kernel(pad, block, share, number, begun, ended, *refs):
    refs = list(refs)
    take = lambda number: [refs.pop(0) for _ in range(number)]
    row_refs, weights = take(number), take(2)
    sums = take(2) if begun else None
    notes = None if begun else take(2)
    outs = take(2)
    notes_out = None if begun else take(3)
    up_ref, down_ref = weights if begun else take(2)
    rows_ref, grads_ref, sems, *kept = refs
    steps = steps_of(share, block)
    if not begun:
        fetch = Fetch(*weights, up_ref, down_ref, sems, lax.axis_index("rep") * share, steps)
    begin = 0
    for ref in row_refs:
        size = ref.shape[0] // 2
        rows_ref[begin : begin + size, :] = ref[:size, :]
        grads_ref[begin : begin + size, :] = ref[size:, :]
        begin += size
    copies = []
    for step, (at, size) in enumerate(steps):
        here = pl.ds(at, size)
        if not begun:
            fetch.wait(step)
        active, slope = silu_parts(dot(up_ref[here, :], rows_ref[...], 1, 1))
        back = dot(down_ref[here, :], grads_ref[...], 1, 1)
        hid_grad = (back * slope).astype(BF16)
        parts = [dot(hid_grad, rows_ref[...], 1, 0), dot(active.astype(BF16), grads_ref[...], 1, 0)]
        for i, part in enumerate(parts):
            if begun:
                part += sums[i][0, here, :]
            if not ended:
                outs[i][0, here, :] = part
                continue
            kept[i][here, :] = part.astype(BF16)
            sem = kept[2].at[2 * step + i]
            copies.append(pltpu.make_async_copy(kept[i].at[here, :], outs[i].at[0, here, :], sem))
            copies[-1].start()
    if not begun:
        note_routes(pad, *notes, *notes_out)
    for copy in copies:
        copy.wait()


def note_routes(pad, routes_ref, gates_ref, pick_ref, hot_ref, spot_ref):
    routes = routes_ref[...]
    gates = gates_ref[...].astype(F32)
    rows, slots = pick_ref.shape
    groups = slots // pad
    hot, slot = slots_of(routes, groups)
    same = lax.broadcasted_iota(jnp.int32, (rows, rows), 0) == lax.broadcasted_iota(
        jnp.int32, (rows, rows), 1
    )
    along = jnp.concatenate([routes, *slot, jnp.zeros((4, rows), jnp.int32)], axis=0)
    down = dot(jnp.where(same, 1.0, 0.0).astype(BF16), along.astype(F32).astype(BF16), 1, 1)
    index = lax.broadcasted_iota(jnp.int32, (rows, slots), 1)
    target = [(down[:, k : k + 1] * pad + down[:, 2 + k : 3 + k]).astype(jnp.int32) for k in (0, 1)]
    pick_ref[...] = jnp.where((index == target[0]) | (index == target[1]), 1.0, 0.0).astype(BF16)
    lane = lax.broadcasted_iota(jnp.int32, (128, routes.shape[1]), 0)
    for k in range(2):
        hot_ref[k] = jnp.where(hot[k], 1.0 / gates[k : k + 1, :], 0.0)
        spot_ref[k] = jnp.where(lane == slot[k], 1.0, 0.0).astype(BF16)


def combine_kernel(cap, pick_ref, hot_ref, spot_ref, back_ref, d_tok_ref, d_gate_ref):
    groups, pad, feat = back_ref.shape
    back = back_ref[...]
    d_tok_ref[...] = dot(pick_ref[...], back.reshape(groups * pad, feat), 1, 0).astype(BF16)
    values = back[:, cap, 0:128]
    for k in range(2):
        found = dot(values, spot_ref[k], 1, 0) * hot_ref[k]
        d_gate_ref[k : k + 1, :] = jnp.sum(found, axis=0, keepdims=True).astype(BF16)


def local(tokens, gates, routes, cotangent, w_up, w_down):
    rows, feat = tokens.shape
    hidden = w_up.shape[1]
    groups = lax.axis_size("exp")
    mirrors = lax.axis_size("rep")
    chips = groups // 2
    cap = max(2, 3 * rows // groups)
    pad = (cap // 16 + 1) * 16
    tight = cap + cap % 2
    slots = chips * pad
    share = hidden // mirrors
    routes_t, gates_t = routes.T, gates.T
    hbm = functools.partial(pltpu.with_memory_space_constraint, memory_space=pltpu.HBM)
    shape = jax.ShapeDtypeStruct
    unit = 2 * slots * feat

    near, far = list(range(1, chips // 2)), list(range(chips // 2, chips))
    order = [k for pair in itertools.zip_longest(far[:-1], near[:-1]) for k in pair if k is not None]
    order += far[-1:] + near[-1:]
    out = call(
        functools.partial(slots_kernel, pad, tight),
        "slots",
        [shape((4 * tight, feat), BF16)] * chips,
        [hbm(a) for a in (routes_t, gates_t, tokens, cotangent)],
        [IN_HBM] * 4,
        [
            pltpu.VMEM((2, rows), jnp.int32),
            pltpu.VMEM((2, rows), BF16),
            pltpu.VMEM((rows, feat), BF16),
            pltpu.VMEM((rows, feat), BF16),
            DMA((4,)),
        ],
        4 * unit * rows,
    )
    pieces = [out[0]] + [lax.ppermute(out[k], "exp", hops_to(chips, k)) for k in order]
    swap = [(i, i ^ 1) for i in range(groups)]
    around = [[(i, (i + s) % mirrors) for i in range(mirrors)] for s in range(1, mirrors)]

    w_up, w_down = hbm(w_up), hbm(w_down)
    up_v, down_v = call(
        fetch_kernel,
        "fetch_weights",
        [shape((hidden, feat), BF16)] * 2,
        [w_up, w_down],
        [IN_HBM] * 2,
        [DMA((2,))],
        0,
        0,
        SMALL,
    )
    block = min(512, hidden)
    late = min(3, chips // 2)

    def scratch(number):
        return [
            pltpu.VMEM((number * pad, feat), BF16),
            pltpu.VMEM((number * pad, feat), BF16),
            pltpu.VMEM((number * pad, feat), F32),
            pltpu.VMEM((number * pad, 128), F32),
        ]

    (early,) = call(
        functools.partial(early_back_kernel, cap, pad, tight, block, chips - late),
        "early_backward",
        [shape((chips - late, pad, feat), BF16)],
        [*pieces[:-late], up_v, down_v],
        [IN_VMEM] * (chips - late + 2),
        scratch(chips - late),
        3 * unit * hidden,
        slots * hidden,
    )

    def join(name, arrays, *lists, after=()):
        return call(
            functools.partial(join_kernel, tight, lists),
            name,
            [shape((len(blocks) * tight, feat), BF16) for blocks in lists],
            [*arrays, *after],
            [IN_VMEM] * len(arrays) + [ANYWHERE] * len(after),
            [],
            0,
            0,
            SMALL,
        )

    soon = 2
    (ahead,) = join("first_rows", pieces[:soon], [(i, at) for at in (0, tight) for i in range(soon)])
    firsts = [lax.ppermute(ahead, "rep", hops) for hops in around]
    blocks = [(i, at) for at in (2 * tight, 3 * tight) for i in range(chips)]
    (handed,) = join("hand_on", [*pieces, early], blocks, after=firsts)
    sibling = lax.ppermute(handed, "exp", swap)
    blocks = [(i, at) for at in (0, tight) for i in range(soon, chips)]
    (arrived,) = join("arrived_rows", [*pieces, handed], blocks)
    firsts += [lax.ppermute(arrived, "rep", hops) for hops in around]
    seconds = [lax.ppermute(sibling, "rep", hops) for hops in around]

    back = pl.pallas_call(
        functools.partial(late_back_kernel, cap, pad, tight, block, [0, *order], late),
        name="late_backward",
        out_shape=pltpu.HBM((groups, pad, feat), BF16),
        in_specs=[IN_VMEM] * (late + 4) + [ANYWHERE],
        out_specs=IN_HBM,
        scratch_shapes=[
            pltpu.VMEM((late + chips, pad, feat), BF16),
            DMA((groups,)),
            *scratch(late + chips),
        ],
        compiler_params=pltpu.CompilerParams(vmem_limit_bytes=MEDIUM),
        cost_estimate=pl.CostEstimate(
            flops=AHEAD, bytes_accessed=4 * hidden * feat, transcendentals=slots * hidden
        ),
    )(*pieces[-late:], sibling, early, up_v, down_v, arrived)
    back = lax.all_to_all(back, "exp", split_axis=0, concat_axis=0, tiled=True)

    part = min(512, share)

    def weights_call(name, arrays, weights, sums, ended, flops):
        begun = bool(sums)
        number = sum(a.shape[0] for a in arrays) // 2
        notes = [] if begun else [
            shape((rows, groups * pad), BF16),
            shape((2, groups, rows), F32),
            shape((2, 128, rows), BF16),
            shape((share, feat), BF16),
            shape((share, feat), BF16),
        ]
        grad = pltpu.HBM((1, share, feat), BF16) if ended else shape((1, share, feat), F32)
        steps = len(steps_of(share, part))
        scratch = [
            pltpu.VMEM((number, feat), BF16),
            pltpu.VMEM((number, feat), BF16),
            DMA((2 * steps,)),
        ]
        if ended:
            scratch += [pltpu.VMEM((share, feat), BF16)] * 2 + [DMA((2 * steps,))]
        return call(
            functools.partial(weights_kernel, pad, part, share, len(arrays), begun, ended),
            name,
            [grad] * 2 + notes,
            [*arrays, *weights, *(sums or [routes_t, gates_t])],
            [IN_VMEM] * len(arrays) + [IN_VMEM if begun else IN_HBM] * 2 + [IN_VMEM] * 2,
            scratch,
            flops,
            number * share,
            LARGE,
            [IN_HBM if ended else IN_VMEM] * 2 + [IN_VMEM] * len(notes),
        )

    joined = [sibling, arrived, ahead, *firsts]
    *sums, pick, hot, spot, up_v, down_v = weights_call(
        "first_weights", joined, [w_up, w_down], [], not seconds, AHEAD
    )
    if seconds:
        sums = weights_call(
            "last_weights", seconds, [up_v, down_v], sums, True, AHEAD
        )
    grad_up, grad_down = sums

    d_tokens, d_gates = call(
        functools.partial(combine_kernel, cap),
        "combine",
        [shape((rows, feat), BF16), shape((2, rows), BF16)],
        [pick, hot, spot, back],
        [IN_VMEM] * 4,
        [],
        4 * unit * rows,
        0,
        SMALL,
    )
    return d_tokens, d_gates.T, grad_up, grad_down


def solution(mesh):
    by_both = P(("rep", "exp"), None)
    by_expert = P("exp", None, None)
    return jax.shard_map(
        local,
        mesh=mesh,
        in_specs=(by_both, by_both, by_both, by_both, by_expert, by_expert),
        out_specs=(by_both, by_both, P("exp", "rep", None), P("exp", "rep", None)),
        check_vma=False,
    )
```

```python
import functools
import itertools
import math

import jax
import jax.numpy as jnp
from jax import lax
from jax.experimental import pallas as pl
from jax.experimental.pallas import tpu as pltpu
from jax.sharding import PartitionSpec as P

F32 = jnp.float32
BF16 = jnp.bfloat16
SMALL, MEDIUM, LARGE = 8 << 20, 12 << 20, 24 << 20
AHEAD = 10**11
IN_HBM = pl.BlockSpec(memory_space=pltpu.HBM)
IN_VMEM = pl.BlockSpec(memory_space=pltpu.VMEM)
ANYWHERE = pl.BlockSpec(memory_space=pl.ANY)
DMA = pltpu.SemaphoreType.DMA


def dot(left, right, left_dim, right_dim):
    return lax.dot_general(
        left, right, (((left_dim,), (right_dim,)), ((), ())), preferred_element_type=F32
    )


def silu_parts(preact):
    sigma = 0.5 * jnp.tanh(0.5 * preact) + 0.5
    active = preact * sigma
    return active, sigma + active * (1.0 - sigma)


def call(body, name, outs, args, in_specs, scratch, flops, transcendentals=0, limit=MEDIUM, out_specs=None):
    moved = sum(math.prod(a.shape) * a.dtype.itemsize for a in (*args, *outs)) if flops else 0
    return pl.pallas_call(
        body,
        name=name,
        out_shape=outs,
        in_specs=in_specs,
        out_specs=out_specs or [IN_VMEM] * len(outs),
        scratch_shapes=scratch,
        compiler_params=pltpu.CompilerParams(vmem_limit_bytes=limit),
        cost_estimate=pl.CostEstimate(
            flops=flops, bytes_accessed=moved, transcendentals=transcendentals if flops else 0
        ),
    )(*args)


def paired(chips):
    return chips & (chips - 1) == 0


def hops_to(chips, k):
    if paired(chips):
        return [(2 * i + c, 2 * (i ^ k) + c) for i in range(chips) for c in range(2)]
    return [(2 * i + c, 2 * ((i + k) % chips) + c) for i in range(chips) for c in range(2)]


def pieces_of(experts, chips):
    me = lax.axis_index("exp")
    if paired(chips):
        return experts ^ me
    chip = (experts // 2 - me // 2 + chips) % chips
    return 2 * chip + (experts + me) % 2


def origin_of(k, core, chips):
    me = lax.axis_index("exp")
    if paired(chips):
        return me ^ (2 * k + core)
    return 2 * ((me // 2 - k + chips) % chips) + (me + core) % 2


def slots_of(pieces, number_of):
    rows = pieces.shape[1]
    number = lax.broadcasted_iota(jnp.int32, (number_of, rows), 0)
    hot = [number == pieces[k : k + 1, :] for k in range(2)]
    as_num = [jnp.where(h, 1.0, 0.0).astype(F32) for h in hot]
    before = jnp.where(
        lax.broadcasted_iota(jnp.int32, (rows, rows), 0)
        < lax.broadcasted_iota(jnp.int32, (rows, rows), 1),
        1.0,
        0.0,
    ).astype(BF16)
    count = dot(jnp.concatenate(as_num, axis=0).astype(BF16), before, 1, 0)
    total = jnp.sum(as_num[0], axis=1, keepdims=True)
    place = [count[:number_of], count[number_of:] + total]
    slot = [
        jnp.sum(jnp.where(h, p, 0.0), axis=0, keepdims=True).astype(jnp.int32)
        for h, p in zip(hot, place)
    ]
    return hot, slot


def picks_of(pieces, slot, number_of, pad):
    index = lax.broadcasted_iota(jnp.int32, (number_of * pad, pieces.shape[1]), 0)
    return [index == pieces[k : k + 1, :] * pad + slot[k] for k in range(2)]


def slots_kernel(pad, tight, routes_hbm, gates_hbm, tok_hbm, cot_hbm, *refs):
    chips = len(refs) - 5
    out_refs, refs = refs[:chips], refs[chips:]
    routes_ref, gates_ref, tok_ref, cot_ref, sems = refs
    pairs = [
        (routes_hbm, routes_ref),
        (gates_hbm, gates_ref),
        (tok_hbm, tok_ref),
        (cot_hbm, cot_ref),
    ]
    copies = [
        pltpu.make_async_copy(src, dst, sems.at[i]) for i, (src, dst) in enumerate(pairs)
    ]
    for copy in copies:
        copy.start()
    copies[0].wait()
    copies[1].wait()
    pieces = pieces_of(routes_ref[...], chips)
    gates = gates_ref[...].astype(F32)
    _, slot = slots_of(pieces, 2 * chips)
    pick = picks_of(pieces, slot, 2 * chips, pad)
    plain = jnp.where(pick[0] | pick[1], 1.0, 0.0).astype(BF16)
    scaled = (
        jnp.where(pick[0], gates[0:1, :], 0.0) + jnp.where(pick[1], gates[1:2, :], 0.0)
    ).astype(BF16)
    copies[2].wait()
    copies[3].wait()
    rows = dot(plain, tok_ref[...], 1, 0).astype(BF16)
    grads = dot(scaled, cot_ref[...], 1, 0).astype(BF16)
    for k, out_ref in enumerate(out_refs):
        for i in range(2):
            here = slice((2 * k + i) * pad, (2 * k + i) * pad + tight)
            out_ref[2 * i * tight : (2 * i + 1) * tight, :] = rows[here, :]
            out_ref[(2 * i + 1) * tight : (2 * i + 2) * tight, :] = grads[here, :]


def steps_of(size, block, begun=False):
    half = block // 2
    if begun and size > block:
        last = size - half // 2
        return [(at, min(block, last - at)) for at in range(0, last, block)] + [(last, half // 2)]
    return [(0, half)] + [(at, block) for at in range(half, size - half, block)] + [(size - half, half)]


class Fetch:
    def __init__(self, up_hbm, down_hbm, up_ref, down_ref, sems, base, steps):
        self.pairs = [(up_hbm, up_ref), (down_hbm, down_ref)]
        self.sems, self.base, self.steps = sems, base, steps
        self.copies = []
        self.start()
        self.start()

    def start(self):
        number = len(self.copies)
        if number == len(self.steps):
            return
        at, size = self.steps[number]
        unit = math.gcd(at, size)
        to, of = pl.ds(at, size), pl.ds(pl.multiple_of(self.base + at, unit), size)
        self.copies.append([
            pltpu.make_async_copy(src.at[0, of, :], dst.at[to, :], self.sems.at[2 * number + i])
            for i, (src, dst) in enumerate(self.pairs)
        ])
        for copy in self.copies[-1]:
            copy.start()

    def wait(self, number):
        for copy in self.copies[number]:
            copy.wait()
        self.start()


def fetch_kernel(up_hbm, down_hbm, up_ref, down_ref, sems):
    size = up_ref.shape[0]
    for copy in Fetch(up_hbm, down_hbm, up_ref, down_ref, sems, 0, [(0, size)]).copies[0]:
        copy.wait()


def join_kernel(size, lists, *refs):
    out_refs = refs[len(refs) - len(lists) :]
    for blocks, out_ref in zip(lists, out_refs):
        for i, (number, at) in enumerate(blocks):
            out_ref[i * size : (i + 1) * size, :] = refs[number][at : at + size, :]


def spread_rows(pad, tight, blocks, rows_ref, grads_ref):
    feat = rows_ref.shape[1]
    for i, (ref, row_at, grad_at) in enumerate(blocks):
        for to_ref, at in [(rows_ref, row_at), (grads_ref, grad_at)]:
            to_ref[i * pad : i * pad + tight, :] = ref[at : at + tight, :]
            to_ref[i * pad + tight : (i + 1) * pad, :] = jnp.zeros((pad - tight, feat), BF16)


def backward(cap, pad, tight, block, blocks, up_ref, down_ref, scratch, put):
    rows_ref, grads_ref, grad_acc, gate_acc = scratch
    spread_rows(pad, tight, blocks, rows_ref, grads_ref)
    slots = rows_ref.shape[0]
    for step in range(up_ref.shape[0] // block):
        part = pl.ds(step * block, block)
        up = up_ref[part, :]
        active, slope = silu_parts(dot(rows_ref[...], up, 1, 1))
        back = dot(grads_ref[...], down_ref[part, :], 1, 1)
        hid_grad = (back * slope).astype(BF16)
        gate = active.astype(BF16).astype(F32) * back
        gate = sum(gate[:, i : i + 128] for i in range(0, block, 128))
        in_grad = dot(hid_grad, up, 1, 0)
        if step == 0:
            grad_acc[...] = in_grad
            gate_acc[...] = gate
        else:
            grad_acc[...] += in_grad
            gate_acc[...] += gate
    gate = jnp.sum(gate_acc[...], axis=1, keepdims=True)
    spot = lax.broadcasted_iota(jnp.int32, (slots, 128), 0) % pad
    lane = lax.broadcasted_iota(jnp.int32, (slots, 128), 1)
    gate = jnp.where(spot == lane, gate, 0.0).reshape(len(blocks), pad, 128)
    gate = jnp.sum(gate, axis=1, keepdims=True)
    line = lax.broadcasted_iota(jnp.int32, (pad, 128), 0)
    for k in range(len(blocks)):
        here = slice(k * pad, (k + 1) * pad)
        first = jnp.where(line == cap, gate[k], grad_acc[here, 0:128])
        put(k, first.astype(BF16), grad_acc[here, 128:].astype(BF16))


def early_back_kernel(cap, pad, tight, block, number, *refs):
    pieces, (up_ref, down_ref, out_ref, *scratch) = refs[:number], refs[number:]

    def put(k, first, rest):
        out_ref[k, :, 0:128] = first
        out_ref[k, :, 128:] = rest

    blocks = [(ref, 0, tight) for ref in pieces]
    backward(cap, pad, tight, block, blocks, up_ref, down_ref, scratch, put)


def late_back_kernel(cap, pad, tight, block, order, number, *refs):
    pieces, refs = refs[:number], refs[number:]
    sibling_ref, early_ref, up_ref, down_ref, _, out_hbm, late_ref, sems, *scratch = refs
    chips = len(order)
    begun = chips - number
    copies = []

    def send(ref, k, core):
        to = out_hbm.at[origin_of(order[k], core, chips)]
        copies.append(pltpu.make_async_copy(ref, to, sems.at[2 * k + core]))
        copies[-1].start()

    for k in range(begun):
        send(early_ref.at[k], k, 0)

    def put(i, first, rest):
        late_ref[i, :, 0:128] = first
        late_ref[i, :, 128:] = rest
        if i < number:
            send(late_ref.at[i], begun + i, 0)
        else:
            send(late_ref.at[i], i - number, 1)

    blocks = [(ref, 0, tight) for ref in pieces]
    blocks += [(sibling_ref, k * tight, (chips + k) * tight) for k in range(chips)]
    backward(cap, pad, tight, block, blocks, up_ref, down_ref, scratch, put)
    for copy in copies:
        copy.wait()


def weights_kernel(pad, block, share, number, begun, ended, *refs):
    refs = list(refs)
    take = lambda number: [refs.pop(0) for _ in range(number)]
    row_refs, weights = take(number), take(2)
    sums = take(2) if begun else None
    notes = None if begun else take(2)
    outs = take(2)
    notes_out = None if begun else take(3)
    up_ref, down_ref = weights if begun else take(2)
    rows_ref, grads_ref, sems, *kept = refs
    steps = steps_of(share, block, begun)
    if not begun:
        fetch = Fetch(*weights, up_ref, down_ref, sems, lax.axis_index("rep") * share, steps)
    for i, ref in enumerate(row_refs):
        size = ref.shape[0] // 2
        rows_ref[i * size : (i + 1) * size, :] = ref[:size, :]
        grads_ref[i * size : (i + 1) * size, :] = ref[size:, :]
    copies = []
    for step, (at, size) in enumerate(steps):
        here = pl.ds(at, size)
        if not begun:
            fetch.wait(step)
        active, slope = silu_parts(dot(up_ref[here, :], rows_ref[...], 1, 1))
        back = dot(down_ref[here, :], grads_ref[...], 1, 1)
        hid_grad = (back * slope).astype(BF16)
        parts = [dot(hid_grad, rows_ref[...], 1, 0), dot(active.astype(BF16), grads_ref[...], 1, 0)]
        for i, part in enumerate(parts):
            if begun:
                part += sums[i][0, here, :]
            if not ended:
                outs[i][0, here, :] = part
                continue
            kept[i][here, :] = part.astype(BF16)
            sem = kept[2].at[2 * step + i]
            copies.append(pltpu.make_async_copy(kept[i].at[here, :], outs[i].at[0, here, :], sem))
            copies[-1].start()
    if not begun:
        note_routes(pad, *notes, *notes_out)
    for copy in copies:
        copy.wait()


def note_routes(pad, routes_ref, gates_ref, pick_ref, hot_ref, spot_ref):
    routes = routes_ref[...]
    gates = gates_ref[...].astype(F32)
    rows, slots = pick_ref.shape
    groups = slots // pad
    hot, slot = slots_of(routes, groups)
    same = lax.broadcasted_iota(jnp.int32, (rows, rows), 0) == lax.broadcasted_iota(
        jnp.int32, (rows, rows), 1
    )
    along = jnp.concatenate([routes, *slot, jnp.zeros((4, rows), jnp.int32)], axis=0)
    down = dot(jnp.where(same, 1.0, 0.0).astype(BF16), along.astype(F32).astype(BF16), 1, 1)
    index = lax.broadcasted_iota(jnp.int32, (rows, slots), 1)
    target = [(down[:, k : k + 1] * pad + down[:, 2 + k : 3 + k]).astype(jnp.int32) for k in (0, 1)]
    pick_ref[...] = jnp.where((index == target[0]) | (index == target[1]), 1.0, 0.0).astype(BF16)
    lane = lax.broadcasted_iota(jnp.int32, (128, routes.shape[1]), 0)
    for k in range(2):
        hot_ref[k] = jnp.where(hot[k], 1.0 / gates[k : k + 1, :], 0.0)
        spot_ref[k] = jnp.where(lane == slot[k], 1.0, 0.0).astype(BF16)


def combine_kernel(cap, pick_ref, hot_ref, spot_ref, back_ref, d_tok_ref, d_gate_ref):
    groups, pad, feat = back_ref.shape
    back = back_ref[...]
    d_tok_ref[...] = dot(pick_ref[...], back.reshape(groups * pad, feat), 1, 0).astype(BF16)
    values = back[:, cap, 0:128]
    for k in range(2):
        found = dot(values, spot_ref[k], 1, 0) * hot_ref[k]
        d_gate_ref[k : k + 1, :] = jnp.sum(found, axis=0, keepdims=True).astype(BF16)


def local(tokens, gates, routes, cotangent, w_up, w_down):
    rows, feat = tokens.shape
    hidden = w_up.shape[1]
    groups = lax.axis_size("exp")
    mirrors = lax.axis_size("rep")
    chips = groups // 2
    cap = max(2, 3 * rows // groups)
    pad = (cap // 16 + 1) * 16
    tight = cap + cap % 2
    slots = chips * pad
    share = hidden // mirrors
    routes_t, gates_t = routes.T, gates.T
    hbm = functools.partial(pltpu.with_memory_space_constraint, memory_space=pltpu.HBM)
    shape = jax.ShapeDtypeStruct
    unit = 2 * slots * feat

    near, far = list(range(1, chips // 2)), list(range(chips // 2, chips))
    order = [k for pair in itertools.zip_longest(far[:-1], near[:-1]) for k in pair if k is not None]
    order += far[-1:] + near[-1:]
    out = call(
        functools.partial(slots_kernel, pad, tight),
        "slots",
        [shape((4 * tight, feat), BF16)] * chips,
        [hbm(a) for a in (routes_t, gates_t, tokens, cotangent)],
        [IN_HBM] * 4,
        [
            pltpu.VMEM((2, rows), jnp.int32),
            pltpu.VMEM((2, rows), BF16),
            pltpu.VMEM((rows, feat), BF16),
            pltpu.VMEM((rows, feat), BF16),
            DMA((4,)),
        ],
        4 * unit * rows,
    )
    pieces = [out[0]] + [lax.ppermute(out[k], "exp", hops_to(chips, k)) for k in order]
    swap = [(i, i ^ 1) for i in range(groups)]
    around = [[(i, (i + s) % mirrors) for i in range(mirrors)] for s in range(1, mirrors)]

    w_up, w_down = hbm(w_up), hbm(w_down)
    up_v, down_v = call(
        fetch_kernel,
        "fetch_weights",
        [shape((hidden, feat), BF16)] * 2,
        [w_up, w_down],
        [IN_HBM] * 2,
        [DMA((2,))],
        0,
        0,
        SMALL,
    )
    block = min(512, hidden)
    late = min(3, chips // 2)

    def scratch(number):
        return [
            pltpu.VMEM((number * pad, feat), BF16),
            pltpu.VMEM((number * pad, feat), BF16),
            pltpu.VMEM((number * pad, feat), F32),
            pltpu.VMEM((number * pad, 128), F32),
        ]

    (early,) = call(
        functools.partial(early_back_kernel, cap, pad, tight, block, chips - late),
        "early_backward",
        [shape((chips - late, pad, feat), BF16)],
        [*pieces[:-late], up_v, down_v],
        [IN_VMEM] * (chips - late + 2),
        scratch(chips - late),
        3 * unit * hidden,
        slots * hidden,
    )

    def join(name, arrays, *lists):
        return call(
            functools.partial(join_kernel, tight, lists),
            name,
            [shape((len(blocks) * tight, feat), BF16) for blocks in lists],
            arrays,
            [IN_VMEM] * len(arrays),
            [],
            0,
            0,
            SMALL,
        )

    (handed,) = join("hand_on", [*pieces, early], [(i, at) for at in (2 * tight, 3 * tight) for i in range(chips)])
    sibling = lax.ppermute(handed, "exp", swap)
    (arrived,) = join("arrived_rows", [*pieces, handed], [(i, at) for at in (0, tight) for i in range(chips)])
    firsts = [lax.ppermute(arrived, "rep", hops) for hops in around]
    seconds = [lax.ppermute(sibling, "rep", hops) for hops in around]

    back = pl.pallas_call(
        functools.partial(late_back_kernel, cap, pad, tight, block, [0, *order], late),
        name="late_backward",
        out_shape=pltpu.HBM((groups, pad, feat), BF16),
        in_specs=[IN_VMEM] * (late + 4) + [ANYWHERE],
        out_specs=IN_HBM,
        scratch_shapes=[
            pltpu.VMEM((late + chips, pad, feat), BF16),
            DMA((groups,)),
            *scratch(late + chips),
        ],
        compiler_params=pltpu.CompilerParams(vmem_limit_bytes=MEDIUM),
        cost_estimate=pl.CostEstimate(
            flops=AHEAD, bytes_accessed=4 * hidden * feat, transcendentals=slots * hidden
        ),
    )(*pieces[-late:], sibling, early, up_v, down_v, arrived)
    back = lax.all_to_all(back, "exp", split_axis=0, concat_axis=0, tiled=True)

    part = min(512, share)

    def weights_call(name, arrays, weights, sums, ended, flops):
        begun = bool(sums)
        number = len(arrays) * chips * tight
        notes = [] if begun else [
            shape((rows, groups * pad), BF16),
            shape((2, groups, rows), F32),
            shape((2, 128, rows), BF16),
            shape((share, feat), BF16),
            shape((share, feat), BF16),
        ]
        grad = pltpu.HBM((1, share, feat), BF16) if ended else shape((1, share, feat), F32)
        steps = len(steps_of(share, part, begun))
        scratch = [
            pltpu.VMEM((number, feat), BF16),
            pltpu.VMEM((number, feat), BF16),
            DMA((2 * steps,)),
        ]
        if ended:
            scratch += [pltpu.VMEM((share, feat), BF16)] * 2 + [DMA((2 * steps,))]
        return call(
            functools.partial(weights_kernel, pad, part, share, len(arrays), begun, ended),
            name,
            [grad] * 2 + notes,
            [*arrays, *weights, *(sums or [routes_t, gates_t])],
            [IN_VMEM] * len(arrays) + [IN_VMEM if begun else IN_HBM] * 2 + [IN_VMEM] * 2,
            scratch,
            flops,
            number * share,
            LARGE,
            [IN_HBM if ended else IN_VMEM] * 2 + [IN_VMEM] * len(notes),
        )

    joined = [sibling, arrived, *firsts]
    *sums, pick, hot, spot, up_v, down_v = weights_call(
        "first_weights", joined, [w_up, w_down], [], not seconds, 0
    )
    if seconds:
        sums = weights_call(
            "last_weights", seconds, [up_v, down_v], sums, True, AHEAD
        )
    grad_up, grad_down = sums

    d_tokens, d_gates = call(
        functools.partial(combine_kernel, cap),
        "combine",
        [shape((rows, feat), BF16), shape((2, rows), BF16)],
        [pick, hot, spot, back],
        [IN_VMEM] * 4,
        [],
        4 * unit * rows,
        0,
        SMALL,
    )
    return d_tokens, d_gates.T, grad_up, grad_down


def solution(mesh):
    by_both = P(("rep", "exp"), None)
    by_expert = P("exp", None, None)
    return jax.shard_map(
        local,
        mesh=mesh,
        in_specs=(by_both, by_both, by_both, by_both, by_expert, by_expert),
        out_specs=(by_both, by_both, P("exp", "rep", None), P("exp", "rep", None)),
        check_vma=False,
    )
```

```python
import functools
import itertools
import math

import jax
import jax.numpy as jnp
from jax import lax
from jax.experimental import pallas as pl
from jax.experimental.pallas import tpu as pltpu
from jax.sharding import PartitionSpec as P

F32 = jnp.float32
BF16 = jnp.bfloat16
SMALL, MEDIUM, LARGE = 8 << 20, 12 << 20, 16 << 20
AHEAD = 10**11
IN_HBM = pl.BlockSpec(memory_space=pltpu.HBM)
IN_VMEM = pl.BlockSpec(memory_space=pltpu.VMEM)
ANYWHERE = pl.BlockSpec(memory_space=pl.ANY)
DMA = pltpu.SemaphoreType.DMA


def dot(left, right, left_dim, right_dim):
    return lax.dot_general(
        left, right, (((left_dim,), (right_dim,)), ((), ())), preferred_element_type=F32
    )


def silu_parts(preact):
    sigma = 0.5 * jnp.tanh(0.5 * preact) + 0.5
    active = preact * sigma
    return active, sigma + active * (1.0 - sigma)


def call(body, name, outs, args, in_specs, scratch, flops, transcendentals=0, limit=MEDIUM, out_specs=None):
    moved = sum(math.prod(a.shape) * a.dtype.itemsize for a in (*args, *outs)) if flops else 0
    return pl.pallas_call(
        body,
        name=name,
        out_shape=outs,
        in_specs=in_specs,
        out_specs=out_specs or [IN_VMEM] * len(outs),
        scratch_shapes=scratch,
        compiler_params=pltpu.CompilerParams(vmem_limit_bytes=limit),
        cost_estimate=pl.CostEstimate(
            flops=flops, bytes_accessed=moved, transcendentals=transcendentals if flops else 0
        ),
    )(*args)


def paired(chips):
    return chips & (chips - 1) == 0


def hops_to(chips, k):
    if paired(chips):
        return [(2 * i + c, 2 * (i ^ k) + c) for i in range(chips) for c in range(2)]
    return [(2 * i + c, 2 * ((i + k) % chips) + c) for i in range(chips) for c in range(2)]


def pieces_of(experts, chips):
    me = lax.axis_index("exp")
    if paired(chips):
        return experts ^ me
    chip = (experts // 2 - me // 2 + chips) % chips
    return 2 * chip + (experts + me) % 2


def origin_of(k, core, chips):
    me = lax.axis_index("exp")
    if paired(chips):
        return me ^ (2 * k + core)
    return 2 * ((me // 2 - k + chips) % chips) + (me + core) % 2


def before_of(rows):
    first = lax.broadcasted_iota(jnp.int32, (rows, rows), 0)
    second = lax.broadcasted_iota(jnp.int32, (rows, rows), 1)
    return jnp.where(first < second, 1.0, 0.0).astype(BF16)


def slots_of(pieces, number_of, before=None):
    rows = pieces.shape[1]
    number = lax.broadcasted_iota(jnp.int32, (number_of, rows), 0)
    hot = [number == pieces[k : k + 1, :] for k in range(2)]
    as_num = [jnp.where(h, 1.0, 0.0).astype(F32) for h in hot]
    before = before_of(rows) if before is None else before
    count = dot(jnp.concatenate(as_num, axis=0).astype(BF16), before, 1, 0)
    total = jnp.sum(as_num[0], axis=1, keepdims=True)
    place = [count[:number_of], count[number_of:] + total]
    slot = [
        jnp.sum(jnp.where(h, p, 0.0), axis=0, keepdims=True).astype(jnp.int32)
        for h, p in zip(hot, place)
    ]
    return hot, slot


def picks_of(pieces, slot, number_of, pad):
    index = lax.broadcasted_iota(jnp.int32, (number_of * pad, pieces.shape[1]), 0)
    return [index == pieces[k : k + 1, :] * pad + slot[k] for k in range(2)]


def slots_kernel(pad, tight, routes_hbm, gates_hbm, tok_hbm, cot_hbm, *refs):
    chips = len(refs) - 5
    out_refs, refs = refs[:chips], refs[chips:]
    routes_ref, gates_ref, tok_ref, cot_ref, sems = refs
    pairs = [
        (routes_hbm, routes_ref),
        (gates_hbm, gates_ref),
        (tok_hbm, tok_ref),
        (cot_hbm, cot_ref),
    ]
    copies = [
        pltpu.make_async_copy(src, dst, sems.at[i]) for i, (src, dst) in enumerate(pairs)
    ]
    for copy in copies:
        copy.start()
    before = before_of(tok_hbm.shape[0])
    copies[0].wait()
    copies[1].wait()
    pieces = pieces_of(routes_ref[...], chips)
    gates = gates_ref[...].astype(F32)
    _, slot = slots_of(pieces, 2 * chips, before)
    pick = picks_of(pieces, slot, 2 * chips, pad)
    plain = jnp.where(pick[0] | pick[1], 1.0, 0.0).astype(BF16)
    scaled = (
        jnp.where(pick[0], gates[0:1, :], 0.0) + jnp.where(pick[1], gates[1:2, :], 0.0)
    ).astype(BF16)
    copies[2].wait()
    copies[3].wait()
    rows = dot(plain, tok_ref[...], 1, 0).astype(BF16)
    grads = dot(scaled, cot_ref[...], 1, 0).astype(BF16)
    for k, out_ref in enumerate(out_refs):
        for i in range(2):
            here = slice((2 * k + i) * pad, (2 * k + i) * pad + tight)
            out_ref[2 * i * tight : (2 * i + 1) * tight, :] = rows[here, :]
            out_ref[(2 * i + 1) * tight : (2 * i + 2) * tight, :] = grads[here, :]


def steps_of(size, block, begun=False):
    half = block // 2
    if begun and size > block:
        last = size - half // 2
        return [(at, min(block, last - at)) for at in range(0, last, block)] + [(last, half // 2)]
    return [(0, half)] + [(at, block) for at in range(half, size - half, block)] + [(size - half, half)]


class Fetch:
    def __init__(self, up_hbm, down_hbm, up_ref, down_ref, sems, base, steps):
        self.pairs = [(up_hbm, up_ref), (down_hbm, down_ref)]
        self.sems, self.base, self.steps = sems, base, steps
        self.copies = []
        self.start()
        self.start()

    def start(self):
        number = len(self.copies)
        if number == len(self.steps):
            return
        at, size = self.steps[number]
        unit = math.gcd(at, size)
        to, of = pl.ds(at, size), pl.ds(pl.multiple_of(self.base + at, unit), size)
        self.copies.append([
            pltpu.make_async_copy(src.at[0, of, :], dst.at[to, :], self.sems.at[2 * number + i])
            for i, (src, dst) in enumerate(self.pairs)
        ])
        for copy in self.copies[-1]:
            copy.start()

    def wait(self, number):
        for copy in self.copies[number]:
            copy.wait()
        self.start()


def fetch_kernel(up_hbm, down_hbm, up_ref, down_ref, sems):
    size = up_ref.shape[0]
    for copy in Fetch(up_hbm, down_hbm, up_ref, down_ref, sems, 0, [(0, size)]).copies[0]:
        copy.wait()


def join_kernel(size, lists, *refs):
    out_refs = refs[len(refs) - len(lists) :]
    for blocks, out_ref in zip(lists, out_refs):
        for i, (number, at) in enumerate(blocks):
            out_ref[i * size : (i + 1) * size, :] = refs[number][at : at + size, :]


def spread_rows(pad, tight, blocks, rows_ref, grads_ref):
    feat = rows_ref.shape[1]
    for i, (ref, row_at, grad_at) in enumerate(blocks):
        for to_ref, at in [(rows_ref, row_at), (grads_ref, grad_at)]:
            to_ref[i * pad : i * pad + tight, :] = ref[at : at + tight, :]
            to_ref[i * pad + tight : (i + 1) * pad, :] = jnp.zeros((pad - tight, feat), BF16)


def backward(cap, pad, tight, block, blocks, up_ref, down_ref, scratch, put):
    rows_ref, grads_ref, grad_acc, gate_acc = scratch
    spread_rows(pad, tight, blocks, rows_ref, grads_ref)
    slots = rows_ref.shape[0]
    for step in range(up_ref.shape[0] // block):
        part = pl.ds(step * block, block)
        up = up_ref[part, :]
        active, slope = silu_parts(dot(rows_ref[...], up, 1, 1))
        back = dot(grads_ref[...], down_ref[part, :], 1, 1)
        hid_grad = (back * slope).astype(BF16)
        gate = active.astype(BF16).astype(F32) * back
        gate = sum(gate[:, i : i + 128] for i in range(0, block, 128))
        in_grad = dot(hid_grad, up, 1, 0)
        if step == 0:
            grad_acc[...] = in_grad
            gate_acc[...] = gate
        else:
            grad_acc[...] += in_grad
            gate_acc[...] += gate
    gate = jnp.sum(gate_acc[...], axis=1, keepdims=True)
    spot = lax.broadcasted_iota(jnp.int32, (slots, 128), 0) % pad
    lane = lax.broadcasted_iota(jnp.int32, (slots, 128), 1)
    gate = jnp.where(spot == lane, gate, 0.0).reshape(len(blocks), pad, 128)
    gate = jnp.sum(gate, axis=1, keepdims=True)
    line = lax.broadcasted_iota(jnp.int32, (pad, 128), 0)
    for k in range(len(blocks)):
        here = slice(k * pad, (k + 1) * pad)
        first = jnp.where(line == cap, gate[k], grad_acc[here, 0:128])
        put(k, first.astype(BF16), grad_acc[here, 128:].astype(BF16))


def early_back_kernel(cap, pad, tight, block, number, *refs):
    pieces, (up_ref, down_ref, out_ref, *scratch) = refs[:number], refs[number:]

    def put(k, first, rest):
        out_ref[k, :, 0:128] = first
        out_ref[k, :, 128:] = rest

    blocks = [(ref, 0, tight) for ref in pieces]
    backward(cap, pad, tight, block, blocks, up_ref, down_ref, scratch, put)


def late_back_kernel(cap, pad, tight, block, order, number, *refs):
    pieces, refs = refs[:number], refs[number:]
    sibling_ref, early_ref, up_ref, down_ref, _, out_hbm, late_ref, sems, *scratch = refs
    chips = len(order)
    begun = chips - number
    copies = []

    def send(ref, k, core):
        to = out_hbm.at[origin_of(order[k], core, chips)]
        copies.append(pltpu.make_async_copy(ref, to, sems.at[2 * k + core]))
        copies[-1].start()

    for k in range(begun):
        send(early_ref.at[k], k, 0)

    def put(i, first, rest):
        late_ref[i, :, 0:128] = first
        late_ref[i, :, 128:] = rest
        if i < number:
            send(late_ref.at[i], begun + i, 0)
        else:
            send(late_ref.at[i], i - number, 1)

    blocks = [(ref, 0, tight) for ref in pieces]
    blocks += [(sibling_ref, k * tight, (chips + k) * tight) for k in range(chips)]
    backward(cap, pad, tight, block, blocks, up_ref, down_ref, scratch, put)
    for copy in copies:
        copy.wait()


def weights_kernel(pad, block, share, number, begun, ended, *refs):
    refs = list(refs)
    take = lambda number: [refs.pop(0) for _ in range(number)]
    row_refs, weights = take(number), take(2)
    sums = take(2) if begun else None
    notes = None if begun else take(2)
    outs = take(2)
    notes_out = None if begun else take(3)
    up_ref, down_ref = weights if begun else take(2)
    rows_ref, grads_ref, sems, *kept = refs
    steps = steps_of(share, block, begun)
    if not begun:
        fetch = Fetch(*weights, up_ref, down_ref, sems, lax.axis_index("rep") * share, steps)
    if len(row_refs) == 1:
        size = row_refs[0].shape[0] // 2
        rows_ref, grads_ref = row_refs[0].at[0:size, :], row_refs[0].at[size : 2 * size, :]
        row_refs = []
    for i, ref in enumerate(row_refs):
        size = ref.shape[0] // 2
        rows_ref[i * size : (i + 1) * size, :] = ref[:size, :]
        grads_ref[i * size : (i + 1) * size, :] = ref[size:, :]
    copies = []
    for step, (at, size) in enumerate(steps):
        here = pl.ds(at, size)
        if not begun:
            fetch.wait(step)
        active, slope = silu_parts(dot(up_ref[here, :], rows_ref[...], 1, 1))
        back = dot(down_ref[here, :], grads_ref[...], 1, 1)
        hid_grad = (back * slope).astype(BF16)
        parts = [dot(hid_grad, rows_ref[...], 1, 0), dot(active.astype(BF16), grads_ref[...], 1, 0)]
        for i, part in enumerate(parts):
            if begun:
                part += sums[i][0, here, :]
            if not ended:
                outs[i][0, here, :] = part
                continue
            kept[i][here, :] = part.astype(BF16)
            sem = kept[2].at[2 * step + i]
            copies.append(pltpu.make_async_copy(kept[i].at[here, :], outs[i].at[0, here, :], sem))
            copies[-1].start()
    if not begun:
        note_routes(pad, *notes, *notes_out)
    for copy in copies:
        copy.wait()


def note_routes(pad, routes_ref, gates_ref, pick_ref, hot_ref, spot_ref):
    routes = routes_ref[...]
    gates = gates_ref[...].astype(F32)
    rows, slots = pick_ref.shape
    groups = slots // pad
    hot, slot = slots_of(routes, groups)
    same = lax.broadcasted_iota(jnp.int32, (rows, rows), 0) == lax.broadcasted_iota(
        jnp.int32, (rows, rows), 1
    )
    along = jnp.concatenate([routes, *slot, jnp.zeros((4, rows), jnp.int32)], axis=0)
    down = dot(jnp.where(same, 1.0, 0.0).astype(BF16), along.astype(F32).astype(BF16), 1, 1)
    index = lax.broadcasted_iota(jnp.int32, (rows, slots), 1)
    target = [(down[:, k : k + 1] * pad + down[:, 2 + k : 3 + k]).astype(jnp.int32) for k in (0, 1)]
    pick_ref[...] = jnp.where((index == target[0]) | (index == target[1]), 1.0, 0.0).astype(BF16)
    lane = lax.broadcasted_iota(jnp.int32, (128, routes.shape[1]), 0)
    for k in range(2):
        hot_ref[k] = jnp.where(hot[k], 1.0 / gates[k : k + 1, :], 0.0)
        spot_ref[k] = jnp.where(lane == slot[k], 1.0, 0.0).astype(BF16)


def combine_kernel(cap, pick_ref, hot_ref, spot_ref, back_ref, d_tok_ref, d_gate_ref):
    groups, pad, feat = back_ref.shape
    back = back_ref[...]
    d_tok_ref[...] = dot(pick_ref[...], back.reshape(groups * pad, feat), 1, 0).astype(BF16)
    values = back[:, cap, 0:128]
    for k in range(2):
        found = dot(values, spot_ref[k], 1, 0) * hot_ref[k]
        d_gate_ref[k : k + 1, :] = jnp.sum(found, axis=0, keepdims=True).astype(BF16)


def local(tokens, gates, routes, cotangent, w_up, w_down):
    rows, feat = tokens.shape
    hidden = w_up.shape[1]
    groups = lax.axis_size("exp")
    mirrors = lax.axis_size("rep")
    chips = groups // 2
    cap = max(2, 3 * rows // groups)
    pad = (cap // 16 + 1) * 16
    tight = cap + cap % 2
    slots = chips * pad
    share = hidden // mirrors
    routes_t, gates_t = routes.T, gates.T
    hbm = functools.partial(pltpu.with_memory_space_constraint, memory_space=pltpu.HBM)
    shape = jax.ShapeDtypeStruct
    unit = 2 * slots * feat

    near, far = list(range(1, chips // 2)), list(range(chips // 2, chips))
    order = [k for pair in itertools.zip_longest(far[:-1], near[:-1]) for k in pair if k is not None]
    order += far[-1:] + near[-1:]
    out = call(
        functools.partial(slots_kernel, pad, tight),
        "slots",
        [shape((4 * tight, feat), BF16)] * chips,
        [hbm(a) for a in (routes_t, gates_t, tokens, cotangent)],
        [IN_HBM] * 4,
        [
            pltpu.VMEM((2, rows), jnp.int32),
            pltpu.VMEM((2, rows), BF16),
            pltpu.VMEM((rows, feat), BF16),
            pltpu.VMEM((rows, feat), BF16),
            DMA((4,)),
        ],
        4 * unit * rows,
    )
    pieces = [out[0]] + [lax.ppermute(out[k], "exp", hops_to(chips, k)) for k in order]
    swap = [(i, i ^ 1) for i in range(groups)]
    around = [[(i, (i + s) % mirrors) for i in range(mirrors)] for s in range(1, mirrors)]

    w_up, w_down = hbm(w_up), hbm(w_down)
    up_v, down_v = call(
        fetch_kernel,
        "fetch_weights",
        [shape((hidden, feat), BF16)] * 2,
        [w_up, w_down],
        [IN_HBM] * 2,
        [DMA((2,))],
        0,
        0,
        SMALL,
    )
    block = min(512, hidden)
    late = min(3, chips // 2)

    def scratch(number):
        return [
            pltpu.VMEM((number * pad, feat), BF16),
            pltpu.VMEM((number * pad, feat), BF16),
            pltpu.VMEM((number * pad, feat), F32),
            pltpu.VMEM((number * pad, 128), F32),
        ]

    (early,) = call(
        functools.partial(early_back_kernel, cap, pad, tight, block, chips - late),
        "early_backward",
        [shape((chips - late, pad, feat), BF16)],
        [*pieces[:-late], up_v, down_v],
        [IN_VMEM] * (chips - late + 2),
        scratch(chips - late),
        3 * unit * hidden,
        slots * hidden,
    )

    def join(name, arrays, *lists):
        return call(
            functools.partial(join_kernel, tight, lists),
            name,
            [shape((len(blocks) * tight, feat), BF16) for blocks in lists],
            arrays,
            [IN_VMEM] * len(arrays),
            [],
            0,
            0,
            SMALL,
        )

    (handed,) = join("hand_on", [*pieces, early], [(i, at) for at in (2 * tight, 3 * tight) for i in range(chips)])
    sibling = lax.ppermute(handed, "exp", swap)
    (arrived,) = join("arrived_rows", [*pieces, handed], [(i, at) for at in (0, tight) for i in range(chips)])
    firsts = [lax.ppermute(arrived, "rep", hops) for hops in around]
    seconds = [lax.ppermute(sibling, "rep", hops) for hops in around]

    back = pl.pallas_call(
        functools.partial(late_back_kernel, cap, pad, tight, block, [0, *order], late),
        name="late_backward",
        out_shape=pltpu.HBM((groups, pad, feat), BF16),
        in_specs=[IN_VMEM] * (late + 4) + [ANYWHERE],
        out_specs=IN_HBM,
        scratch_shapes=[
            pltpu.VMEM((late + chips, pad, feat), BF16),
            DMA((groups,)),
            *scratch(late + chips),
        ],
        compiler_params=pltpu.CompilerParams(vmem_limit_bytes=MEDIUM),
        cost_estimate=pl.CostEstimate(
            flops=AHEAD, bytes_accessed=4 * hidden * feat, transcendentals=slots * hidden
        ),
    )(*pieces[-late:], sibling, early, up_v, down_v, arrived)
    back = lax.all_to_all(back, "exp", split_axis=0, concat_axis=0, tiled=True)

    part = min(512, share)

    def weights_call(name, arrays, weights, sums, ended, flops):
        begun = bool(sums)
        number = len(arrays) * chips * tight
        notes = [] if begun else [
            shape((rows, groups * pad), BF16),
            shape((2, groups, rows), F32),
            shape((2, 128, rows), BF16),
            shape((share, feat), BF16),
            shape((share, feat), BF16),
        ]
        grad = pltpu.HBM((1, share, feat), BF16) if ended else shape((1, share, feat), F32)
        steps = len(steps_of(share, part, begun))
        scratch = [
            pltpu.VMEM((number, feat), BF16),
            pltpu.VMEM((number, feat), BF16),
            DMA((2 * steps,)),
        ]
        if ended:
            scratch += [pltpu.VMEM((share, feat), BF16)] * 2 + [DMA((2 * steps,))]
        return call(
            functools.partial(weights_kernel, pad, part, share, len(arrays), begun, ended),
            name,
            [grad] * 2 + notes,
            [*arrays, *weights, *(sums or [routes_t, gates_t])],
            [IN_VMEM] * len(arrays) + [IN_VMEM if begun else IN_HBM] * 2 + [IN_VMEM] * 2,
            scratch,
            flops,
            number * share,
            LARGE,
            [IN_HBM if ended else IN_VMEM] * 2 + [IN_VMEM] * len(notes),
        )

    joined = [sibling, arrived, *firsts]
    *sums, pick, hot, spot, up_v, down_v = weights_call(
        "first_weights", joined, [w_up, w_down], [], not seconds, AHEAD
    )
    if seconds:
        sums = weights_call(
            "last_weights", seconds, [up_v, down_v], sums, True, AHEAD
        )
    grad_up, grad_down = sums

    d_tokens, d_gates = call(
        functools.partial(combine_kernel, cap),
        "combine",
        [shape((rows, feat), BF16), shape((2, rows), BF16)],
        [pick, hot, spot, back],
        [IN_VMEM] * 4,
        [],
        4 * unit * rows,
        0,
        SMALL,
    )
    return d_tokens, d_gates.T, grad_up, grad_down


def solution(mesh):
    by_both = P(("rep", "exp"), None)
    by_expert = P("exp", None, None)
    return jax.shard_map(
        local,
        mesh=mesh,
        in_specs=(by_both, by_both, by_both, by_both, by_expert, by_expert),
        out_specs=(by_both, by_both, P("exp", "rep", None), P("exp", "rep", None)),
        check_vma=False,
    )
```
